32 devices in a mesh: seq: 4 (over x, core), band: 8 (over z, y).
Axes of the slice: x: 2, y: 2, z: 4, core: 2. Of those that a mesh axis runs over, the one named last changes fastest.
Arguments:
- block_in: bfloat16 [4, 1024, 1024], P('seq', 'band'), may hold values from -6 to 6
- attention_norm_gain: bfloat16 [1024], P(('seq', 'band')), may hold values from 0.5 to 1.5
- attention_norm_bias: bfloat16 [1024], P(('seq', 'band')), may hold values from -3 to 3
- query_key_value: bfloat16 [1024, 3072], P(('seq', 'band')), may hold values from -0.1875 to 0.1875
- query_bias: bfloat16 [1024], P(('seq', 'band')), may hold values from -3 to 3
- value_bias: bfloat16 [1024], P(('seq', 'band')), may hold values from -3 to 3
- output_weight: bfloat16 [1024, 1024], P(('seq', 'band')), may hold values from -1.5 to 1.5
- output_bias: bfloat16 [1024], P(('seq', 'band')), may hold values from -3 to 3
- mlp_norm_gain: bfloat16 [1024], P(('seq', 'band')), may hold values from 0.5 to 1.5
- mlp_norm_bias: bfloat16 [1024], P(('seq', 'band')), may hold values from -3 to 3
- mlp_in_weight: bfloat16 [1024, 4096], P(('seq', 'band')), may hold values from -0.1875 to 0.1875
- mlp_in_bias: bfloat16 [4096], P(('seq', 'band')), may hold values from -3 to 3
- mlp_out_weight: bfloat16 [4096, 1024], P(('seq', 'band')), may hold values from -0.09375 to 0.09375
- mlp_out_bias: bfloat16 [1024], P(('seq', 'band')), may hold values from -3 to 3
- cotangent: bfloat16 [4, 1024, 1024], P('seq', 'band'), may hold values from -6 to 6
- segment_ids: int32 [4, 1024], P('seq', 'band'), may hold values from 0 to 7, as said below
- sub_lengths: int32 [4, 8], P('seq'), may hold values from 1 to 640, as said below
Outputs:
- block_out: bfloat16 [4, 1024, 1024], P('seq', 'band')
- input_grad: bfloat16 [4, 1024, 1024], P('seq', 'band')
- grad_attention_norm_gain: float32 [1024], P(('seq', 'band'))
- grad_attention_norm_bias: float32 [1024], P(('seq', 'band'))
- grad_query_key_value: float32 [1024, 3072], P(('seq', 'band'))
- grad_query_bias: float32 [1024], P(('seq', 'band'))
- grad_value_bias: float32 [1024], P(('seq', 'band'))
- grad_output_weight: float32 [1024, 1024], P(('seq', 'band'))
- grad_output_bias: float32 [1024], P(('seq', 'band'))
- grad_mlp_norm_gain: float32 [1024], P(('seq', 'band'))
- grad_mlp_norm_bias: float32 [1024], P(('seq', 'band'))
- grad_mlp_in_weight: float32 [1024, 4096], P(('seq', 'band'))
- grad_mlp_in_bias: float32 [4096], P(('seq', 'band'))
- grad_mlp_out_weight: float32 [4096, 1024], P(('seq', 'band'))
- grad_mlp_out_bias: float32 [1024], P(('seq', 'band'))
The draws below stay inside these ranges and needn't reach their ends.
Inputs may be any that keep to these rules, and one draw needn't show every extreme that they name: `segment_ids`: in each sequence the largest subgrid holds exactly 640 slots; the slots of a subgrid may lie anywhere in the sequence. `sub_lengths`: each length is at most the number of slots of its subgrid, and the largest subgrid of each sequence has length 640.
All inputs are finite; a program needn't handle non-finite values.
Results may differ from the reference program's by a relative error of at most 0.012.
Values may be sent and summed in bfloat16 or wider, within the bound.
A program may use at most 256 MiB of HBM per device.

```python
import math
import jax
import jax.numpy as jnp
from jax import lax

D = 1024
HEADS = 16
HEAD_DIM = 64
FF = 4096
SUBGRIDS = 8
LENGTH = 1024
SEQS = 4
MOST = 640


def segment_table(key):
    base_key = jax.random.fold_in(key, 7)
    seq_keys = jax.random.split(base_key, SEQS)

    def one_sequence(sequence_key):
        key_big, key_perm, key_other, key_cut = jax.random.split(sequence_key, 4)
        big_label = jax.random.randint(key_big, (), 0, SUBGRIDS)
        slot_order = jax.random.permutation(key_perm, LENGTH)
        other_label = (big_label + 1 + jax.random.randint(key_other, (LENGTH,), 0, SUBGRIDS - 1)) % SUBGRIDS
        slot_ids = jnp.where(slot_order < MOST, big_label, other_label).astype(jnp.int32)
        labels = jnp.arange(SUBGRIDS, dtype=jnp.int32)
        counts = jnp.sum((slot_ids[:, None] == labels[None, :]).astype(jnp.int32), axis=0)
        cut_back = jax.random.randint(key_cut, (SUBGRIDS,), 0, 1000000) % (counts // 4 + 1) + 1
        lengths = jnp.maximum(counts - cut_back, 1)
        lengths = jnp.where(labels == big_label, MOST, lengths).astype(jnp.int32)
        return (slot_ids, lengths)
    return jax.vmap(one_sequence)(seq_keys)


def draw_segment_ids(key, part):
    return segment_table(key)[0]


def draw_sub_lengths(key, part):
    return segment_table(key)[1]


def shard_levels(key, dims, cuts, low, high):
    level, own = 1.0, jax.random.fold_in(key, 6)
    for position, blocks in cuts:
        steps = jnp.exp(jax.random.uniform(jax.random.fold_in(own, position), (blocks,), jnp.float32, low / len(cuts), high / len(cuts)))
        level = level * jnp.repeat(steps, dims[position] // blocks).reshape([-1 if axis == position else 1 for axis in range(len(dims))])
    return level


def gaussian(rng, shape, width, limit, cuts=(), kind=jnp.bfloat16):
    entries = width * jax.random.normal(rng, shape, jnp.float32)
    if cuts:
        entries = entries * shard_levels(rng, shape, cuts, -0.22, 0.18)
    return jnp.clip(entries, -limit, limit).astype(kind)


def setup_inputs(seed: int = 0) -> dict:
    streams_of = jax.random.split(jax.random.key(seed), 18)
    block_in = gaussian(streams_of[0], (SEQS, LENGTH, D), 1.0, 6.0, ((0, 4), (1, 8)))
    attention_norm_gain = jnp.clip(1.0 + 0.1 * jax.random.normal(streams_of[1], (D,), jnp.float32), 0.5, 1.5).astype(jnp.bfloat16)
    attention_norm_bias = gaussian(streams_of[2], (D,), 0.3, 3.0, ((0, 32),))
    query_key_value = gaussian(streams_of[3], (D, 3 * D), D ** -0.5, 0.1875, ((0, 32),))
    query_bias = gaussian(streams_of[4], (D,), 0.5, 3.0, ((0, 32),))
    value_bias = gaussian(streams_of[5], (D,), 0.5, 3.0, ((0, 32),))
    output_weight = gaussian(streams_of[6], (D, D), (D // 64) ** -0.5, 1.5, ((0, 32),))
    output_bias = gaussian(streams_of[7], (D,), 0.3, 3.0, ((0, 32),))
    mlp_norm_gain = jnp.clip(1.0 + 0.1 * jax.random.normal(streams_of[8], (D,), jnp.float32), 0.5, 1.5).astype(jnp.bfloat16)
    mlp_norm_bias = gaussian(streams_of[9], (D,), 0.3, 3.0, ((0, 32),))
    mlp_in_weight = gaussian(streams_of[10], (D, FF), D ** -0.5, 0.1875, ((0, 32),))
    mlp_in_bias = gaussian(streams_of[11], (FF,), 0.5, 3.0, ((0, 32),))
    mlp_out_weight = gaussian(streams_of[12], (FF, D), FF ** -0.5, 0.09375, ((0, 32),))
    mlp_out_bias = gaussian(streams_of[13], (D,), 0.3, 3.0, ((0, 32),))
    cotangent = gaussian(streams_of[14], (SEQS, LENGTH, D), 1.0, 6.0, ((0, 4), (1, 8)))
    segment_ids = draw_segment_ids(jax.random.fold_in(streams_of[17], 71), 0)
    sub_lengths = draw_sub_lengths(jax.random.fold_in(streams_of[17], 71), 0)
    return {"block_in": block_in, "attention_norm_gain": attention_norm_gain, "attention_norm_bias": attention_norm_bias, "query_key_value": query_key_value, "query_bias": query_bias, "value_bias": value_bias, "output_weight": output_weight, "output_bias": output_bias, "mlp_norm_gain": mlp_norm_gain, "mlp_norm_bias": mlp_norm_bias, "mlp_in_weight": mlp_in_weight, "mlp_in_bias": mlp_in_bias, "mlp_out_weight": mlp_out_weight, "mlp_out_bias": mlp_out_bias, "cotangent": cotangent, "segment_ids": segment_ids, "sub_lengths": sub_lengths}


EPSILON = 1e-05
HIGHEST = lax.Precision.HIGHEST

@jax.custom_vjp
def low(v):
    return lax.optimization_barrier(v.astype(jnp.bfloat16)).astype(jnp.float32)

@jax.custom_vjp
def low_back(v):
    return v

def low_keep(v):
    return (low(v), None)

def low_pass(kept, grad):
    return (grad,)

def back_keep(v):
    return (v, None)

def back_low(kept, grad):
    return (low(grad),)
low.defvjp(low_keep, low_pass)
low_back.defvjp(back_keep, back_low)

def layer_norm(values_in, norm_gain, norm_shift):
    average = lax.optimization_barrier(jnp.mean(values_in, axis=-1, keepdims=True))
    centered = values_in - average
    variance = lax.optimization_barrier(jnp.mean(centered * centered, axis=-1, keepdims=True))
    return centered * lax.rsqrt(variance + EPSILON) * norm_gain + norm_shift

def patch_codes(seg_row, length_row):
    labels = jnp.arange(SUBGRIDS, dtype=jnp.int32)
    onehot_ids = (seg_row[:, None] == labels[None, :]).astype(jnp.int32)
    before = jnp.cumsum(onehot_ids, axis=0) - onehot_ids
    patch_rank = lax.optimization_barrier(jnp.sum(before * onehot_ids, axis=1))
    limits = lax.optimization_barrier(jnp.sum(onehot_ids * length_row[None, :], axis=1))
    realness = patch_rank < limits
    return (jnp.where(realness, seg_row, -1).astype(jnp.int32), realness)

def attend_block(keys_all, values_all, key_codes, block_items):
    query_part, seg_part = block_items
    scores = jnp.einsum('qhe,khe->hqk', query_part, keys_all, precision=HIGHEST) * HEAD_DIM ** (-0.5)
    scores = low_back(scores)
    allowed = (seg_part[:, None] == key_codes[None, :])[None]
    scores = jnp.where(allowed, scores, -1e+30)
    soft_probs = low(jax.nn.softmax(scores, axis=-1))
    return jnp.einsum('hqk,khe->qhe', soft_probs, values_all, precision=HIGHEST)

def sequence_forward(inputs, weights, seg_row, key_codes):
    gain_one, shift_one, joint_weight, bias_query, bias_value, proj_weight, proj_bias, gain_two, shift_two, up_weight, up_bias, down_weight, down_bias = weights
    normed_one = low(layer_norm(inputs, gain_one, shift_one))
    mixed_all = jnp.dot(normed_one, joint_weight, precision=HIGHEST)
    queries = low(low_back(mixed_all[:, :D] + bias_query))
    keys_all = low(low_back(mixed_all[:, D:2 * D]))
    values_all = low(low_back(mixed_all[:, 2 * D:] + bias_value))
    block_rows = math.gcd(LENGTH, 512)
    block_count = LENGTH // block_rows
    key_heads = keys_all.reshape(LENGTH, HEADS, HEAD_DIM)
    value_heads = values_all.reshape(LENGTH, HEADS, HEAD_DIM)

    def one_block(block_items):
        return attend_block(key_heads, value_heads, key_codes, block_items)
    attended = lax.map(jax.checkpoint(one_block), (queries.reshape(block_count, block_rows, HEADS, HEAD_DIM), seg_row.reshape(block_count, block_rows)))
    attended = low(low_back(attended.reshape(LENGTH, D)))
    branch = low_back(jnp.dot(attended, proj_weight, precision=HIGHEST) + proj_bias)
    residual = inputs + branch
    normed_two = low(layer_norm(residual, gain_two, shift_two))
    hidden_pre = low_back(jnp.dot(normed_two, up_weight, precision=HIGHEST) + up_bias)
    hidden_act = low(jax.nn.gelu(hidden_pre, approximate=False))
    return residual + low_back(jnp.dot(hidden_act, down_weight, precision=HIGHEST) + down_bias)

def reference(block_in, attention_norm_gain, attention_norm_bias, query_key_value, query_bias, value_bias, output_weight, output_bias, mlp_norm_gain, mlp_norm_bias, mlp_in_weight, mlp_in_bias, mlp_out_weight, mlp_out_bias, cotangent, segment_ids, sub_lengths):
    weights = tuple((member.astype(jnp.float32) for member in (attention_norm_gain, attention_norm_bias, query_key_value, query_bias, value_bias, output_weight, output_bias, mlp_norm_gain, mlp_norm_bias, mlp_in_weight, mlp_in_bias, mlp_out_weight, mlp_out_bias)))

    def per_sequence(totals, scan_items):
        inputs, grad_rows, seg_row, length_row = scan_items
        key_codes, realness = patch_codes(seg_row, length_row)

        def forward(layer_in, layer_weights):
            return sequence_forward(layer_in, layer_weights, seg_row, key_codes)
        result, pullback = jax.vjp(forward, inputs.astype(jnp.float32), weights)
        grad_in, grad_weights = pullback(grad_rows.astype(jnp.float32) * realness[:, None].astype(jnp.float32))
        totals = tuple((total_part + new_part for total_part, new_part in zip(totals, grad_weights)))
        return (totals, (result.astype(jnp.bfloat16), grad_in.astype(jnp.bfloat16)))
    zero_grads = tuple((jnp.zeros(member.shape, jnp.float32) for member in weights))
    totals, (block_out, input_grad) = lax.scan(per_sequence, zero_grads, (block_in, cotangent, segment_ids, sub_lengths))
    return (block_out, input_grad, totals[0], totals[1], totals[2], totals[3], totals[4], totals[5], totals[6], totals[7], totals[8], totals[9], totals[10], totals[11], totals[12])
```

```python
import functools
import math

import jax
import jax.numpy as jnp
from jax import lax
from jax.experimental import pallas as pl
from jax.experimental.pallas import tpu as pltpu
from jax.sharding import PartitionSpec as P

D = 1024
HEADS = 16
HEAD_DIM = 64
SUBGRIDS = 8


EPSILON = 1e-05
NEGATIVE = -1e30


def prefix(part, axis, combine, identity):
    place = lax.axis_index(axis)
    gathered = lax.all_gather(part, axis)
    state = jnp.zeros_like(part) + jnp.asarray(identity, part.dtype)

    def one(lap, state):
        return combine(state, lax.dynamic_index_in_dim(gathered, lap, 0, False))

    return lax.fori_loop(0, place, one, state)


def layer_norm(values_in, norm_gain, norm_shift):
    average = jnp.mean(values_in, axis=-1, keepdims=True)
    centered = values_in - average
    variance = jnp.mean(centered * centered, axis=-1, keepdims=True)
    return centered * lax.rsqrt(variance + EPSILON) * norm_gain + norm_shift


def gelu_exact(values_in):
    return jax.nn.gelu(values_in, approximate=False)


def add_counts(first_part, second_part):
    return first_part + second_part


def block_scores(query_part, key_part, seg_part, code_part, scale_factor):
    scores = (
        jnp.einsum("qhe,khe->hqk", query_part, key_part, preferred_element_type=jnp.float32)
        * scale_factor
    )
    allowed = (seg_part[:, None] == code_part[None, :])[None]
    return (jnp.where(allowed, scores, NEGATIVE), allowed)


def split_blocks(array_in, block_rows):
    return array_in.reshape((array_in.shape[0] // block_rows, block_rows) + array_in.shape[1:])


def shards(
    block_in,
    attention_norm_gain,
    attention_norm_bias,
    query_key_value,
    query_bias,
    value_bias,
    output_weight,
    output_bias,
    mlp_norm_gain,
    mlp_norm_bias,
    mlp_in_weight,
    mlp_in_bias,
    mlp_out_weight,
    mlp_out_bias,
    cotangent,
    segment_ids,
    sub_lengths,
):
    float_type = jnp.float32
    half_type = jnp.bfloat16
    rows_local = block_in.shape[1]
    seq_length = rows_local * lax.axis_size("band")
    scale_factor = HEAD_DIM ** (-0.5)
    block_rows = math.gcd(seq_length, 1024)
    seg_local = segment_ids[0]
    labels = jnp.arange(SUBGRIDS, dtype=jnp.int32)
    onehot_ids = (seg_local[:, None] == labels[None, :]).astype(jnp.int32)
    earlier_counts = prefix(
        jnp.sum(onehot_ids, axis=0), "band", add_counts, jnp.zeros((SUBGRIDS,), jnp.int32)
    )
    slots = jnp.arange(rows_local)
    earlier = (slots[None, :] < slots[:, None]).astype(float_type)
    before = (
        jnp.dot(earlier, onehot_ids.astype(float_type), precision=lax.Precision.HIGHEST).astype(
            jnp.int32
        )
        + earlier_counts[None, :]
    )
    patch_rank = jnp.sum(before * onehot_ids, axis=1)
    limits = jnp.sum(onehot_ids * sub_lengths[0][None, :], axis=1)
    realness = patch_rank < limits
    key_codes = jnp.where(realness, seg_local, -1)
    gathered = (
        lax.all_gather(attention_norm_gain, ("seq", "band"), axis=0, tiled=True),
        lax.all_gather(attention_norm_bias, ("seq", "band"), axis=0, tiled=True),
        lax.all_gather(query_key_value, ("seq", "band"), axis=0, tiled=True),
        lax.all_gather(query_bias, ("seq", "band"), axis=0, tiled=True),
        lax.all_gather(value_bias, ("seq", "band"), axis=0, tiled=True),
        lax.all_gather(output_weight, ("seq", "band"), axis=0, tiled=True),
        lax.all_gather(output_bias, ("seq", "band"), axis=0, tiled=True),
        lax.all_gather(mlp_norm_gain, ("seq", "band"), axis=0, tiled=True),
        lax.all_gather(mlp_norm_bias, ("seq", "band"), axis=0, tiled=True),
        lax.all_gather(mlp_in_weight, ("seq", "band"), axis=0, tiled=True),
        lax.all_gather(mlp_in_bias, ("seq", "band"), axis=0, tiled=True),
        lax.all_gather(mlp_out_weight, ("seq", "band"), axis=0, tiled=True),
        lax.all_gather(mlp_out_bias, ("seq", "band"), axis=0, tiled=True),
    )
    (
        gain_one,
        shift_one,
        joint_weight,
        bias_query,
        bias_value,
        proj_weight,
        proj_bias,
        gain_two,
        shift_two,
        up_weight,
        up_bias,
        down_weight,
        down_bias,
    ) = gathered
    inputs = block_in[0].astype(float_type)
    normed_float, norm_pull_one = jax.vjp(
        layer_norm, inputs, gain_one.astype(float_type), shift_one.astype(float_type)
    )
    normed_one = normed_float.astype(half_type)
    mixed_all = jnp.dot(normed_one, joint_weight, preferred_element_type=float_type)
    queries = (mixed_all[:, :D] + bias_query.astype(float_type)).astype(half_type)
    keys_local = mixed_all[:, D : 2 * D].astype(half_type)
    values_local = (mixed_all[:, 2 * D :] + bias_value.astype(float_type)).astype(half_type)
    keys_seq, values_seq, codes_seq = (
        lax.all_gather(keys_local, "band", axis=0, tiled=True),
        lax.all_gather(values_local, "band", axis=0, tiled=True),
        lax.all_gather(key_codes, "band", axis=0, tiled=True),
    )
    query_heads = queries.reshape(rows_local, HEADS, HEAD_DIM)
    key_blocks = split_blocks(keys_seq.reshape(seq_length, HEADS, HEAD_DIM), block_rows)
    value_blocks = split_blocks(values_seq.reshape(seq_length, HEADS, HEAD_DIM), block_rows)
    code_blocks = split_blocks(codes_seq, block_rows)

    def stats_step(running, block_items):
        top_now, total_now = running
        key_part, code_part = block_items
        scores, allowed = block_scores(query_heads, key_part, seg_local, code_part, scale_factor)
        top_new = jnp.maximum(top_now, jnp.max(scores, axis=-1))
        exp_terms = jnp.where(allowed, jnp.exp(scores - top_new[..., None]), 0.0)
        return (
            (top_new, total_now * jnp.exp(top_now - top_new) + jnp.sum(exp_terms, axis=-1)),
            None,
        )

    start_stats = (
        jnp.full((HEADS, rows_local), NEGATIVE, float_type),
        jnp.zeros((HEADS, rows_local), float_type),
    )
    (top_final, total_final), unused_stats = lax.scan(
        stats_step, start_stats, (key_blocks, code_blocks)
    )
    log_total = top_final + jnp.log(total_final)

    def value_step(accum_out, block_items):
        key_part, value_part, code_part = block_items
        scores, allowed = block_scores(query_heads, key_part, seg_local, code_part, scale_factor)
        soft_probs = jnp.where(allowed, jnp.exp(scores - log_total[..., None]), 0.0).astype(
            half_type
        )
        return (
            accum_out
            + jnp.einsum("hqk,khe->qhe", soft_probs, value_part, preferred_element_type=float_type),
            None,
        )

    attended, unused_values = lax.scan(
        value_step,
        jnp.zeros((rows_local, HEADS, HEAD_DIM), float_type),
        (key_blocks, value_blocks, code_blocks),
    )
    attended_low = attended.reshape(rows_local, D).astype(half_type)
    residual = (
        inputs
        + jnp.dot(attended_low, proj_weight, preferred_element_type=float_type)
        + proj_bias.astype(float_type)
    )
    normed_float_two, norm_pull_two = jax.vjp(
        layer_norm, residual, gain_two.astype(float_type), shift_two.astype(float_type)
    )
    normed_two = normed_float_two.astype(half_type)
    hidden_pre = jnp.dot(normed_two, up_weight, preferred_element_type=float_type) + up_bias.astype(
        float_type
    )
    hidden_value, gelu_pull = jax.vjp(gelu_exact, hidden_pre)
    hidden_act = hidden_value.astype(half_type)
    block_result = (
        residual
        + jnp.dot(hidden_act, down_weight, preferred_element_type=float_type)
        + down_bias.astype(float_type)
    )
    gathered_back = (
        lax.all_gather(attention_norm_gain, ("seq", "band"), axis=0, tiled=True),
        lax.all_gather(attention_norm_bias, ("seq", "band"), axis=0, tiled=True),
        lax.all_gather(query_key_value, ("seq", "band"), axis=0, tiled=True),
        lax.all_gather(query_bias, ("seq", "band"), axis=0, tiled=True),
        lax.all_gather(value_bias, ("seq", "band"), axis=0, tiled=True),
        lax.all_gather(output_weight, ("seq", "band"), axis=0, tiled=True),
        lax.all_gather(output_bias, ("seq", "band"), axis=0, tiled=True),
        lax.all_gather(mlp_norm_gain, ("seq", "band"), axis=0, tiled=True),
        lax.all_gather(mlp_norm_bias, ("seq", "band"), axis=0, tiled=True),
        lax.all_gather(mlp_in_weight, ("seq", "band"), axis=0, tiled=True),
        lax.all_gather(mlp_in_bias, ("seq", "band"), axis=0, tiled=True),
        lax.all_gather(mlp_out_weight, ("seq", "band"), axis=0, tiled=True),
        lax.all_gather(mlp_out_bias, ("seq", "band"), axis=0, tiled=True),
    )
    joint_back = gathered_back[2]
    proj_back = gathered_back[5]
    up_back = gathered_back[9]
    down_back = gathered_back[11]
    grad_out = cotangent[0].astype(float_type) * realness[:, None].astype(float_type)
    grad_mlp = grad_out.astype(half_type)
    grad_down_weight = jnp.einsum(
        "rf,rd->fd", hidden_act, grad_mlp, preferred_element_type=float_type
    )
    grad_down_bias = jnp.sum(grad_mlp.astype(float_type), axis=0)
    grad_act = jnp.einsum("rd,fd->rf", grad_mlp, down_back, preferred_element_type=float_type)
    grad_pre = gelu_pull(grad_act)[0].astype(half_type)
    grad_up_weight = jnp.einsum(
        "rd,rf->df", normed_two, grad_pre, preferred_element_type=float_type
    )
    grad_up_bias = jnp.sum(grad_pre.astype(float_type), axis=0)
    grad_normed_two = jnp.einsum("rf,df->rd", grad_pre, up_back, preferred_element_type=float_type)
    grad_resid_part, grad_gain_two, grad_shift_two = norm_pull_two(grad_normed_two)
    grad_residual = grad_out + grad_resid_part
    grad_branch = grad_residual.astype(half_type)
    grad_proj_weight = jnp.einsum(
        "rd,re->de", attended_low, grad_branch, preferred_element_type=float_type
    )
    grad_proj_bias = jnp.sum(grad_branch.astype(float_type), axis=0)
    grad_attended = jnp.einsum(
        "re,de->rd", grad_branch, proj_back, preferred_element_type=float_type
    ).astype(half_type)
    grad_heads = grad_attended.reshape(rows_local, HEADS, HEAD_DIM)
    row_delta = jnp.sum(grad_heads.astype(float_type) * attended, axis=-1).T
    keys_back = lax.all_gather(keys_local, "band", axis=0, tiled=True)
    values_back = lax.all_gather(values_local, "band", axis=0, tiled=True)
    codes_back = lax.all_gather(key_codes, "band", axis=0, tiled=True)
    key_back_blocks = split_blocks(keys_back.reshape(seq_length, HEADS, HEAD_DIM), block_rows)
    value_back_blocks = split_blocks(values_back.reshape(seq_length, HEADS, HEAD_DIM), block_rows)
    code_back_blocks = split_blocks(codes_back, block_rows)

    def key_step(query_accum, block_items):
        key_part, value_part, code_part = block_items
        scores, allowed = block_scores(query_heads, key_part, seg_local, code_part, scale_factor)
        soft_probs = jnp.where(allowed, jnp.exp(scores - log_total[..., None]), 0.0)
        grad_probs = jnp.einsum(
            "qhe,khe->hqk", grad_heads, value_part, preferred_element_type=float_type
        )
        grad_scores = (soft_probs * (grad_probs - row_delta[..., None])).astype(half_type)
        query_accum = query_accum + jnp.einsum(
            "hqk,khe->qhe", grad_scores, key_part, preferred_element_type=float_type
        )
        return (query_accum, None)

    query_total, joined_blocks = lax.scan(
        key_step,
        jnp.zeros((rows_local, HEADS, HEAD_DIM), float_type),
        (key_back_blocks, value_back_blocks, code_back_blocks),
    )
    grad_query = (query_total * scale_factor).reshape(rows_local, D)
    query_seq = lax.all_gather(queries, "band", axis=0, tiled=True)
    grad_seq = lax.all_gather(grad_attended, "band", axis=0, tiled=True)
    total_seq = lax.all_gather(log_total, "band", axis=1, tiled=True)
    delta_seq = lax.all_gather(row_delta, "band", axis=1, tiled=True)
    seg_seq = lax.all_gather(seg_local, "band", axis=0, tiled=True)
    block_count = seq_length // block_rows
    key_heads_local = keys_local.reshape(rows_local, HEADS, HEAD_DIM)
    value_heads_local = values_local.reshape(rows_local, HEADS, HEAD_DIM)

    def query_step(running, block_items):
        key_accum, value_accum = running
        query_part, grad_part, total_part, delta_part, seg_part = block_items
        scores, allowed = block_scores(
            query_part, key_heads_local, seg_part, key_codes, scale_factor
        )
        soft_probs = jnp.where(allowed, jnp.exp(scores - total_part[..., None]), 0.0)
        grad_probs = jnp.einsum(
            "qhe,khe->hqk", grad_part, value_heads_local, preferred_element_type=float_type
        )
        grad_scores = (soft_probs * (grad_probs - delta_part[..., None])).astype(half_type)
        key_accum = key_accum + jnp.einsum(
            "hqk,qhe->khe", grad_scores, query_part, preferred_element_type=float_type
        )
        value_accum = value_accum + jnp.einsum(
            "hqk,qhe->khe",
            soft_probs.astype(half_type),
            grad_part,
            preferred_element_type=float_type,
        )
        return ((key_accum, value_accum), None)

    zero_heads = jnp.zeros((rows_local, HEADS, HEAD_DIM), float_type)
    (key_total, value_total), query_blocks = lax.scan(
        query_step,
        (zero_heads, zero_heads),
        (
            split_blocks(query_seq.reshape(seq_length, HEADS, HEAD_DIM), block_rows),
            split_blocks(grad_seq.reshape(seq_length, HEADS, HEAD_DIM), block_rows),
            total_seq.reshape(HEADS, block_count, block_rows).transpose(1, 0, 2),
            delta_seq.reshape(HEADS, block_count, block_rows).transpose(1, 0, 2),
            split_blocks(seg_seq, block_rows),
        ),
    )
    grad_key = (key_total * scale_factor).reshape(rows_local, D)
    grad_value = value_total.reshape(rows_local, D)
    grad_query_low = grad_query.astype(half_type)
    grad_value_low = grad_value.astype(half_type)
    grad_mixed = jnp.concatenate(
        [grad_query_low, grad_key.astype(half_type), grad_value_low], axis=1
    )
    grad_joint_weight = jnp.einsum(
        "rd,rm->dm", normed_one, grad_mixed, preferred_element_type=float_type
    )
    grad_bias_query = jnp.sum(grad_query_low.astype(float_type), axis=0)
    grad_bias_value = jnp.sum(grad_value_low.astype(float_type), axis=0)
    grad_normed_one = jnp.einsum(
        "rm,dm->rd", grad_mixed, joint_back, preferred_element_type=float_type
    )
    grad_input_part, grad_gain_one, grad_shift_one = norm_pull_one(grad_normed_one)
    input_grad = (grad_residual + grad_input_part).astype(half_type)
    shard_grads = (
        lax.psum_scatter(grad_gain_one, ("seq", "band"), scatter_dimension=0, tiled=True),
        lax.psum_scatter(grad_shift_one, ("seq", "band"), scatter_dimension=0, tiled=True),
        lax.psum_scatter(grad_joint_weight, ("seq", "band"), scatter_dimension=0, tiled=True),
        lax.psum_scatter(grad_bias_query, ("seq", "band"), scatter_dimension=0, tiled=True),
        lax.psum_scatter(grad_bias_value, ("seq", "band"), scatter_dimension=0, tiled=True),
        lax.psum_scatter(grad_proj_weight, ("seq", "band"), scatter_dimension=0, tiled=True),
        lax.psum_scatter(grad_proj_bias, ("seq", "band"), scatter_dimension=0, tiled=True),
        lax.psum_scatter(grad_gain_two, ("seq", "band"), scatter_dimension=0, tiled=True),
        lax.psum_scatter(grad_shift_two, ("seq", "band"), scatter_dimension=0, tiled=True),
        lax.psum_scatter(grad_up_weight, ("seq", "band"), scatter_dimension=0, tiled=True),
        lax.psum_scatter(grad_up_bias, ("seq", "band"), scatter_dimension=0, tiled=True),
        lax.psum_scatter(grad_down_weight, ("seq", "band"), scatter_dimension=0, tiled=True),
        lax.psum_scatter(grad_down_bias, ("seq", "band"), scatter_dimension=0, tiled=True),
    )
    return (
        block_result.astype(half_type)[None],
        input_grad[None],
        shard_grads[0],
        shard_grads[1],
        shard_grads[2],
        shard_grads[3],
        shard_grads[4],
        shard_grads[5],
        shard_grads[6],
        shard_grads[7],
        shard_grads[8],
        shard_grads[9],
        shard_grads[10],
        shard_grads[11],
        shard_grads[12],
    )


F32 = jnp.float32
BF16 = jnp.bfloat16
MESH_ID = pl.DeviceIdType.MESH
ROWS = 128
LANES = 128


def dot(lhs, rhs):
    return jnp.dot(lhs, rhs, preferred_element_type=F32)


def dot_nt(lhs, rhs):
    return lax.dot_general(lhs, rhs, (((1,), (1,)), ((), ())), preferred_element_type=F32)


def dot_tn(lhs, rhs):
    return lax.dot_general(lhs, rhs, (((0,), (0,)), ((), ())), preferred_element_type=F32)


def fused_kernel(copies, *refs):
    (
        xin, cin, sgin, pkin, wq, wo, wi, wd,
        out_block, out_input, out_q, out_o, out_i, out_d, out_small,
        X, N1, N2, GM, GB, SG, SP, FULL, PV,
        WSQ, RQ, WQ, WO, WSI, RI, WI, WD,
        QS, KK, VV, QT, KT, VT, CODE, SC, PT, INV, OT, OL,
        PA, CS, PB, CSB, SB, RV, XO, N2F, HAT, HA, GP,
        DK, DV, DQ, GMX,
        GQ, GI, GD, XQ, XI, XD, HQ, HI, HD, ZQ, ZI, ZD, TQ, TI, RGQ, RGI,
        GO, GOF, XGO, TGO, RGO,
        VG, VR, SL, SLR, RS_, BG,
        ssem, rsem,
    ) = refs
    s = lax.axis_index("seq")
    b = lax.axis_index("band")
    x, c = lax.div(s, 2), lax.rem(s, 2)
    zh, l = lax.div(b, 4), lax.rem(b, 4)
    zl, y = lax.div(l, 2), lax.rem(l, 2)
    t, j = x * 2 + zh, c * 4 + l

    def flip(v, d):
        return 1 - v if d else v

    def flip_l(d):
        return flip(zl, d // 2) * 2 + flip(y, d % 2)

    def dev(dx=0, dc=0, dzh=0, dl=0):
        return (flip(x, dx) * 2 + flip(c, dc), flip(zh, dzh) * 4 + flip_l(dl))

    counter = [0]
    pending = []

    def slots(n=1):
        first = counter[0]
        counter[0] += n
        assert counter[0] <= copies
        return first

    def send(src, dst, device, sem):
        copy = pltpu.make_async_remote_copy(
            src_ref=src, dst_ref=dst, send_sem=ssem.at[sem], recv_sem=rsem.at[sem],
            device_id=device, device_id_type=MESH_ID)
        copy.start()
        return copy

    def push(src, dst, device, sem):
        copy = send(src, dst, device, sem)
        pending.append(copy)
        return copy

    def arrive(dst, sem):
        pltpu.make_async_remote_copy(
            src_ref=dst, dst_ref=dst, send_sem=ssem.at[sem], recv_sem=rsem.at[sem],
            device_id=dev(dc=1), device_id_type=MESH_ID).wait_recv()

    def left(src, sem):
        pltpu.make_async_remote_copy(
            src_ref=src, dst_ref=src, send_sem=ssem.at[sem], recv_sem=rsem.at[sem],
            device_id=dev(dc=1), device_id_type=MESH_ID).wait_send()

    group_masks = [(dc, dl) for dl in (1, 2, 3, 0) for dc in (0, 1) if (dc, dl) != (0, 0)]
    line_masks = [(dx, dc, dzh) for dx in (0, 1) for dc in (0, 1) for dzh in (0, 1) if dx + dc + dzh]

    barrier = pltpu.get_barrier_semaphore()
    peers = [dict(dc=dc, dl=dl) for dc, dl in group_masks]
    peers += [dict(dx=a, dc=e, dzh=f) for a, e, f in line_masks if (a, e, f) != (0, 1, 0)]
    for peer in peers:
        pl.semaphore_signal(barrier, inc=1, device_id=dev(**peer), device_id_type=MESH_ID)
    pl.semaphore_wait(barrier, len(peers))

    native = c == zh
    partner = dev(dc=1, dzh=1)
    their_block = (1 - c) * 4 + l

    sem_px, sem_pc, sem_ps = slots(), slots(), slots()

    @pl.when(native)
    def _():
        X[j] = xin[...]
        SG[j] = sgin[...]

    @pl.when(jnp.logical_not(native))
    def _():
        send(sgin, SG.at[their_block], partner, sem_ps)
        send(xin, X.at[their_block], partner, sem_px)

    sem_s1 = slots(4)
    for dl in (1, 2, 3):
        push(pkin, SP.at[dl], dev(dl=dl), sem_s1 + dl)

    for jj in range(8):
        for ch in range(3):
            WSQ[jj, ch] = wq[:, ch * D + jj * LANES : ch * D + (jj + 1) * LANES]
    sem_wq = slots(8)
    for dc, dl in group_masks:
        peer_j = flip(c, dc) * 4 + flip_l(dl)
        push(WSQ.at[peer_j], RQ.at[t, j], dev(dc=dc, dl=dl), sem_wq + dc * 4 + dl)
    RQ[t, j] = WSQ[j]

    class Gather:
        def __init__(self, buf):
            self.buf, self.far, self.near = buf, slots(4), slots(4)

        def start(self):
            for dl in (1, 2, 3):
                push(self.buf.at[j], self.buf.at[j], dev(dl=dl), self.far + dl)
            push(self.buf.at[j], self.buf.at[j], dev(dc=1), self.near)

        def forward(self, dl):
            block = self.buf.at[c * 4 + flip_l(dl)]
            arrive(block, self.far + dl)
            push(block, block, dev(dc=1), self.near + dl)

        def sibling(self, dl):
            arrive(self.buf.at[(1 - c) * 4 + flip_l(dl)], self.near + dl)

    @pl.when(jnp.logical_not(native))
    def _():
        arrive(SG.at[j], sem_ps)

    sem_sg = slots(8)
    for dc, dl in group_masks:
        push(SG.at[j], SG.at[j], dev(dc=dc, dl=dl), sem_sg + dc * 4 + dl)

    @pl.when(jnp.logical_not(native))
    def _():
        arrive(X.at[j], sem_px)

    gather_x = Gather(X)
    gather_x.start()

    q_own = x * 4 + c * 2 + zh
    slab = pkin[...]
    for dl in (1, 2, 3):
        arrive(SP.at[dl], sem_s1 + dl)
        slab += SP[dl]
    FULL[q_own] = slab
    sem_s2 = slots(8)
    for dx, dc, dzh in line_masks:
        push(FULL.at[q_own], FULL.at[q_own], dev(dx=dx, dc=dc, dzh=dzh), sem_s2 + dx * 4 + dc * 2 + dzh)

    class Spread:
        def __init__(self, buf):
            self.buf, self.sem = buf, slots(3)

        def start(self):
            block = self.buf.at[t]
            push(block, block, dev(dzh=1), self.sem)
            push(block, block, dev(dx=1), self.sem + 1)

        def forward(self):
            block = self.buf.at[x * 2 + 1 - zh]
            arrive(block, self.sem)
            push(block, block, dev(dx=1), self.sem + 2)

        def finish(self):
            arrive(self.buf.at[(1 - x) * 2 + zh], self.sem + 1)
            arrive(self.buf.at[(1 - x) * 2 + 1 - zh], self.sem + 2)

    for dc, dl in group_masks:
        arrive(RQ.at[t, flip(c, dc) * 4 + flip_l(dl)], sem_wq + dc * 4 + dl)
    spread_q = Spread(RQ)
    spread_q.start()

    for dx, dc, dzh in line_masks:
        arrive(FULL.at[flip(x, dx) * 4 + flip(c, dc) * 2 + flip(zh, dzh)], sem_s2 + dx * 4 + dc * 2 + dzh)
    for q in range(8):
        PV[:, q * LANES : (q + 1) * LANES] = FULL[q]
    gain1, shift1 = PV[0:1, :], PV[1:2, :]

    def norm_rows(value, gain, shift):
        average = jnp.mean(value, axis=-1, keepdims=True)
        centered = value - average
        root = lax.rsqrt(jnp.mean(centered * centered, axis=-1, keepdims=True) + EPSILON)
        normal = centered * root
        return normal, root, normal * gain + shift

    def norm_one(block):
        def body(i, carry):
            rows = pl.ds(pl.multiple_of(i * 32, 32), 32)
            N1[block, rows] = norm_rows(X[block, rows].astype(F32), gain1, shift1)[2].astype(BF16)
            return carry

        lax.fori_loop(0, ROWS // 32, body, 0)

    norm_one(j)
    for dl in (1, 2):
        gather_x.forward(dl)
    gather_x.sibling(0)
    norm_one((1 - c) * 4 + l)
    norm_one(c * 4 + flip_l(1))
    gather_x.forward(3)
    norm_one(c * 4 + flip_l(2))
    spread_q.forward()

    @pl.when(native)
    def _():
        GM[j] = cin[...]

    @pl.when(jnp.logical_not(native))
    def _():
        send(cin, GM.at[their_block], partner, sem_pc)

    sem_wi = slots(8)
    for jj in range(8):
        for ch in range(4):
            flat = (ch // 2) * 16 + (jj // 4) * 8 + (ch % 2) * 4 + jj % 4
            WSI[jj, ch] = wi[:, flat * LANES : (flat + 1) * LANES]
    for dc, dl in group_masks:
        peer_j = flip(c, dc) * 4 + flip_l(dl)
        push(WSI.at[peer_j], RI.at[t, j], dev(dc=dc, dl=dl), sem_wi + dc * 4 + dl)
    RI[t, j] = WSI[j]
    WD[t] = wd[...]

    sem_wo, sem_wt = slots(4), slots(4)
    pair_l = c * 2 + zh
    to_self = jnp.logical_and(x == c, l == pair_l)
    is_root = jnp.logical_and(x == c, zh == y)
    root_mask = jnp.abs(x - c) * 2 + jnp.abs(zh - y)

    @pl.when(to_self)
    def _():
        WO[l] = wo[...]

    @pl.when(jnp.logical_not(to_self))
    def _():
        send(wo, WO.at[l], (x * 2 + x, zh * 4 + pair_l), sem_wo + l)

    for dl in (1, 2, 3):
        gather_x.sibling(dl)
        norm_one((1 - c) * 4 + flip_l(dl))
    norm_one(c * 4 + flip_l(3))

    for dc, dl in group_masks:
        arrive(SG.at[flip(c, dc) * 4 + flip_l(dl)], sem_sg + dc * 4 + dl)
    lens = SG[j, 1:2, :]
    row_ids = lax.broadcasted_iota(jnp.int32, (LANES, LANES), 0)
    lane_ids = lax.broadcasted_iota(jnp.int32, (LANES, LANES), 1)
    label_row = lane_ids.astype(F32)
    label_col = row_ids.astype(F32)
    earlier = (lane_ids < row_ids).astype(BF16)
    running = jnp.zeros((1, LANES), F32)
    for blk in range(8):
        onehot = (label_col == SG[blk, 0:1, :]).astype(F32).T
        before = dot(earlier, onehot.astype(BF16)) + running
        running = running + jnp.sum(onehot, axis=0, keepdims=True)
        rank = jnp.sum(before * onehot, axis=1, keepdims=True)
        limit = jnp.sum(onehot * lens, axis=1, keepdims=True)
        ident = jnp.sum(label_row * onehot, axis=1, keepdims=True)
        CODE[blk] = jnp.broadcast_to(jnp.where(rank < limit, ident, -1.0), (ROWS, LANES))

    @pl.when(jnp.logical_not(native))
    def _():
        arrive(GM.at[j], sem_pc)

    is_real = CODE[j][:, 0:1] >= 0.0
    GM[j] = jnp.where(is_real, GM[j].astype(F32), 0.0).astype(BF16)
    gather_g = Gather(GM)

    spread_q.finish()
    for i in range(32):
        for ch in range(3):
            WQ[i * 32 : (i + 1) * 32, ch * LANES : (ch + 1) * LANES] = RQ[
                (i // 16) * 2 + (i // 4) % 2, ((i // 8) % 2) * 4 + i % 4, ch]
    gather_g.start()
    bias_q, bias_v = FULL[j][2:3, :], FULL[j][3:4, :]

    def project(k, carry):
        rows = pl.ds(pl.multiple_of(k * 256, 256), 256)
        normed = N1[pl.ds(k * 2, 2)].reshape(256, D)
        mixed = dot(normed, WQ[...])
        queries = (mixed[:, :LANES] + bias_q).astype(BF16).astype(F32) * (HEAD_DIM ** -0.5)
        keys = mixed[:, LANES : 2 * LANES]
        values = mixed[:, 2 * LANES :] + bias_v
        QS[rows] = queries.astype(BF16)
        KK[rows] = keys.astype(BF16)
        VV[rows] = values.astype(BF16)
        QT[:, rows] = queries.T.astype(BF16)
        KT[:, rows] = keys.T.astype(BF16)
        VT[:, rows] = values.T.astype(BF16)
        return carry

    lax.fori_loop(0, 4, project, 0)

    for slot in range(4):
        @pl.when(jnp.logical_and(is_root, jnp.logical_not(jnp.logical_and(zl == c, l == slot))))
        def _():
            arrive(WO.at[slot], sem_wo + slot)

    @pl.when(is_root)
    def _():
        for dx, dzh in ((0, 1), (1, 0), (1, 1)):
            send(WO, WO, dev(dx=dx, dzh=dzh), sem_wt + dx * 2 + dzh)

    for dc, dl in group_masks:
        arrive(RI.at[t, flip(c, dc) * 4 + flip_l(dl)], sem_wi + dc * 4 + dl)
    spread_i, spread_d = Spread(RI), Spread(WD)
    spread_i.start()
    spread_d.start()

    @pl.when(jnp.logical_not(is_root))
    def _():
        arrive(WO, sem_wt + root_mask)

    def pair_lanes(lp):
        return (pl.ds(pl.multiple_of(lp * LANES, LANES), LANES), pl.ds(pl.multiple_of(512 + lp * LANES, LANES), LANES))

    def cat_lanes(ref, lp):
        first, second = pair_lanes(lp)
        return jnp.concatenate([ref[:, first], ref[:, second]], axis=1)

    def cat_rows(ref, lp):
        return jnp.concatenate([ref[lp], ref[4 + lp]], axis=0)

    class Scatter:
        def __init__(self, part, chip, number, before=None):
            self.part, self.chip, self.number, self.before = part, chip, number, before
            self.near, self.far = slots(4), slots(4)

        def emit(self, m, value):
            if self.before is not None:
                left(self.part.at[m, 1 - c], self.before.near + m)
            low = value.astype(BF16)
            self.part[m, 0] = low[:ROWS]
            self.part[m, 1] = low[ROWS:]
            send(self.part.at[m, 1 - c], SB.at[self.number, m], dev(dc=1), self.near + m)

        def reduce(self, m):
            arrive(SB.at[self.number, m], self.near + m)
            if m == 0:
                return
            if self.before is not None:
                left(self.chip.at[m], self.before.far + m)
            self.chip[m] = (self.part[m, c].astype(F32) + SB[self.number, m].astype(F32)).astype(BF16)
            send(self.chip.at[m], RV.at[self.number, m], dev(dl=m), self.far + m)

        def finish(self):
            for m in (1, 2, 3):
                arrive(RV.at[self.number, m], self.far + m)

        def rows(self, rows):
            total = self.part[0, c, rows].astype(F32) + SB[self.number, 0, rows].astype(F32)
            for m in (1, 2, 3):
                total += RV[self.number, m, rows].astype(F32)
            return total

        def close(self):
            for m in range(4):
                left(self.part.at[m, 1 - c], self.near + m)
                if m:
                    left(self.chip.at[m], self.far + m)

    head_rows = lax.broadcasted_iota(jnp.int32, (LANES, 256), 0)
    head_lanes = lax.broadcasted_iota(jnp.int32, (256, LANES), 1)

    def only_rows(value, h):
        return jnp.where((head_rows >= h * 64) & (head_rows < (h + 1) * 64), value, jnp.zeros_like(value))

    def only_lanes(value, h):
        return jnp.where((head_lanes >= h * 64) & (head_lanes < (h + 1) * 64), value, jnp.zeros_like(value))

    scatter_a = Scatter(PA, CS, 0)
    attend_order = (3, 1, 2, 0)
    for k, m in enumerate(attend_order):
        lp = flip_l(m)
        queries_t = cat_lanes(QT, lp)
        seg_q = jnp.concatenate([SG[lp, 0:1, :], SG[4 + lp, 0:1, :]], axis=1)
        for h in range(2):
            masked_t = only_rows(queries_t.astype(F32), h).astype(BF16)

            def score(i, top):
                rows = pl.ds(pl.multiple_of(i * ROWS, ROWS), ROWS)
                value = dot(KK[rows], masked_t)
                code = CODE[i]
                allowed = jnp.concatenate([code, code], axis=1) == seg_q
                value = jnp.where(allowed, value, NEGATIVE)
                SC[rows] = value
                return jnp.maximum(top, jnp.max(value.reshape(16, 8, 256), axis=0))

            top = lax.fori_loop(0, 8, score, jnp.full((8, 256), NEGATIVE, F32))
            top = jnp.max(top, axis=0, keepdims=True)

            def expo(i, total):
                rows = pl.ds(pl.multiple_of(i * ROWS, ROWS), ROWS)
                value = jnp.exp(SC[rows] - top)
                PT[m, h, rows] = value.astype(BF16)
                return total + jnp.sum(value.reshape(16, 8, 256), axis=0)

            total = lax.fori_loop(0, 8, expo, jnp.zeros((8, 256), F32))
            inverse = 1.0 / jnp.sum(total, axis=0, keepdims=True)
            INV[m, h] = jnp.broadcast_to(inverse, (8, 256))
            OT[m, h * 64 : (h + 1) * 64] = dot(VT[h * 64 : (h + 1) * 64, :], PT[m, h]) * inverse
        joined = OT[m]
        OL[m] = joined.astype(BF16)
        partial = dot(joined.T.astype(BF16), WO[...].reshape(LANES, D))
        scatter_a.emit(m, partial)
        if k:
            scatter_a.reduce(attend_order[k - 1])
        if k == 0:
            for dl in (1, 2):
                gather_g.forward(dl)
        if k == 1:
            gather_g.forward(3)
        if k == 2:
            spread_i.forward()
        if k == 3:
            spread_d.forward()
    scatter_a.reduce(0)
    scatter_a.finish()

    gain2, shift2, bias_o = PV[5:6, :], PV[6:7, :], PV[4:5, :]
    for r in range(4):
        rows = pl.ds(r * 32, 32)
        residual = X[j, rows].astype(F32) + scatter_a.rows(rows) + bias_o
        XO[rows] = residual
        normal, root, value = norm_rows(residual, gain2, shift2)
        N2F[rows] = normal
        RS_[rows] = jnp.broadcast_to(root, (32, LANES))
        N2[j, rows] = value.astype(BF16)
    gather_n = Gather(N2)
    gather_n.start()

    spread_i.finish()
    spread_d.finish()
    for i in range(32):
        for ch in range(4):
            WI[i * 32 : (i + 1) * 32, ch * LANES : (ch + 1) * LANES] = RI[
                (i // 16) * 2 + (i // 4) % 2, ((i // 8) % 2) * 4 + i % 4, ch]
    for dl in range(4):
        gather_g.sibling(dl)
    pick = lax.broadcasted_iota(jnp.int32, (16, LANES), 0) == 8 + l
    bias_in = jnp.concatenate(
        [
            jnp.sum(jnp.where(pick, FULL[(ch // 2) * 4 + c * 2 + ch % 2], 0.0), axis=0, keepdims=True)
            for ch in range(4)
        ],
        axis=1,
    )
    scatter_m = Scatter(PA, CS, 1, scatter_a)
    scatter_b = Scatter(PB, CSB, 2)
    BG[0:1] = jnp.zeros((1, 512), F32)

    def mlp(m):
        lp = flip_l(m)
        first, second = pair_lanes(lp)
        hidden = dot(cat_rows(N2, lp), WI[...]) + bias_in
        phi_cap = 0.5 * (1.0 + lax.erf(hidden * 0.7071067811865476))
        phi = jnp.exp(-0.5 * hidden * hidden) * 0.3989422804014327
        act = hidden * phi_cap
        slope = phi_cap + hidden * phi
        HA[m] = act.astype(BF16)
        act_t = act.T.astype(BF16)
        HAT[:, first] = act_t[:, :ROWS]
        HAT[:, second] = act_t[:, ROWS:]
        grad_act = dot_nt(cat_rows(GM, lp), WD[...].reshape(512, D))
        grad_pre = (grad_act * slope).astype(BF16)
        GP[lp] = grad_pre[:ROWS]
        GP[4 + lp] = grad_pre[ROWS:]
        BG[0:1] += jnp.sum(grad_pre.astype(F32), axis=0, keepdims=True)
        scatter_m.emit(m, dot_nt(grad_pre, WI[...]))

    gather_n.sibling(0)
    mlp(0)
    gather_n.forward(1)
    gather_n.forward(2)
    scatter_m.reduce(0)
    gather_n.sibling(1)
    mlp(1)
    gather_n.forward(3)
    gather_n.sibling(2)
    mlp(2)
    scatter_m.reduce(1)
    gather_n.sibling(3)
    mlp(3)
    scatter_m.reduce(2)
    scatter_m.reduce(3)
    for k, m in enumerate((1, 2, 3, 0)):
        scatter_b.emit(m, dot(HA[m], WD[...].reshape(512, D)))
        if k:
            scatter_b.reduce((1, 2, 3, 0)[k - 1])
    scatter_b.reduce(0)
    scatter_m.finish()

    def norm_back(grad, normal, root, gain):
        scaled = grad * gain
        return root * (scaled - jnp.mean(scaled, axis=-1, keepdims=True)
                       - normal * jnp.mean(scaled * normal, axis=-1, keepdims=True))

    sums = [jnp.zeros((1, D), F32) for _ in range(4)]
    for r in range(4):
        rows = pl.ds(r * 32, 32)
        grad = scatter_m.rows(rows)
        normal = N2F[rows]
        top_grad = GM[j, rows].astype(F32)
        grad_residual = top_grad + norm_back(grad, normal, RS_[rows][:, 0:1], gain2)
        low = grad_residual.astype(BF16)
        GB[j, rows] = low
        N2F[rows] = grad_residual
        for i, value in enumerate((grad * normal, grad, low.astype(F32), top_grad)):
            sums[i] += jnp.sum(value, axis=0, keepdims=True)
    vectors = {5: sums[0], 6: sums[1], 4: sums[2], 7: sums[3]}
    gather_b = Gather(GB)
    gather_b.start()

    class Total:
        def __init__(self, part, from_x, middle, from_z):
            self.part, self.from_x, self.middle, self.from_z = part, from_x, middle, from_z
            self.sem = slots(2)

        def start(self):
            half = pl.ds((1 - x) * 2, 2)
            push(self.part.at[half], self.from_x, dev(dx=1), self.sem)

        def second(self):
            arrive(self.from_x, self.sem)
            self.middle[...] = (
                self.part[x * 2 + 1 - zh].astype(F32) + self.from_x[1 - zh].astype(F32)
            ).astype(BF16)
            push(self.middle, self.from_z, dev(dzh=1), self.sem + 1)

        def result(self):
            arrive(self.from_z, self.sem + 1)
            return self.part[t].astype(F32) + self.from_x[zh].astype(F32) + self.from_z[...].astype(F32)

    total_d = Total(GD, XD, HD, ZD)
    total_i = Total(GI, XI, HI, ZI)
    total_q = Total(GQ, XQ, HQ, ZQ)
    for ch in range(4):
        GD[ch] = dot(HAT[ch * LANES : (ch + 1) * LANES, :], GM[...].reshape(8 * ROWS, D)).astype(BF16)
    total_d.start()
    gather_b.forward(1)
    gather_b.forward(2)
    all_pre = GP[...].reshape(8 * ROWS, 512)
    for blk in range(8):
        product = dot_tn(N2[:, :, blk * LANES : (blk + 1) * LANES].reshape(8 * ROWS, LANES), all_pre).astype(BF16)
        for r in range(4):
            i = blk * 4 + r
            for ch in range(4):
                GI[(i // 16) * 2 + (i // 4) % 2, ((i // 8) % 2) * 4 + i % 4, ch] = product[
                    r * 32 : (r + 1) * 32, ch * LANES : (ch + 1) * LANES]
    total_i.start()
    gather_b.forward(3)

    bias_d = PV[7:8, :]
    sem_out, sem_in = slots(), slots()
    scatter_b.finish()
    for r in range(4):
        rows = pl.ds(r * 32, 32)
        CSB[0, rows] = (XO[rows] + scatter_b.rows(rows) + bias_d).astype(BF16)

    @pl.when(native)
    def _():
        out_block[...] = CSB[0]

    @pl.when(jnp.logical_not(native))
    def _():
        send(CSB.at[0], out_block, partner, sem_out)

    DK[...] = jnp.zeros_like(DK)
    DV[...] = jnp.zeros_like(DV)
    GOF[...] = jnp.zeros_like(GOF)
    for k, m in enumerate((0, 1, 2, 3)):
        gather_b.sibling(m)
        lp = flip_l(m)
        first, second = pair_lanes(lp)
        branch = cat_rows(GB, lp)
        grad_att = dot_nt(branch, WO[...].reshape(LANES, D)).astype(BF16).astype(F32)
        GOF[...] += dot(OL[m], branch)
        grad_att_t = grad_att.T
        both = grad_att_t * OT[m]
        queries = jnp.concatenate([QS[first], QS[second]], axis=0).astype(F32)
        for h in range(2):
            inverse = INV[m, h][0:1]
            delta = jnp.sum(both[h * 64 : (h + 1) * 64], axis=0, keepdims=True) * inverse
            scaled_t = only_rows(grad_att_t * inverse, h)
            scaled_low_t = scaled_t.astype(BF16)
            scaled_low = scaled_t.T.astype(BF16)
            queries_h = only_lanes(queries, h).astype(BF16)

            def back(i, carry):
                rows = pl.ds(i * ROWS, ROWS)
                probs = PT[m, h, rows]
                value = dot(VV[rows], scaled_low_t)
                grad_scores = (probs.astype(F32) * (value - delta)).astype(BF16)
                DV[rows] += dot(probs, scaled_low)
                DK[rows] += dot(grad_scores, queries_h)
                PT[m, h, rows] = grad_scores
                return carry

            for i in range(8):
                back(i, 0)
            DQ[h * 64 : (h + 1) * 64, :] = dot(KT[h * 64 : (h + 1) * 64, :], PT[m, h]) * (HEAD_DIM ** -0.5)
        dq_rows = DQ[...].T.astype(BF16)
        GMX[lp, :, 0:LANES] = dq_rows[:ROWS]
        GMX[4 + lp, :, 0:LANES] = dq_rows[ROWS:]
        if k == 0:
            total_d.second()
        if k == 2:
            total_i.second()

    GO[...] = GOF[...].astype(BF16)
    sem_go, sem_gs = slots(4), slots(4)

    @pl.when(jnp.logical_not(is_root))
    def _():
        send(GO, XGO.at[root_mask], (c * 2 + c, y * 4 + l), sem_go + root_mask)

    for blk in range(8):
        rows = pl.ds(blk * ROWS, ROWS)
        GMX[blk, :, LANES : 2 * LANES] = DK[rows].astype(BF16)
        GMX[blk, :, 2 * LANES :] = DV[rows].astype(BF16)

    scatter_n = Scatter(PA, CS, 3, scatter_m)
    for k, m in enumerate(attend_order):
        scatter_n.emit(m, dot_nt(cat_rows(GMX, flip_l(m)), WQ[...]))
        if k:
            scatter_n.reduce(attend_order[k - 1])
    all_mixed = GMX[...].reshape(8 * ROWS, 3 * LANES)
    for blk in range(8):
        product = dot_tn(N1[:, :, blk * LANES : (blk + 1) * LANES].reshape(8 * ROWS, LANES), all_mixed).astype(BF16)
        for r in range(4):
            i = blk * 4 + r
            for ch in range(3):
                GQ[(i // 16) * 2 + (i // 4) % 2, ((i // 8) % 2) * 4 + i % 4, ch] = product[
                    r * 32 : (r + 1) * 32, ch * LANES : (ch + 1) * LANES]
        if blk == 1:
            scatter_n.reduce(0)
    total_q.start()

    out_d[...] = total_d.result()
    TI[...] = total_i.result().astype(BF16)
    sem_ti, sem_tq = slots(8), slots(8)
    for dc, dl in group_masks:
        peer_j = flip(c, dc) * 4 + flip_l(dl)
        push(TI.at[peer_j], RGI.at[j], dev(dc=dc, dl=dl), sem_ti + dc * 4 + dl)
    RGI[j] = TI[j]

    @pl.when(is_root)
    def _():
        total = GOF[...]
        for mask in (1, 2, 3):
            arrive(XGO.at[mask], sem_go + mask)
            total += XGO[mask].astype(F32)
        TGO[...] = total.astype(BF16).reshape(4, 32, D)
        for slot in range(4):
            mine = jnp.logical_and(zl == c, l == slot)

            @pl.when(mine)
            def _():
                RGO[...] = TGO[slot]

            @pl.when(jnp.logical_not(mine))
            def _():
                send(TGO.at[slot], RGO, (x * 2 + zl, zh * 4 + slot), sem_gs + slot)

    scatter_n.finish()
    sums = [jnp.zeros((1, D), F32) for _ in range(2)]
    for r in range(4):
        rows = pl.ds(r * 32, 32)
        grad = scatter_n.rows(rows)
        normal, root, _ = norm_rows(X[j, rows].astype(F32), gain1, shift1)
        XO[rows] = N2F[rows] + norm_back(grad, normal, root, gain1)
        for i, value in enumerate((grad * normal, grad)):
            sums[i] += jnp.sum(value, axis=0, keepdims=True)
    vectors[0], vectors[1] = sums
    left(CSB.at[1], scatter_b.far + 1)
    CSB[1] = XO[...].astype(BF16)

    @pl.when(native)
    def _():
        out_input[...] = CSB[1]

    @pl.when(jnp.logical_not(native))
    def _():
        send(CSB.at[1], out_input, partner, sem_in)

    mixed_sums = jnp.sum(all_mixed.astype(F32), axis=0, keepdims=True)
    for q in range(8):
        VG[q] = jnp.zeros((16, LANES), F32)
        for p in (0, 1, 4, 5, 6, 7):
            VG[q, p : p + 1] = vectors[p][:, q * LANES : (q + 1) * LANES]
        for p, ch in ((2, 0), (3, 2)):
            VG[q, p : p + 1] = jnp.where(j == q, mixed_sums[:, ch * LANES : (ch + 1) * LANES], 0.0)
        ch = (q // 4) * 2 + q % 2
        for r in range(4):
            here = jnp.logical_and(c == (q // 2) % 2, l == r)
            VG[q, 8 + r : 9 + r] = jnp.where(here, BG[0:1, ch * LANES : (ch + 1) * LANES], 0.0)
    sem_v1, sem_v2 = slots(8), slots(4)
    for dx, dc, dzh in line_masks:
        mask = dx * 4 + dc * 2 + dzh
        push(VG.at[flip(x, dx) * 4 + flip(c, dc) * 2 + flip(zh, dzh)], VR.at[mask], dev(dx=dx, dc=dc, dzh=dzh), sem_v1 + mask)

    total_q.second()
    for dc, dl in group_masks:
        arrive(RGI.at[flip(c, dc) * 4 + flip_l(dl)], sem_ti + dc * 4 + dl)
    for jj in range(8):
        for ch in range(4):
            flat = (ch // 2) * 16 + (jj // 4) * 8 + (ch % 2) * 4 + jj % 4
            out_i[:, flat * LANES : (flat + 1) * LANES] = RGI[jj, ch].astype(F32)

    slab = VG[q_own]
    for dx, dc, dzh in line_masks:
        mask = dx * 4 + dc * 2 + dzh
        arrive(VR.at[mask], sem_v1 + mask)
        slab += VR[mask]
    SL[...] = slab
    for dl in (1, 2, 3):
        push(SL, SLR.at[dl], dev(dl=dl), sem_v2 + dl)

    from_self = jnp.logical_and(x == c, l == pair_l)

    @pl.when(jnp.logical_not(from_self))
    def _():
        arrive(RGO, sem_gs + l)

    out_o[...] = RGO[...].astype(F32)

    TQ[...] = total_q.result().astype(BF16)
    for dc, dl in group_masks:
        peer_j = flip(c, dc) * 4 + flip_l(dl)
        push(TQ.at[peer_j], RGQ.at[j], dev(dc=dc, dl=dl), sem_tq + dc * 4 + dl)
    RGQ[j] = TQ[j]

    for dl in (1, 2, 3):
        arrive(SLR.at[dl], sem_v2 + dl)
        slab += SLR[dl]
    out_small[...] = slab

    for dc, dl in group_masks:
        arrive(RGQ.at[flip(c, dc) * 4 + flip_l(dl)], sem_tq + dc * 4 + dl)
    for jj in range(8):
        for ch in range(3):
            out_q[:, ch * D + jj * LANES : ch * D + (jj + 1) * LANES] = RGQ[jj, ch].astype(F32)

    @pl.when(jnp.logical_not(native))
    def _():
        left(sgin, sem_ps)
        left(xin, sem_px)
        left(cin, sem_pc)
        left(CSB.at[0], sem_out)
        left(CSB.at[1], sem_in)
        arrive(out_block, sem_out)
        arrive(out_input, sem_in)

    @pl.when(jnp.logical_not(to_self))
    def _():
        left(wo, sem_wo + l)

    @pl.when(jnp.logical_not(is_root))
    def _():
        left(GO, sem_go + root_mask)

    @pl.when(is_root)
    def _():
        for mask in (1, 2, 3):
            left(WO, sem_wt + mask)
        for slot in range(4):
            @pl.when(jnp.logical_not(jnp.logical_and(zl == c, l == slot)))
            def _():
                left(TGO.at[slot], sem_gs + slot)

    scatter_n.close()
    for m in range(4):
        left(PB.at[m, 1 - c], scatter_b.near + m)
        if m > 1:
            left(CSB.at[m], scatter_b.far + m)
    for copy in pending:
        copy.wait_send()


def fused_scratch(copies):
    def v(*shape, dtype=BF16):
        return pltpu.VMEM(shape, dtype)

    def f(*shape):
        return pltpu.VMEM(shape, F32)

    blocks = (8, ROWS, D)
    return [
        v(*blocks), v(*blocks), v(*blocks), v(*blocks), v(*blocks),
        f(8, 8, LANES), f(4, 16, LANES), f(8, 16, LANES), f(16, D),
        v(8, 3, 32, LANES), v(4, 8, 3, 32, LANES), v(D, 3 * LANES), v(4, 32, D),
        v(8, 4, 32, LANES), v(4, 8, 4, 32, LANES), v(D, 512), v(4, LANES, D),
        v(D, LANES), v(D, LANES), v(D, LANES), v(LANES, D), v(LANES, D), v(LANES, D),
        f(8, ROWS, LANES), f(D, 256), v(4, 2, D, 256), f(4, 2, 8, 256),
        f(4, LANES, 256), v(4, LANES, 256),
        v(4, 2, ROWS, D), v(4, ROWS, D), v(4, 2, ROWS, D), v(4, ROWS, D),
        v(4, 4, ROWS, D), v(4, 4, ROWS, D), f(ROWS, D), f(ROWS, D),
        v(512, D), v(4, 256, 512), v(8, ROWS, 512),
        f(D, LANES), f(D, LANES), f(LANES, 256), v(8, ROWS, 3 * LANES),
        v(4, 8, 3, 32, LANES), v(4, 8, 4, 32, LANES), v(4, LANES, D),
        v(2, 8, 3, 32, LANES), v(2, 8, 4, 32, LANES), v(2, LANES, D),
        v(8, 3, 32, LANES), v(8, 4, 32, LANES), v(LANES, D),
        v(8, 3, 32, LANES), v(8, 4, 32, LANES), v(LANES, D),
        v(8, 3, 32, LANES), v(8, 4, 32, LANES),
        v(8, 3, 32, LANES), v(8, 4, 32, LANES),
        v(LANES, D), f(LANES, D), v(4, LANES, D), v(4, 32, D), v(32, D),
        f(8, 16, LANES), f(8, 16, LANES), f(16, LANES), f(4, 16, LANES), f(ROWS, LANES), f(8, 512),
        pltpu.SemaphoreType.DMA((copies,)),
        pltpu.SemaphoreType.DMA((copies,)),
    ]


def fused_shards(
    block_in,
    attention_norm_gain,
    attention_norm_bias,
    query_key_value,
    query_bias,
    value_bias,
    output_weight,
    output_bias,
    mlp_norm_gain,
    mlp_norm_bias,
    mlp_in_weight,
    mlp_in_bias,
    mlp_out_weight,
    mlp_out_bias,
    cotangent,
    segment_ids,
    sub_lengths,
):
    place = lax.rem(lax.axis_index("band"), 4)
    small = jnp.stack(
        [
            attention_norm_gain, attention_norm_bias, query_bias, value_bias,
            output_bias, mlp_norm_gain, mlp_norm_bias, mlp_out_bias,
        ]
    ).astype(F32)
    spread = (jnp.arange(LANES) // 32 == place)[None, :]
    packed = jnp.concatenate(
        [
            jnp.where(spread, jnp.tile(small, (1, 4)), 0.0),
            jnp.where((jnp.arange(8) == place)[:, None], mlp_in_bias.astype(F32)[None, :], 0.0),
        ]
    )
    slots = jnp.concatenate(
        [
            segment_ids.astype(F32),
            jnp.pad(sub_lengths.astype(F32), ((0, 6), (0, LANES - SUBGRIDS))),
        ]
    )
    copies = 200
    vmem = pl.BlockSpec(memory_space=pltpu.VMEM)
    block, grad_in, grad_q, grad_o, grad_i, grad_d, grad_small = pl.pallas_call(
        functools.partial(fused_kernel, copies),
        out_shape=(
            jax.ShapeDtypeStruct((ROWS, D), BF16),
            jax.ShapeDtypeStruct((ROWS, D), BF16),
            jax.ShapeDtypeStruct((32, 3 * D), F32),
            jax.ShapeDtypeStruct((32, D), F32),
            jax.ShapeDtypeStruct((32, 4 * D), F32),
            jax.ShapeDtypeStruct((LANES, D), F32),
            jax.ShapeDtypeStruct((16, LANES), F32),
        ),
        in_specs=[vmem] * 8,
        out_specs=(vmem,) * 7,
        scratch_shapes=fused_scratch(copies),
        compiler_params=pltpu.CompilerParams(
            collective_id=0, has_side_effects=True, vmem_limit_bytes=63 * 2**20
        ),
    )(
        block_in[0], cotangent[0], slots, packed,
        query_key_value, output_weight, mlp_in_weight, mlp_out_weight,
    )
    mine = lax.dynamic_slice(grad_small, (0, place * 32), (8, 32))
    grad_up_bias = lax.dynamic_index_in_dim(grad_small, 8 + place, 0, False)
    return (
        block[None], grad_in[None], mine[0], mine[1], grad_q, mine[2], mine[3], grad_o,
        mine[4], mine[5], mine[6], grad_i, grad_up_bias, grad_d, mine[7],
    )


def solution(mesh):
    small_slice = dict(mesh.shape) == {"seq": 4, "band": 8}
    return jax.shard_map(
        fused_shards if small_slice else shards,
        mesh=mesh,
        in_specs=(
            P("seq", "band", None),
            P(("seq", "band")),
            P(("seq", "band")),
            P(("seq", "band"), None),
            P(("seq", "band")),
            P(("seq", "band")),
            P(("seq", "band"), None),
            P(("seq", "band")),
            P(("seq", "band")),
            P(("seq", "band")),
            P(("seq", "band"), None),
            P(("seq", "band")),
            P(("seq", "band"), None),
            P(("seq", "band")),
            P("seq", "band", None),
            P("seq", "band"),
            P("seq", None),
        ),
        out_specs=(
            P("seq", "band", None),
            P("seq", "band", None),
            P(("seq", "band")),
            P(("seq", "band")),
            P(("seq", "band"), None),
            P(("seq", "band")),
            P(("seq", "band")),
            P(("seq", "band"), None),
            P(("seq", "band")),
            P(("seq", "band")),
            P(("seq", "band")),
            P(("seq", "band"), None),
            P(("seq", "band")),
            P(("seq", "band"), None),
            P(("seq", "band")),
        ),
        check_vma=False,
    )
```

```python
import functools
import math

import jax
import jax.numpy as jnp
from jax import lax
from jax.experimental import pallas as pl
from jax.experimental.pallas import tpu as pltpu
from jax.sharding import PartitionSpec as P

D = 1024
HEADS = 16
HEAD_DIM = 64
SUBGRIDS = 8


EPSILON = 1e-05
NEGATIVE = -1e30


def prefix(part, axis, combine, identity):
    place = lax.axis_index(axis)
    gathered = lax.all_gather(part, axis)
    state = jnp.zeros_like(part) + jnp.asarray(identity, part.dtype)

    def one(lap, state):
        return combine(state, lax.dynamic_index_in_dim(gathered, lap, 0, False))

    return lax.fori_loop(0, place, one, state)


def layer_norm(values_in, norm_gain, norm_shift):
    average = jnp.mean(values_in, axis=-1, keepdims=True)
    centered = values_in - average
    variance = jnp.mean(centered * centered, axis=-1, keepdims=True)
    return centered * lax.rsqrt(variance + EPSILON) * norm_gain + norm_shift


def gelu_exact(values_in):
    return jax.nn.gelu(values_in, approximate=False)


def add_counts(first_part, second_part):
    return first_part + second_part


def block_scores(query_part, key_part, seg_part, code_part, scale_factor):
    scores = (
        jnp.einsum("qhe,khe->hqk", query_part, key_part, preferred_element_type=jnp.float32)
        * scale_factor
    )
    allowed = (seg_part[:, None] == code_part[None, :])[None]
    return (jnp.where(allowed, scores, NEGATIVE), allowed)


def split_blocks(array_in, block_rows):
    return array_in.reshape((array_in.shape[0] // block_rows, block_rows) + array_in.shape[1:])


def shards(
    block_in,
    attention_norm_gain,
    attention_norm_bias,
    query_key_value,
    query_bias,
    value_bias,
    output_weight,
    output_bias,
    mlp_norm_gain,
    mlp_norm_bias,
    mlp_in_weight,
    mlp_in_bias,
    mlp_out_weight,
    mlp_out_bias,
    cotangent,
    segment_ids,
    sub_lengths,
):
    float_type = jnp.float32
    half_type = jnp.bfloat16
    rows_local = block_in.shape[1]
    seq_length = rows_local * lax.axis_size("band")
    scale_factor = HEAD_DIM ** (-0.5)
    block_rows = math.gcd(seq_length, 1024)
    seg_local = segment_ids[0]
    labels = jnp.arange(SUBGRIDS, dtype=jnp.int32)
    onehot_ids = (seg_local[:, None] == labels[None, :]).astype(jnp.int32)
    earlier_counts = prefix(
        jnp.sum(onehot_ids, axis=0), "band", add_counts, jnp.zeros((SUBGRIDS,), jnp.int32)
    )
    slots = jnp.arange(rows_local)
    earlier = (slots[None, :] < slots[:, None]).astype(float_type)
    before = (
        jnp.dot(earlier, onehot_ids.astype(float_type), precision=lax.Precision.HIGHEST).astype(
            jnp.int32
        )
        + earlier_counts[None, :]
    )
    patch_rank = jnp.sum(before * onehot_ids, axis=1)
    limits = jnp.sum(onehot_ids * sub_lengths[0][None, :], axis=1)
    realness = patch_rank < limits
    key_codes = jnp.where(realness, seg_local, -1)
    gathered = (
        lax.all_gather(attention_norm_gain, ("seq", "band"), axis=0, tiled=True),
        lax.all_gather(attention_norm_bias, ("seq", "band"), axis=0, tiled=True),
        lax.all_gather(query_key_value, ("seq", "band"), axis=0, tiled=True),
        lax.all_gather(query_bias, ("seq", "band"), axis=0, tiled=True),
        lax.all_gather(value_bias, ("seq", "band"), axis=0, tiled=True),
        lax.all_gather(output_weight, ("seq", "band"), axis=0, tiled=True),
        lax.all_gather(output_bias, ("seq", "band"), axis=0, tiled=True),
        lax.all_gather(mlp_norm_gain, ("seq", "band"), axis=0, tiled=True),
        lax.all_gather(mlp_norm_bias, ("seq", "band"), axis=0, tiled=True),
        lax.all_gather(mlp_in_weight, ("seq", "band"), axis=0, tiled=True),
        lax.all_gather(mlp_in_bias, ("seq", "band"), axis=0, tiled=True),
        lax.all_gather(mlp_out_weight, ("seq", "band"), axis=0, tiled=True),
        lax.all_gather(mlp_out_bias, ("seq", "band"), axis=0, tiled=True),
    )
    (
        gain_one,
        shift_one,
        joint_weight,
        bias_query,
        bias_value,
        proj_weight,
        proj_bias,
        gain_two,
        shift_two,
        up_weight,
        up_bias,
        down_weight,
        down_bias,
    ) = gathered
    inputs = block_in[0].astype(float_type)
    normed_float, norm_pull_one = jax.vjp(
        layer_norm, inputs, gain_one.astype(float_type), shift_one.astype(float_type)
    )
    normed_one = normed_float.astype(half_type)
    mixed_all = jnp.dot(normed_one, joint_weight, preferred_element_type=float_type)
    queries = (mixed_all[:, :D] + bias_query.astype(float_type)).astype(half_type)
    keys_local = mixed_all[:, D : 2 * D].astype(half_type)
    values_local = (mixed_all[:, 2 * D :] + bias_value.astype(float_type)).astype(half_type)
    keys_seq, values_seq, codes_seq = (
        lax.all_gather(keys_local, "band", axis=0, tiled=True),
        lax.all_gather(values_local, "band", axis=0, tiled=True),
        lax.all_gather(key_codes, "band", axis=0, tiled=True),
    )
    query_heads = queries.reshape(rows_local, HEADS, HEAD_DIM)
    key_blocks = split_blocks(keys_seq.reshape(seq_length, HEADS, HEAD_DIM), block_rows)
    value_blocks = split_blocks(values_seq.reshape(seq_length, HEADS, HEAD_DIM), block_rows)
    code_blocks = split_blocks(codes_seq, block_rows)

    def stats_step(running, block_items):
        top_now, total_now = running
        key_part, code_part = block_items
        scores, allowed = block_scores(query_heads, key_part, seg_local, code_part, scale_factor)
        top_new = jnp.maximum(top_now, jnp.max(scores, axis=-1))
        exp_terms = jnp.where(allowed, jnp.exp(scores - top_new[..., None]), 0.0)
        return (
            (top_new, total_now * jnp.exp(top_now - top_new) + jnp.sum(exp_terms, axis=-1)),
            None,
        )

    start_stats = (
        jnp.full((HEADS, rows_local), NEGATIVE, float_type),
        jnp.zeros((HEADS, rows_local), float_type),
    )
    (top_final, total_final), unused_stats = lax.scan(
        stats_step, start_stats, (key_blocks, code_blocks)
    )
    log_total = top_final + jnp.log(total_final)

    def value_step(accum_out, block_items):
        key_part, value_part, code_part = block_items
        scores, allowed = block_scores(query_heads, key_part, seg_local, code_part, scale_factor)
        soft_probs = jnp.where(allowed, jnp.exp(scores - log_total[..., None]), 0.0).astype(
            half_type
        )
        return (
            accum_out
            + jnp.einsum("hqk,khe->qhe", soft_probs, value_part, preferred_element_type=float_type),
            None,
        )

    attended, unused_values = lax.scan(
        value_step,
        jnp.zeros((rows_local, HEADS, HEAD_DIM), float_type),
        (key_blocks, value_blocks, code_blocks),
    )
    attended_low = attended.reshape(rows_local, D).astype(half_type)
    residual = (
        inputs
        + jnp.dot(attended_low, proj_weight, preferred_element_type=float_type)
        + proj_bias.astype(float_type)
    )
    normed_float_two, norm_pull_two = jax.vjp(
        layer_norm, residual, gain_two.astype(float_type), shift_two.astype(float_type)
    )
    normed_two = normed_float_two.astype(half_type)
    hidden_pre = jnp.dot(normed_two, up_weight, preferred_element_type=float_type) + up_bias.astype(
        float_type
    )
    hidden_value, gelu_pull = jax.vjp(gelu_exact, hidden_pre)
    hidden_act = hidden_value.astype(half_type)
    block_result = (
        residual
        + jnp.dot(hidden_act, down_weight, preferred_element_type=float_type)
        + down_bias.astype(float_type)
    )
    gathered_back = (
        lax.all_gather(attention_norm_gain, ("seq", "band"), axis=0, tiled=True),
        lax.all_gather(attention_norm_bias, ("seq", "band"), axis=0, tiled=True),
        lax.all_gather(query_key_value, ("seq", "band"), axis=0, tiled=True),
        lax.all_gather(query_bias, ("seq", "band"), axis=0, tiled=True),
        lax.all_gather(value_bias, ("seq", "band"), axis=0, tiled=True),
        lax.all_gather(output_weight, ("seq", "band"), axis=0, tiled=True),
        lax.all_gather(output_bias, ("seq", "band"), axis=0, tiled=True),
        lax.all_gather(mlp_norm_gain, ("seq", "band"), axis=0, tiled=True),
        lax.all_gather(mlp_norm_bias, ("seq", "band"), axis=0, tiled=True),
        lax.all_gather(mlp_in_weight, ("seq", "band"), axis=0, tiled=True),
        lax.all_gather(mlp_in_bias, ("seq", "band"), axis=0, tiled=True),
        lax.all_gather(mlp_out_weight, ("seq", "band"), axis=0, tiled=True),
        lax.all_gather(mlp_out_bias, ("seq", "band"), axis=0, tiled=True),
    )
    joint_back = gathered_back[2]
    proj_back = gathered_back[5]
    up_back = gathered_back[9]
    down_back = gathered_back[11]
    grad_out = cotangent[0].astype(float_type) * realness[:, None].astype(float_type)
    grad_mlp = grad_out.astype(half_type)
    grad_down_weight = jnp.einsum(
        "rf,rd->fd", hidden_act, grad_mlp, preferred_element_type=float_type
    )
    grad_down_bias = jnp.sum(grad_mlp.astype(float_type), axis=0)
    grad_act = jnp.einsum("rd,fd->rf", grad_mlp, down_back, preferred_element_type=float_type)
    grad_pre = gelu_pull(grad_act)[0].astype(half_type)
    grad_up_weight = jnp.einsum(
        "rd,rf->df", normed_two, grad_pre, preferred_element_type=float_type
    )
    grad_up_bias = jnp.sum(grad_pre.astype(float_type), axis=0)
    grad_normed_two = jnp.einsum("rf,df->rd", grad_pre, up_back, preferred_element_type=float_type)
    grad_resid_part, grad_gain_two, grad_shift_two = norm_pull_two(grad_normed_two)
    grad_residual = grad_out + grad_resid_part
    grad_branch = grad_residual.astype(half_type)
    grad_proj_weight = jnp.einsum(
        "rd,re->de", attended_low, grad_branch, preferred_element_type=float_type
    )
    grad_proj_bias = jnp.sum(grad_branch.astype(float_type), axis=0)
    grad_attended = jnp.einsum(
        "re,de->rd", grad_branch, proj_back, preferred_element_type=float_type
    ).astype(half_type)
    grad_heads = grad_attended.reshape(rows_local, HEADS, HEAD_DIM)
    row_delta = jnp.sum(grad_heads.astype(float_type) * attended, axis=-1).T
    keys_back = lax.all_gather(keys_local, "band", axis=0, tiled=True)
    values_back = lax.all_gather(values_local, "band", axis=0, tiled=True)
    codes_back = lax.all_gather(key_codes, "band", axis=0, tiled=True)
    key_back_blocks = split_blocks(keys_back.reshape(seq_length, HEADS, HEAD_DIM), block_rows)
    value_back_blocks = split_blocks(values_back.reshape(seq_length, HEADS, HEAD_DIM), block_rows)
    code_back_blocks = split_blocks(codes_back, block_rows)

    def key_step(query_accum, block_items):
        key_part, value_part, code_part = block_items
        scores, allowed = block_scores(query_heads, key_part, seg_local, code_part, scale_factor)
        soft_probs = jnp.where(allowed, jnp.exp(scores - log_total[..., None]), 0.0)
        grad_probs = jnp.einsum(
            "qhe,khe->hqk", grad_heads, value_part, preferred_element_type=float_type
        )
        grad_scores = (soft_probs * (grad_probs - row_delta[..., None])).astype(half_type)
        query_accum = query_accum + jnp.einsum(
            "hqk,khe->qhe", grad_scores, key_part, preferred_element_type=float_type
        )
        return (query_accum, None)

    query_total, joined_blocks = lax.scan(
        key_step,
        jnp.zeros((rows_local, HEADS, HEAD_DIM), float_type),
        (key_back_blocks, value_back_blocks, code_back_blocks),
    )
    grad_query = (query_total * scale_factor).reshape(rows_local, D)
    query_seq = lax.all_gather(queries, "band", axis=0, tiled=True)
    grad_seq = lax.all_gather(grad_attended, "band", axis=0, tiled=True)
    total_seq = lax.all_gather(log_total, "band", axis=1, tiled=True)
    delta_seq = lax.all_gather(row_delta, "band", axis=1, tiled=True)
    seg_seq = lax.all_gather(seg_local, "band", axis=0, tiled=True)
    block_count = seq_length // block_rows
    key_heads_local = keys_local.reshape(rows_local, HEADS, HEAD_DIM)
    value_heads_local = values_local.reshape(rows_local, HEADS, HEAD_DIM)

    def query_step(running, block_items):
        key_accum, value_accum = running
        query_part, grad_part, total_part, delta_part, seg_part = block_items
        scores, allowed = block_scores(
            query_part, key_heads_local, seg_part, key_codes, scale_factor
        )
        soft_probs = jnp.where(allowed, jnp.exp(scores - total_part[..., None]), 0.0)
        grad_probs = jnp.einsum(
            "qhe,khe->hqk", grad_part, value_heads_local, preferred_element_type=float_type
        )
        grad_scores = (soft_probs * (grad_probs - delta_part[..., None])).astype(half_type)
        key_accum = key_accum + jnp.einsum(
            "hqk,qhe->khe", grad_scores, query_part, preferred_element_type=float_type
        )
        value_accum = value_accum + jnp.einsum(
            "hqk,qhe->khe",
            soft_probs.astype(half_type),
            grad_part,
            preferred_element_type=float_type,
        )
        return ((key_accum, value_accum), None)

    zero_heads = jnp.zeros((rows_local, HEADS, HEAD_DIM), float_type)
    (key_total, value_total), query_blocks = lax.scan(
        query_step,
        (zero_heads, zero_heads),
        (
            split_blocks(query_seq.reshape(seq_length, HEADS, HEAD_DIM), block_rows),
            split_blocks(grad_seq.reshape(seq_length, HEADS, HEAD_DIM), block_rows),
            total_seq.reshape(HEADS, block_count, block_rows).transpose(1, 0, 2),
            delta_seq.reshape(HEADS, block_count, block_rows).transpose(1, 0, 2),
            split_blocks(seg_seq, block_rows),
        ),
    )
    grad_key = (key_total * scale_factor).reshape(rows_local, D)
    grad_value = value_total.reshape(rows_local, D)
    grad_query_low = grad_query.astype(half_type)
    grad_value_low = grad_value.astype(half_type)
    grad_mixed = jnp.concatenate(
        [grad_query_low, grad_key.astype(half_type), grad_value_low], axis=1
    )
    grad_joint_weight = jnp.einsum(
        "rd,rm->dm", normed_one, grad_mixed, preferred_element_type=float_type
    )
    grad_bias_query = jnp.sum(grad_query_low.astype(float_type), axis=0)
    grad_bias_value = jnp.sum(grad_value_low.astype(float_type), axis=0)
    grad_normed_one = jnp.einsum(
        "rm,dm->rd", grad_mixed, joint_back, preferred_element_type=float_type
    )
    grad_input_part, grad_gain_one, grad_shift_one = norm_pull_one(grad_normed_one)
    input_grad = (grad_residual + grad_input_part).astype(half_type)
    shard_grads = (
        lax.psum_scatter(grad_gain_one, ("seq", "band"), scatter_dimension=0, tiled=True),
        lax.psum_scatter(grad_shift_one, ("seq", "band"), scatter_dimension=0, tiled=True),
        lax.psum_scatter(grad_joint_weight, ("seq", "band"), scatter_dimension=0, tiled=True),
        lax.psum_scatter(grad_bias_query, ("seq", "band"), scatter_dimension=0, tiled=True),
        lax.psum_scatter(grad_bias_value, ("seq", "band"), scatter_dimension=0, tiled=True),
        lax.psum_scatter(grad_proj_weight, ("seq", "band"), scatter_dimension=0, tiled=True),
        lax.psum_scatter(grad_proj_bias, ("seq", "band"), scatter_dimension=0, tiled=True),
        lax.psum_scatter(grad_gain_two, ("seq", "band"), scatter_dimension=0, tiled=True),
        lax.psum_scatter(grad_shift_two, ("seq", "band"), scatter_dimension=0, tiled=True),
        lax.psum_scatter(grad_up_weight, ("seq", "band"), scatter_dimension=0, tiled=True),
        lax.psum_scatter(grad_up_bias, ("seq", "band"), scatter_dimension=0, tiled=True),
        lax.psum_scatter(grad_down_weight, ("seq", "band"), scatter_dimension=0, tiled=True),
        lax.psum_scatter(grad_down_bias, ("seq", "band"), scatter_dimension=0, tiled=True),
    )
    return (
        block_result.astype(half_type)[None],
        input_grad[None],
        shard_grads[0],
        shard_grads[1],
        shard_grads[2],
        shard_grads[3],
        shard_grads[4],
        shard_grads[5],
        shard_grads[6],
        shard_grads[7],
        shard_grads[8],
        shard_grads[9],
        shard_grads[10],
        shard_grads[11],
        shard_grads[12],
    )


F32 = jnp.float32
BF16 = jnp.bfloat16
MESH_ID = pl.DeviceIdType.MESH
ROWS = 128
LANES = 128
COPIES = 240


def dot(lhs, rhs):
    return jnp.dot(lhs, rhs, preferred_element_type=F32)


def dot_nt(lhs, rhs):
    return lax.dot_general(lhs, rhs, (((1,), (1,)), ((), ())), preferred_element_type=F32)


def dot_tn(lhs, rhs):
    return lax.dot_general(lhs, rhs, (((0,), (0,)), ((), ())), preferred_element_type=F32)


def flat_column(jj, ch):
    return (ch // 2) * 16 + (jj // 4) * 8 + (ch % 2) * 4 + jj % 4


def shard_place(i):
    return (i // 16) * 2 + (i // 4) % 2, ((i // 8) % 2) * 4 + i % 4


def fused_kernel(copies, *refs):
    (
        xin, cin, seg_in, len_in, wq, wo, wi, wd,
        p0, p1, p2, p3, p4, p5, p6, p7, pb,
        out_block, out_input, out_q, out_o, out_i, out_d, out_small,
        X, N0, N1, N2, GM, GB, SGI, SG, PK, SP, FULL, PV,
        WQI, WSQ, RQ, WQ, WO, WII, WSI, RI, WI, WD,
        QS, KK, VV, QT, KT, VT, CODE, SC, PT, INV, OT, OL,
        PA, CS, PB, CSB, SB, RV, XO, N2F, HAT, HA, GP, GA,
        DK, DV, DQ, GMX,
        GQ, GI, GD, XQ, XI, XD, HQ, HI, HD, ZQ, ZI, ZD, TQ, TI, TD,
        GO, GOF, XGO, TGO,
        VG, VR, SL, SLR, SLF, RS_, BG, BO, BI,
        ssem, rsem, lsem,
    ) = refs
    s = lax.axis_index("seq")
    b = lax.axis_index("band")
    x, c = lax.div(s, 2), lax.rem(s, 2)
    zh, l = lax.div(b, 4), lax.rem(b, 4)
    zl, y = lax.div(l, 2), lax.rem(l, 2)
    t, j = x * 2 + zh, c * 4 + l

    def flip(v, d):
        return 1 - v if d else v

    def flip_l(d):
        return flip(zl, d // 2) * 2 + flip(y, d % 2)

    def dev(dx=0, dc=0, dzh=0, dl=0):
        return (flip(x, dx) * 2 + flip(c, dc), flip(zh, dzh) * 4 + flip_l(dl))

    roles = (l, flip_l(2), flip_l(1), flip_l(3))

    counter = [0]
    pending = []

    def slots(n=1):
        first = counter[0]
        counter[0] += n
        assert counter[0] <= copies
        return first

    def send(src, dst, device, sem):
        copy = pltpu.make_async_remote_copy(
            src_ref=src, dst_ref=dst, send_sem=ssem.at[sem], recv_sem=rsem.at[sem],
            device_id=device, device_id_type=MESH_ID)
        copy.start()
        return copy

    def push(src, dst, device, sem):
        copy = send(src, dst, device, sem)
        pending.append(copy)
        return copy

    def arrive(dst, sem):
        pltpu.make_async_remote_copy(
            src_ref=dst, dst_ref=dst, send_sem=ssem.at[sem], recv_sem=rsem.at[sem],
            device_id=dev(dc=1), device_id_type=MESH_ID).wait_recv()

    def left(src, sem):
        pltpu.make_async_remote_copy(
            src_ref=src, dst_ref=src, send_sem=ssem.at[sem], recv_sem=rsem.at[sem],
            device_id=dev(dc=1), device_id_type=MESH_ID).wait_send()

    def move(src, dst, sem):
        return pltpu.make_async_copy(src, dst, lsem.at[sem])

    group_masks = [(dc, dl) for dl in (3, 1, 2, 0) for dc in (0, 1) if (dc, dl) != (0, 0)]
    line_masks = [(dx, dc, dzh) for dx in (1, 0) for dc in (0, 1) for dzh in (1, 0) if dx + dc + dzh]

    def group(dc, dl):
        return flip(c, dc) * 4 + flip_l(dl)

    native = c == zh
    foreign = jnp.logical_not(native)
    partner = dev(dc=1, dzh=1)
    their_block = (1 - c) * 4 + l

    barrier = pltpu.get_barrier_semaphore()
    peers = [dict(dc=dc, dl=dl) for dc, dl in group_masks]
    peers += [dict(dx=a, dc=e, dzh=f) for a, e, f in line_masks if (a, e, f) != (0, 1, 0)]
    for peer in peers:
        pl.semaphore_signal(barrier, inc=1, device_id=dev(**peer), device_id_type=MESH_ID)
    get_q, get_i, get_d = move(wq, WQI, 0), move(wi, WII, 1), move(wd, WD.at[t], 2)
    get_x, get_c = move(xin.at[0], X.at[j], 3), move(cin.at[0], GM.at[j], 4)
    get_q.start()
    get_i.start()
    get_d.start()

    @pl.when(native)
    def _():
        get_x.start()
        get_c.start()

    lane_group = lax.broadcasted_iota(jnp.int32, (1, LANES), 1) // 32
    PK[...] = jnp.zeros_like(PK)
    for p, ref in enumerate((p0, p1, p2, p3, p4, p5, p6, p7)):
        value = ref[...].astype(F32).reshape(1, 32)
        PK[p : p + 1] = jnp.where(lane_group == l, jnp.concatenate([value] * 4, axis=1), 0.0)
    own_bias = pb[...].astype(F32).reshape(1, LANES)
    for r in range(4):
        PK[8 + r : 9 + r] = jnp.where(l == r, own_bias, jnp.zeros_like(own_bias))
    SGI[...] = jnp.zeros_like(SGI)
    SGI[0:1] = seg_in[...].astype(F32)
    SGI[1:2, 0:SUBGRIDS] = len_in[...].astype(F32)
    get_q.wait()
    for jj in range(8):
        for ch in range(3):
            WSQ[jj, ch] = WQI[:, ch * D + jj * LANES : ch * D + (jj + 1) * LANES]
    for ch in range(3):
        RQ[ch, t, j] = WSQ[j, ch]
    pl.semaphore_wait(barrier, len(peers))

    sem_px, sem_pc, sem_ps = slots(), slots(), slots()
    sem_wq, sem_s1 = slots(8), slots(4)
    for dl in (1, 2, 3):
        push(PK, SP.at[dl], dev(dl=dl), sem_s1 + dl)

    @pl.when(native)
    def _():
        SG[j] = SGI[...]

    @pl.when(foreign)
    def _():
        send(SGI, SG.at[their_block], partner, sem_ps)
        send(xin.at[0], X.at[their_block], partner, sem_px)

    for dc, dl in group_masks:
        push(WSQ.at[group(dc, dl)], RQ.at[:, t, j], dev(dc=dc, dl=dl), sem_wq + dc * 4 + dl)

    class Gather:
        def __init__(self, buf):
            self.buf, self.far, self.near = buf, slots(4), slots(4)

        def start(self):
            block = self.buf.at[j]
            copies_out = [
                send(block, block, (s, zh * 4 + roles[1]), self.far + 1),
                send(block, block, (s, zh * 4 + roles[2]), self.far + 2),
                send(block, block, dev(dc=1), self.near),
            ]
            return copies_out

        def begin(self):
            pending.extend(self.start())

        def forward(self, k):
            block = self.buf.at[c * 4 + roles[k]]
            arrive(block, self.far + k)
            if k == 1:
                push(block, block, (s, zh * 4 + roles[2]), self.far + 3)
            push(block, block, dev(dc=1), self.near + k)

        def sibling(self, k):
            arrive(self.buf.at[(1 - c) * 4 + roles[k]], self.near + k)

    gather_x = Gather(X)
    gather_g = Gather(GM)

    @pl.when(native)
    def _():
        get_x.wait()
        gather_x.start()

    sem_wo, sem_wt = slots(4), slots(4)
    pair_l = c * 2 + zh
    to_self = jnp.logical_and(x == c, l == pair_l)
    is_root = jnp.logical_and(x == c, zh == y)
    root_mask = jnp.abs(x - c) * 2 + jnp.abs(zh - y)
    get_o = move(wo, WO.at[l], 5)

    @pl.when(to_self)
    def _():
        get_o.start()

    @pl.when(jnp.logical_not(to_self))
    def _():
        send(wo, WO.at[l], (x * 2 + x, zh * 4 + pair_l), sem_wo + l)

    q_own = x * 4 + c * 2 + zh
    slab = PK[...]
    for dl in (1, 2, 3):
        arrive(SP.at[dl], sem_s1 + dl)
        slab += SP[dl]
    FULL[q_own] = slab
    sem_s2 = slots(8)
    for dx, dc, dzh in line_masks:
        push(FULL.at[q_own], FULL.at[q_own], dev(dx=dx, dc=dc, dzh=dzh), sem_s2 + dx * 4 + dc * 2 + dzh)

    class Spread:
        def __init__(self, buf):
            self.buf, self.sem = buf, slots(3)

        def start(self):
            block = self.buf.at[t]
            push(block, block, dev(dzh=1), self.sem)
            push(block, block, dev(dx=1), self.sem + 1)

        def forward(self):
            block = self.buf.at[x * 2 + 1 - zh]
            arrive(block, self.sem)
            push(block, block, dev(dx=1), self.sem + 2)

        def finish(self):
            arrive(self.buf.at[(1 - x) * 2 + zh], self.sem + 1)
            arrive(self.buf.at[(1 - x) * 2 + 1 - zh], self.sem + 2)

    spread_q = [Spread(RQ.at[ch]) for ch in range(3)]
    for dc, dl in group_masks:
        arrive(RQ.at[:, t, group(dc, dl)], sem_wq + dc * 4 + dl)
    for ch in range(3):
        spread_q[ch].start()

    sem_sg = slots(8)

    @pl.when(foreign)
    def _():
        arrive(SG.at[j], sem_ps)

    for dc, dl in group_masks:
        push(SG.at[j], SG.at[j], dev(dc=dc, dl=dl), sem_sg + dc * 4 + dl)
    @pl.when(foreign)
    def _():
        arrive(X.at[j], sem_px)
        gather_x.start()

    for slot in range(4):
        @pl.when(jnp.logical_and(is_root, jnp.logical_not(jnp.logical_and(zl == c, l == slot))))
        def _():
            arrive(WO.at[slot], sem_wo + slot)

    @pl.when(to_self)
    def _():
        get_o.wait()

    @pl.when(is_root)
    def _():
        send(WO, WO, dev(dzh=1), sem_wt + 1)
        send(WO, WO, dev(dx=1), sem_wt + 2)


    for dx, dc, dzh in line_masks:
        arrive(FULL.at[flip(x, dx) * 4 + flip(c, dc) * 2 + flip(zh, dzh)], sem_s2 + dx * 4 + dc * 2 + dzh)
    for q in range(8):
        PV[:, q * LANES : (q + 1) * LANES] = FULL[q]
    gain1, shift1 = PV[0:1, :], PV[1:2, :]

    def norm_rows(value, gain, shift):
        average = jnp.mean(value, axis=-1, keepdims=True)
        centered = value - average
        root = lax.rsqrt(jnp.mean(centered * centered, axis=-1, keepdims=True) + EPSILON)
        normal = centered * root
        return normal, root, normal * gain + shift

    def norm_one(block):
        for r in range(2):
            rows = pl.ds(r * 64, 64)
            normal, _, value = norm_rows(X[block, rows].astype(F32), gain1, shift1)
            N0[block, rows] = normal.astype(BF16)
            N1[block, rows] = value.astype(BF16)

    norm_one(j)

    gather_x.sibling(0)
    norm_one((1 - c) * 4 + l)
    gather_x.forward(1)
    gather_x.forward(2)
    norm_one(c * 4 + roles[1])
    norm_one(c * 4 + roles[2])
    spread_q[0].forward()
    for k in (1, 2):
        gather_x.sibling(k)
    gather_x.forward(3)
    norm_one((1 - c) * 4 + roles[1])
    spread_q[1].forward()
    norm_one((1 - c) * 4 + roles[2])
    norm_one(c * 4 + roles[3])
    spread_q[2].forward()
    gather_x.sibling(3)
    norm_one((1 - c) * 4 + roles[3])

    @pl.when(foreign)
    def _():
        send(cin.at[0], GM.at[their_block], partner, sem_pc)

    get_i.wait()
    for jj in range(8):
        for ch in range(4):
            flat = flat_column(jj, ch)
            WSI[jj, ch] = WII[:, flat * LANES : (flat + 1) * LANES]
    sem_wi = slots(8)
    for dc, dl in group_masks:
        push(WSI.at[group(dc, dl)], RI.at[t, j], dev(dc=dc, dl=dl), sem_wi + dc * 4 + dl)
    RI[t, j] = WSI[j]
    get_d.wait()
    spread_i, spread_d = Spread(RI), Spread(WD)

    for dc, dl in group_masks:
        arrive(SG.at[group(dc, dl)], sem_sg + dc * 4 + dl)
    lens = SG[j, 1:2, :]
    row_ids = lax.broadcasted_iota(jnp.int32, (LANES, LANES), 0)
    lane_ids = lax.broadcasted_iota(jnp.int32, (LANES, LANES), 1)
    label_row = lane_ids.astype(F32)
    label_col = row_ids.astype(F32)
    earlier = (lane_ids < row_ids).astype(BF16)
    running = jnp.zeros((1, LANES), F32)
    for blk in range(8):
        onehot = (label_col == SG[blk, 0:1, :]).astype(F32).T
        before = dot(earlier, onehot.astype(BF16)) + running
        running = running + jnp.sum(onehot, axis=0, keepdims=True)
        rank = jnp.sum(before * onehot, axis=1, keepdims=True)
        limit = jnp.sum(onehot * lens, axis=1, keepdims=True)
        ident = jnp.sum(label_row * onehot, axis=1, keepdims=True)
        CODE[blk] = jnp.broadcast_to(jnp.where(rank < limit, ident, -1.0), (ROWS, LANES))

    @pl.when(jnp.logical_not(is_root))
    def _():
        arrive(WO, sem_wt + root_mask)

    @pl.when(root_mask == 1)
    def _():
        send(WO, WO, dev(dx=1), sem_wt + 3)

    for ch in range(3):
        spread_q[ch].finish()
        for i in range(32):
            tt, jj = shard_place(i)
            WQ[i * 32 : (i + 1) * 32, ch * LANES : (ch + 1) * LANES] = RQ[ch, tt, jj]
    bias_q, bias_v = FULL[j][2:3, :], FULL[j][3:4, :]
    for k in range(4):
        rows = pl.ds(k * 256, 256)
        normed = N1[2 * k : 2 * k + 2].reshape(256, D)
        mixed = dot(normed, WQ[...])
        queries = (mixed[:, :LANES] + bias_q).astype(BF16).astype(F32) * (HEAD_DIM ** -0.5)
        keys = mixed[:, LANES : 2 * LANES]
        values = mixed[:, 2 * LANES :] + bias_v
        QS[rows] = queries.astype(BF16)
        KK[rows] = keys.astype(BF16)
        VV[rows] = values.astype(BF16)
        QT[:, rows] = queries.T.astype(BF16)
        KT[:, rows] = keys.T.astype(BF16)
        VT[:, rows] = values.T.astype(BF16)

    for dc, dl in group_masks:
        arrive(RI.at[t, group(dc, dl)], sem_wi + dc * 4 + dl)
    spread_i.start()
    spread_d.start()

    @pl.when(native)
    def _():
        get_c.wait()

    @pl.when(foreign)
    def _():
        arrive(GM.at[j], sem_pc)

    is_real = CODE[j][:, 0:1] >= 0.0
    GM[j] = jnp.where(is_real, GM[j].astype(F32), 0.0).astype(BF16)
    gather_g.begin()

    def pair_lanes(lp):
        return (pl.ds(pl.multiple_of(lp * LANES, LANES), LANES), pl.ds(pl.multiple_of(512 + lp * LANES, LANES), LANES))

    def cat_lanes(ref, lp):
        first, second = pair_lanes(lp)
        return jnp.concatenate([ref[:, first], ref[:, second]], axis=1)

    def cat_rows(ref, lp):
        return jnp.concatenate([ref[lp], ref[4 + lp]], axis=0)

    class Scatter:
        def __init__(self, part, chip, number, before=None, tree=True):
            self.part, self.chip, self.number, self.before, self.tree = part, chip, number, before, tree
            self.near, self.far = slots(4), slots(4)

        def emit(self, m, value):
            if self.before is not None:
                left(self.part.at[m, 1 - c], self.before.near + m)
            low = value.astype(BF16)
            self.part[m, 0] = low[:ROWS]
            self.part[m, 1] = low[ROWS:]
            send(self.part.at[m, 1 - c], SB.at[self.number, m], dev(dc=1), self.near + m)

        def reduce(self, m):
            arrive(SB.at[self.number, m], self.near + m)
            if m == 0:
                return
            if self.before is not None:
                left(self.chip.at[m], self.before.far + m)
            total = self.part[m, c].astype(F32) + SB[self.number, m].astype(F32)
            if self.tree and m == 2:
                arrive(RV.at[self.number, 3], self.far + 3)
                total += RV[self.number, 3].astype(F32)
            self.chip[m] = total.astype(BF16)
            device = dev(dl=1) if self.tree and m == 3 else dev(dl=m)
            send(self.chip.at[m], RV.at[self.number, m], device, self.far + m)

        def finish(self):
            for m in (1, 2) if self.tree else (1, 2, 3):
                arrive(RV.at[self.number, m], self.far + m)

        def rows(self, rows):
            total = self.part[0, c, rows].astype(F32) + SB[self.number, 0, rows].astype(F32)
            for m in (1, 2) if self.tree else (1, 2, 3):
                total += RV[self.number, m, rows].astype(F32)
            return total

        def close(self):
            for m in range(4):
                left(self.part.at[m, 1 - c], self.near + m)
                if m:
                    left(self.chip.at[m], self.far + m)

    head_rows = lax.broadcasted_iota(jnp.int32, (LANES, 256), 0)
    head_lanes = lax.broadcasted_iota(jnp.int32, (256, LANES), 1)

    def only_rows(value, h):
        return jnp.where((head_rows >= h * 64) & (head_rows < (h + 1) * 64), value, jnp.zeros_like(value))

    def only_lanes(value, h):
        return jnp.where((head_lanes >= h * 64) & (head_lanes < (h + 1) * 64), value, jnp.zeros_like(value))

    scatter_a = Scatter(PA, CS, 0)
    attend_order = (3, 1, 2, 0)
    for k, m in enumerate(attend_order):
        lp = flip_l(m)
        queries_t = cat_lanes(QT, lp)
        seg_q = jnp.concatenate([SG[lp, 0:1, :], SG[4 + lp, 0:1, :]], axis=1)
        for h in range(2):
            masked_t = only_rows(queries_t.astype(F32), h).astype(BF16)
            top = jnp.full((8, 256), NEGATIVE, F32)
            for i in range(8):
                rows = pl.ds(i * ROWS, ROWS)
                value = dot(KK[rows], masked_t)
                code = CODE[i]
                allowed = jnp.concatenate([code, code], axis=1) == seg_q
                value = jnp.where(allowed, value, NEGATIVE)
                SC[h, rows] = value
                top = jnp.maximum(top, jnp.max(value.reshape(16, 8, 256), axis=0))
            top = jnp.max(top, axis=0, keepdims=True)
            total = jnp.zeros((8, 256), F32)
            for i in range(8):
                rows = pl.ds(i * ROWS, ROWS)
                value = jnp.exp(SC[h, rows] - top)
                PT[m, h, rows] = value.astype(BF16)
                total = total + jnp.sum(value.reshape(16, 8, 256), axis=0)
            inverse = 1.0 / jnp.sum(total, axis=0, keepdims=True)
            INV[m, h] = jnp.broadcast_to(inverse, (8, 256))
            OT[m, h * 64 : (h + 1) * 64] = dot(VT[h * 64 : (h + 1) * 64, :], PT[m, h]) * inverse
            if k and h == 0:
                scatter_a.reduce(attend_order[k - 1])
        joined = OT[m]
        OL[m] = joined.astype(BF16)
        scatter_a.emit(m, dot(joined.T.astype(BF16), WO[...].reshape(LANES, D)))
    spread_i.forward()
    scatter_a.reduce(0)
    scatter_a.finish()

    gain2, shift2, bias_o = PV[5:6, :], PV[6:7, :], PV[4:5, :]
    for r in range(4):
        rows = pl.ds(r * 32, 32)
        residual = X[j, rows].astype(F32) + scatter_a.rows(rows) + bias_o
        XO[rows] = residual
        normal, root, value = norm_rows(residual, gain2, shift2)
        N2F[rows] = normal
        RS_[rows] = jnp.broadcast_to(root, (32, LANES))
        N2[j, rows] = value.astype(BF16)
    gather_n = Gather(N2)
    gather_n.begin()

    for k in (1, 2):
        gather_g.forward(k)
    spread_d.forward()
    spread_i.finish()
    for i in range(32):
        tt, jj = shard_place(i)
        for ch in range(4):
            WI[i * 32 : (i + 1) * 32, ch * LANES : (ch + 1) * LANES] = RI[tt, jj, ch]
    pick = lax.broadcasted_iota(jnp.int32, (16, LANES), 0) == 8 + l
    bias_in = jnp.concatenate(
        [
            jnp.sum(jnp.where(pick, FULL[(ch // 2) * 4 + c * 2 + ch % 2], 0.0), axis=0, keepdims=True)
            for ch in range(4)
        ],
        axis=1,
    )
    scatter_m = Scatter(PA, CS, 1, scatter_a, tree=False)
    scatter_b = Scatter(PB, CSB, 2)
    BG[0:1] = jnp.zeros((1, 512), F32)

    def hidden_part(m):
        lp = flip_l(m)
        first, second = pair_lanes(lp)
        hidden = dot(cat_rows(N2, lp), WI[...]) + bias_in
        phi_cap = 0.5 * (1.0 + lax.erf(hidden * 0.7071067811865476))
        phi = jnp.exp(-0.5 * hidden * hidden) * 0.3989422804014327
        act = hidden * phi_cap
        GA[m] = phi_cap + hidden * phi
        HA[m] = act.astype(BF16)
        act_t = act.T.astype(BF16)
        HAT[:, first] = act_t[:, :ROWS]
        HAT[:, second] = act_t[:, ROWS:]

    def hidden_back(m):
        lp = flip_l(m)
        grad_act = dot_nt(cat_rows(GM, lp), WD[...].reshape(512, D))
        grad_pre = (grad_act * GA[m]).astype(BF16)
        GP[lp] = grad_pre[:ROWS]
        GP[4 + lp] = grad_pre[ROWS:]
        BG[0:1] += jnp.sum(grad_pre.astype(F32), axis=0, keepdims=True)
        scatter_m.emit(m, dot_nt(grad_pre, WI[...]))

    gather_n.sibling(0)
    hidden_part(0)
    gather_n.forward(2)
    gather_n.forward(1)
    gather_g.forward(3)
    gather_g.sibling(0)
    spread_d.finish()
    hidden_back(0)
    gather_n.sibling(2)
    hidden_part(1)
    gather_g.sibling(2)
    hidden_back(1)
    scatter_m.reduce(0)
    gather_n.sibling(1)
    hidden_part(2)
    gather_g.sibling(1)
    hidden_back(2)
    gather_n.forward(3)
    scatter_m.reduce(1)
    gather_n.sibling(3)
    hidden_part(3)
    gather_g.sibling(3)
    scatter_m.reduce(2)
    hidden_back(3)
    scatter_m.reduce(3)

    class Total:
        def __init__(self, part, from_x, middle, from_z):
            self.part, self.from_x, self.middle, self.from_z = part, from_x, middle, from_z
            self.sem = slots(2)

        def start(self):
            half = pl.ds((1 - x) * 2, 2)
            push(self.part.at[half], self.from_x, dev(dx=1), self.sem)

        def second(self):
            arrive(self.from_x, self.sem)
            self.middle[...] = (
                self.part[x * 2 + 1 - zh].astype(F32) + self.from_x[1 - zh].astype(F32)
            ).astype(BF16)
            push(self.middle, self.from_z, dev(dzh=1), self.sem + 1)

        def result(self):
            arrive(self.from_z, self.sem + 1)
            return self.part[t].astype(F32) + self.from_x[zh].astype(F32) + self.from_z[...].astype(F32)

    total_d = Total(GD, XD, HD, ZD)
    total_i = Total(GI, XI, HI, ZI)
    total_q = [Total(GQ.at[ch], XQ.at[ch], HQ.at[ch], ZQ.at[ch]) for ch in range(3)]
    for ch in range(4):
        GD[ch] = dot(HAT[ch * LANES : (ch + 1) * LANES, :], GM[...].reshape(8 * ROWS, D)).astype(BF16)
    total_d.start()
    all_pre = GP[...].reshape(8 * ROWS, 512)
    for blk in range(8):
        product = dot_tn(N2[:, :, blk * LANES : (blk + 1) * LANES].reshape(8 * ROWS, LANES), all_pre).astype(BF16)
        for r in range(4):
            tt, jj = shard_place(blk * 4 + r)
            for ch in range(4):
                GI[tt, jj, ch] = product[r * 32 : (r + 1) * 32, ch * LANES : (ch + 1) * LANES]
    total_i.start()

    def norm_back(grad, normal, root, gain):
        scaled = grad * gain
        return root * (scaled - jnp.mean(scaled, axis=-1, keepdims=True)
                       - normal * jnp.mean(scaled * normal, axis=-1, keepdims=True))

    scatter_m.finish()
    sums = [jnp.zeros((1, D), F32) for _ in range(4)]
    for r in range(4):
        rows = pl.ds(r * 32, 32)
        grad = scatter_m.rows(rows)
        normal = N2F[rows]
        top_grad = GM[j, rows].astype(F32)
        grad_residual = top_grad + norm_back(grad, normal, RS_[rows][:, 0:1], gain2)
        low = grad_residual.astype(BF16)
        GB[j, rows] = low
        N2F[rows] = grad_residual
        for i, value in enumerate((grad * normal, grad, low.astype(F32), top_grad)):
            sums[i] += jnp.sum(value, axis=0, keepdims=True)
    vectors = {5: sums[0], 6: sums[1], 4: sums[2], 7: sums[3]}
    gather_b = Gather(GB)
    gather_b.begin()

    DK[...] = jnp.zeros_like(DK)
    DV[...] = jnp.zeros_like(DV)
    GOF[...] = jnp.zeros_like(GOF)

    def attend_back(m):
        lp = flip_l(m)
        first, second = pair_lanes(lp)
        branch = cat_rows(GB, lp)
        grad_att = dot_nt(branch, WO[...].reshape(LANES, D)).astype(BF16).astype(F32)
        GOF[...] += dot(OL[m], branch)
        grad_att_t = grad_att.T
        both = grad_att_t * OT[m]
        queries = jnp.concatenate([QS[first], QS[second]], axis=0).astype(F32)
        for h in range(2):
            inverse = INV[m, h][0:1]
            delta = jnp.sum(both[h * 64 : (h + 1) * 64], axis=0, keepdims=True) * inverse
            scaled_t = only_rows(grad_att_t * inverse, h)
            scaled_low_t = scaled_t.astype(BF16)
            scaled_low = scaled_t.T.astype(BF16)
            queries_h = only_lanes(queries, h).astype(BF16)
            for i in range(8):
                rows = pl.ds(i * ROWS, ROWS)
                probs = PT[m, h, rows]
                value = dot(VV[rows], scaled_low_t)
                grad_scores = (probs.astype(F32) * (value - delta)).astype(BF16)
                DV[rows] += dot(probs, scaled_low)
                DK[rows] += dot(grad_scores, queries_h)
                PT[m, h, rows] = grad_scores
            DQ[h * 64 : (h + 1) * 64, :] = dot(KT[h * 64 : (h + 1) * 64, :], PT[m, h]) * (HEAD_DIM ** -0.5)
        dq_rows = DQ[...].T.astype(BF16)
        GMX[lp, :, 0:LANES] = dq_rows[:ROWS]
        GMX[4 + lp, :, 0:LANES] = dq_rows[ROWS:]

    def forward_out(m):
        scatter_b.emit(m, dot(HA[m], WD[...].reshape(512, D)))

    gather_b.sibling(0)
    attend_back(0)
    gather_b.forward(2)
    gather_b.forward(1)
    total_d.second()
    gather_b.sibling(2)
    attend_back(1)
    gather_b.sibling(1)
    attend_back(2)
    gather_b.forward(3)
    for m in attend_order:
        forward_out(m)
    total_i.second()
    scatter_b.reduce(3)
    gather_b.sibling(3)
    attend_back(3)
    scatter_b.reduce(1)
    scatter_b.reduce(2)
    scatter_b.reduce(0)

    for blk in range(8):
        rows = pl.ds(blk * ROWS, ROWS)
        GMX[blk, :, LANES : 2 * LANES] = DK[rows].astype(BF16)
        GMX[blk, :, 2 * LANES :] = DV[rows].astype(BF16)
    all_mixed = GMX[...].reshape(8 * ROWS, 3 * LANES)
    scatter_n = Scatter(PA, CS, 3, scatter_m)
    scatter_n.emit(3, dot_nt(cat_rows(GMX, flip_l(3)), WQ[...]))
    for blk in range(8):
        product = dot_tn(N1[:, :, blk * LANES : (blk + 1) * LANES].reshape(8 * ROWS, LANES), all_mixed).astype(BF16)
        for r in range(4):
            tt, jj = shard_place(blk * 4 + r)
            for ch in range(3):
                GQ[ch, tt, jj] = product[r * 32 : (r + 1) * 32, ch * LANES : (ch + 1) * LANES]
    scatter_n.reduce(3)
    for ch in range(3):
        total_q[ch].start()

    for k, m in enumerate(attend_order):
        if k:
            scatter_n.emit(m, dot_nt(cat_rows(GMX, flip_l(m)), WQ[...]))
        if k > 1:
            scatter_n.reduce(attend_order[k - 1])
    scatter_n.reduce(0)

    sums = [jnp.zeros((1, D), F32) for _ in range(2)]
    for m in range(4):
        lp = flip_l(m)
        for half in range(2):
            value = PA[m, half].astype(F32)
            sums[0] += jnp.sum(value * N0[half * 4 + lp].astype(F32), axis=0, keepdims=True)
            sums[1] += jnp.sum(value, axis=0, keepdims=True)
    vectors[0], vectors[1] = sums

    mixed_sums = jnp.sum(all_mixed.astype(F32), axis=0, keepdims=True)
    for q in range(8):
        VG[q] = jnp.zeros((16, LANES), F32)
        for p in (0, 1, 4, 5, 6, 7):
            VG[q, p : p + 1] = vectors[p][:, q * LANES : (q + 1) * LANES]
        for p, ch in ((2, 0), (3, 2)):
            VG[q, p : p + 1] = jnp.where(j == q, mixed_sums[:, ch * LANES : (ch + 1) * LANES], 0.0)
        ch = (q // 4) * 2 + q % 2
        for r in range(4):
            here = jnp.logical_and(c == (q // 2) % 2, l == r)
            VG[q, 8 + r : 9 + r] = jnp.where(here, BG[0:1, ch * LANES : (ch + 1) * LANES], 0.0)
    sem_v1, sem_v2 = slots(8), slots(4)
    for dx, dc, dzh in line_masks:
        mask = dx * 4 + dc * 2 + dzh
        push(VG.at[flip(x, dx) * 4 + flip(c, dc) * 2 + flip(zh, dzh)], VR.at[mask], dev(dx=dx, dc=dc, dzh=dzh), sem_v1 + mask)

    GO[...] = GOF[...].astype(BF16)
    sem_go, sem_gs = slots(4), slots(4)

    @pl.when(jnp.logical_not(is_root))
    def _():
        send(GO, XGO.at[root_mask], (c * 2 + c, y * 4 + l), sem_go + root_mask)

    bias_d = PV[7:8, :]
    sem_out, sem_in = slots(), slots()
    scatter_b.finish()
    for r in range(4):
        rows = pl.ds(r * 32, 32)
        BO[rows] = (XO[rows] + scatter_b.rows(rows) + bias_d).astype(BF16)
    put_block = move(BO, out_block.at[0], 6)

    @pl.when(native)
    def _():
        put_block.start()

    @pl.when(foreign)
    def _():
        send(BO, out_block.at[0], partner, sem_out)

    slab = VG[q_own]
    for dx, dc, dzh in line_masks:
        mask = dx * 4 + dc * 2 + dzh
        arrive(VR.at[mask], sem_v1 + mask)
        slab += VR[mask]
    SL[...] = slab
    for dl in (1, 2, 3):
        push(SL, SLR.at[dl], dev(dl=dl), sem_v2 + dl)

    TD[...] = total_d.result().astype(BF16)
    put_d = move(TD, out_d, 7)
    put_d.start()
    TI[...] = total_i.result().astype(BF16)
    sem_ti, sem_tq = slots(8), slots(8 * 3)
    for dc, dl in group_masks:
        push(TI.at[group(dc, dl)], out_i.at[j], dev(dc=dc, dl=dl), sem_ti + dc * 4 + dl)
    put_i = move(TI.at[j], out_i.at[j], 8)
    put_i.start()

    total_q[0].second()
    total_q[1].second()

    scatter_n.finish()
    for r in range(4):
        rows = pl.ds(r * 32, 32)
        grad = scatter_n.rows(rows)
        normal, root, _ = norm_rows(X[j, rows].astype(F32), gain1, shift1)
        BI[rows] = (N2F[rows] + norm_back(grad, normal, root, gain1)).astype(BF16)
    put_input = move(BI, out_input.at[0], 9)

    @pl.when(native)
    def _():
        put_input.start()

    @pl.when(foreign)
    def _():
        send(BI, out_input.at[0], partner, sem_in)

    total_q[2].second()

    put_o = move(TGO.at[l], out_o, 10)

    @pl.when(is_root)
    def _():
        total = GOF[...]
        for mask in (1, 2, 3):
            arrive(XGO.at[mask], sem_go + mask)
            total += XGO[mask].astype(F32)
        TGO[...] = total.astype(BF16).reshape(4, 32, D)
        for slot in range(4):
            mine = jnp.logical_and(zl == c, l == slot)

            @pl.when(mine)
            def _():
                put_o.start()

            @pl.when(jnp.logical_not(mine))
            def _():
                send(TGO.at[slot], out_o, (x * 2 + zl, zh * 4 + slot), sem_gs + slot)

    for ch in range(3):
        TQ[ch] = total_q[ch].result().astype(BF16)
        for dc, dl in group_masks:
            push(TQ.at[ch, group(dc, dl)], out_q.at[ch, j], dev(dc=dc, dl=dl), sem_tq + ch * 8 + dc * 4 + dl)
    put_q = [move(TQ.at[ch, j], out_q.at[ch, j], 11 + ch) for ch in range(3)]
    for ch in range(3):
        put_q[ch].start()

    for dl in (1, 2, 3):
        arrive(SLR.at[dl], sem_v2 + dl)
        slab += SLR[dl]
    SLF[...] = slab
    put_small = move(SLF, out_small, 14)
    put_small.start()

    for dc, dl in group_masks:
        arrive(out_i.at[group(dc, dl)], sem_ti + dc * 4 + dl)
        for ch in range(3):
            arrive(out_q.at[ch, group(dc, dl)], sem_tq + ch * 8 + dc * 4 + dl)

    put_d.wait()
    put_i.wait()
    put_small.wait()
    for ch in range(3):
        put_q[ch].wait()

    @pl.when(native)
    def _():
        put_block.wait()
        put_input.wait()

    @pl.when(foreign)
    def _():
        left(SGI, sem_ps)
        left(xin.at[0], sem_px)
        left(cin.at[0], sem_pc)
        left(BO, sem_out)
        left(BI, sem_in)
        arrive(out_block.at[0], sem_out)
        arrive(out_input.at[0], sem_in)

    @pl.when(to_self)
    def _():
        put_o.wait()

    @pl.when(jnp.logical_not(to_self))
    def _():
        left(wo, sem_wo + l)
        arrive(out_o, sem_gs + l)

    @pl.when(jnp.logical_not(is_root))
    def _():
        left(GO, sem_go + root_mask)

    @pl.when(root_mask == 1)
    def _():
        left(WO, sem_wt + 3)

    @pl.when(is_root)
    def _():
        for mask in (1, 2):
            left(WO, sem_wt + mask)
        for slot in range(4):
            @pl.when(jnp.logical_not(jnp.logical_and(zl == c, l == slot)))
            def _():
                left(TGO.at[slot], sem_gs + slot)

    scatter_n.close()
    scatter_b.close()
    for k in (1, 2):
        left(X.at[j], gather_x.far + k)
    left(X.at[j], gather_x.near)
    for copy in pending:
        copy.wait_send()


def fused_scratch():
    def v(*shape):
        return pltpu.VMEM(shape, BF16)

    def f(*shape):
        return pltpu.VMEM(shape, F32)

    blocks = (8, ROWS, D)
    return [
        v(*blocks), v(*blocks), v(*blocks), v(*blocks), v(*blocks), v(*blocks),
        f(8, LANES), f(8, 8, LANES), f(16, LANES), f(4, 16, LANES), f(8, 16, LANES), f(16, D),
        v(32, 3 * D), v(8, 3, 32, LANES), v(3, 4, 8, 32, LANES), v(D, 3 * LANES), v(4, 32, D),
        v(32, 4 * D), v(8, 4, 32, LANES), v(4, 8, 4, 32, LANES), v(D, 512), v(4, LANES, D),
        v(D, LANES), v(D, LANES), v(D, LANES), v(LANES, D), v(LANES, D), v(LANES, D),
        f(8, ROWS, LANES), f(2, D, 256), v(4, 2, D, 256), f(4, 2, 8, 256),
        f(4, LANES, 256), v(4, LANES, 256),
        v(4, 2, ROWS, D), v(4, ROWS, D), v(4, 2, ROWS, D), v(4, ROWS, D),
        v(4, 4, ROWS, D), v(4, 4, ROWS, D), f(ROWS, D), f(ROWS, D),
        v(512, D), v(4, 256, 512), v(8, ROWS, 512), f(4, 256, 512),
        f(D, LANES), f(D, LANES), f(LANES, 256), v(8, ROWS, 3 * LANES),
        v(3, 4, 8, 32, LANES), v(4, 8, 4, 32, LANES), v(4, LANES, D),
        v(3, 2, 8, 32, LANES), v(2, 8, 4, 32, LANES), v(2, LANES, D),
        v(3, 8, 32, LANES), v(8, 4, 32, LANES), v(LANES, D),
        v(3, 8, 32, LANES), v(8, 4, 32, LANES), v(LANES, D),
        v(3, 8, 32, LANES), v(8, 4, 32, LANES), v(LANES, D),
        v(LANES, D), f(LANES, D), v(4, LANES, D), v(4, 32, D),
        f(8, 16, LANES), f(8, 16, LANES), f(16, LANES), f(4, 16, LANES), f(16, LANES),
        f(ROWS, LANES), f(8, 512), v(ROWS, D), v(ROWS, D),
        pltpu.SemaphoreType.DMA((COPIES,)),
        pltpu.SemaphoreType.DMA((COPIES,)),
        pltpu.SemaphoreType.DMA((16,)),
    ]


def finish_kernel(
    block, grad_in, grad_q, grad_o, grad_i, grad_d, small,
    out_block, out_input, o0, o1, out_q, o2, o3, out_o, o4, o5, o6, out_i, ob, out_d, o7,
):
    place = lax.rem(lax.axis_index("band"), 4)
    out_block[...] = block[...]
    out_input[...] = grad_in[...]
    for jj in range(8):
        for ch in range(3):
            out_q[:, ch * D + jj * LANES : ch * D + (jj + 1) * LANES] = grad_q[ch, jj].astype(F32)
        for ch in range(4):
            flat = flat_column(jj, ch)
            out_i[:, flat * LANES : (flat + 1) * LANES] = grad_i[jj, ch].astype(F32)
    out_o[...] = grad_o[...].astype(F32)
    out_d[...] = grad_d[...].astype(F32)
    slab = small[...]
    mine = jnp.zeros((16, 32), F32)
    for k in range(4):
        mine = jnp.where(place == k, slab[:, k * 32 : (k + 1) * 32], mine)
    for p, ref in enumerate((o0, o1, o2, o3, o4, o5, o6, o7)):
        ref[...] = mine[p : p + 1].reshape(32)
    pick = lax.broadcasted_iota(jnp.int32, (16, LANES), 0) == 8 + place
    ob[...] = jnp.sum(jnp.where(pick, slab, 0.0), axis=0, keepdims=True).reshape(LANES)


def fused_shards(
    block_in,
    attention_norm_gain,
    attention_norm_bias,
    query_key_value,
    query_bias,
    value_bias,
    output_weight,
    output_bias,
    mlp_norm_gain,
    mlp_norm_bias,
    mlp_in_weight,
    mlp_in_bias,
    mlp_out_weight,
    mlp_out_bias,
    cotangent,
    segment_ids,
    sub_lengths,
):
    vmem = pl.BlockSpec(memory_space=pltpu.VMEM)
    hbm = pl.BlockSpec(memory_space=pl.ANY)

    def shape(dims, kind):
        return jax.ShapeDtypeStruct(dims, kind)

    parts = pl.pallas_call(
        functools.partial(fused_kernel, COPIES),
        out_shape=(
            shape((1, ROWS, D), BF16),
            shape((1, ROWS, D), BF16),
            shape((3, 8, 32, LANES), BF16),
            shape((32, D), BF16),
            shape((8, 4, 32, LANES), BF16),
            shape((LANES, D), BF16),
            shape((16, LANES), F32),
        ),
        in_specs=[hbm, hbm, vmem, vmem, hbm, hbm, hbm, hbm] + [vmem] * 9,
        out_specs=(hbm,) * 7,
        scratch_shapes=fused_scratch(),
        compiler_params=pltpu.CompilerParams(
            collective_id=0, has_side_effects=True, vmem_limit_bytes=63 * 2**20
        ),
    )(
        block_in, cotangent, segment_ids, sub_lengths,
        query_key_value, output_weight, mlp_in_weight, mlp_out_weight,
        attention_norm_gain, attention_norm_bias, query_bias, value_bias,
        output_bias, mlp_norm_gain, mlp_norm_bias, mlp_out_bias, mlp_in_bias,
    )
    vector = shape((32,), F32)
    return pl.pallas_call(
        finish_kernel,
        out_shape=(
            shape((1, ROWS, D), BF16), shape((1, ROWS, D), BF16), vector, vector,
            shape((32, 3 * D), F32), vector, vector, shape((32, D), F32), vector, vector, vector,
            shape((32, 4 * D), F32), shape((LANES,), F32), shape((LANES, D), F32), vector,
        ),
        in_specs=[vmem] * 7,
        out_specs=(vmem,) * 15,
    )(*parts)


def solution(mesh):
    small_slice = dict(mesh.shape) == {"seq": 4, "band": 8}
    return jax.shard_map(
        fused_shards if small_slice else shards,
        mesh=mesh,
        in_specs=(
            P("seq", "band", None),
            P(("seq", "band")),
            P(("seq", "band")),
            P(("seq", "band"), None),
            P(("seq", "band")),
            P(("seq", "band")),
            P(("seq", "band"), None),
            P(("seq", "band")),
            P(("seq", "band")),
            P(("seq", "band")),
            P(("seq", "band"), None),
            P(("seq", "band")),
            P(("seq", "band"), None),
            P(("seq", "band")),
            P("seq", "band", None),
            P("seq", "band"),
            P("seq", None),
        ),
        out_specs=(
            P("seq", "band", None),
            P("seq", "band", None),
            P(("seq", "band")),
            P(("seq", "band")),
            P(("seq", "band"), None),
            P(("seq", "band")),
            P(("seq", "band")),
            P(("seq", "band"), None),
            P(("seq", "band")),
            P(("seq", "band")),
            P(("seq", "band")),
            P(("seq", "band"), None),
            P(("seq", "band")),
            P(("seq", "band"), None),
            P(("seq", "band")),
        ),
        check_vma=False,
    )
```

```python
import functools
import math

import jax
import jax.numpy as jnp
from jax import lax
from jax.experimental import pallas as pl
from jax.experimental.pallas import tpu as pltpu
from jax.sharding import PartitionSpec as P

D = 1024
HEADS = 16
HEAD_DIM = 64
SUBGRIDS = 8


EPSILON = 1e-05
NEGATIVE = -1e30


def prefix(part, axis, combine, identity):
    place = lax.axis_index(axis)
    gathered = lax.all_gather(part, axis)
    state = jnp.zeros_like(part) + jnp.asarray(identity, part.dtype)

    def one(lap, state):
        return combine(state, lax.dynamic_index_in_dim(gathered, lap, 0, False))

    return lax.fori_loop(0, place, one, state)


def layer_norm(values_in, norm_gain, norm_shift):
    average = jnp.mean(values_in, axis=-1, keepdims=True)
    centered = values_in - average
    variance = jnp.mean(centered * centered, axis=-1, keepdims=True)
    return centered * lax.rsqrt(variance + EPSILON) * norm_gain + norm_shift


def gelu_exact(values_in):
    return jax.nn.gelu(values_in, approximate=False)


def add_counts(first_part, second_part):
    return first_part + second_part


def block_scores(query_part, key_part, seg_part, code_part, scale_factor):
    scores = (
        jnp.einsum("qhe,khe->hqk", query_part, key_part, preferred_element_type=jnp.float32)
        * scale_factor
    )
    allowed = (seg_part[:, None] == code_part[None, :])[None]
    return (jnp.where(allowed, scores, NEGATIVE), allowed)


def split_blocks(array_in, block_rows):
    return array_in.reshape((array_in.shape[0] // block_rows, block_rows) + array_in.shape[1:])


def shards(
    block_in,
    attention_norm_gain,
    attention_norm_bias,
    query_key_value,
    query_bias,
    value_bias,
    output_weight,
    output_bias,
    mlp_norm_gain,
    mlp_norm_bias,
    mlp_in_weight,
    mlp_in_bias,
    mlp_out_weight,
    mlp_out_bias,
    cotangent,
    segment_ids,
    sub_lengths,
):
    float_type = jnp.float32
    half_type = jnp.bfloat16
    rows_local = block_in.shape[1]
    seq_length = rows_local * lax.axis_size("band")
    scale_factor = HEAD_DIM ** (-0.5)
    block_rows = math.gcd(seq_length, 1024)
    seg_local = segment_ids[0]
    labels = jnp.arange(SUBGRIDS, dtype=jnp.int32)
    onehot_ids = (seg_local[:, None] == labels[None, :]).astype(jnp.int32)
    earlier_counts = prefix(
        jnp.sum(onehot_ids, axis=0), "band", add_counts, jnp.zeros((SUBGRIDS,), jnp.int32)
    )
    slots = jnp.arange(rows_local)
    earlier = (slots[None, :] < slots[:, None]).astype(float_type)
    before = (
        jnp.dot(earlier, onehot_ids.astype(float_type), precision=lax.Precision.HIGHEST).astype(
            jnp.int32
        )
        + earlier_counts[None, :]
    )
    patch_rank = jnp.sum(before * onehot_ids, axis=1)
    limits = jnp.sum(onehot_ids * sub_lengths[0][None, :], axis=1)
    realness = patch_rank < limits
    key_codes = jnp.where(realness, seg_local, -1)
    gathered = (
        lax.all_gather(attention_norm_gain, ("seq", "band"), axis=0, tiled=True),
        lax.all_gather(attention_norm_bias, ("seq", "band"), axis=0, tiled=True),
        lax.all_gather(query_key_value, ("seq", "band"), axis=0, tiled=True),
        lax.all_gather(query_bias, ("seq", "band"), axis=0, tiled=True),
        lax.all_gather(value_bias, ("seq", "band"), axis=0, tiled=True),
        lax.all_gather(output_weight, ("seq", "band"), axis=0, tiled=True),
        lax.all_gather(output_bias, ("seq", "band"), axis=0, tiled=True),
        lax.all_gather(mlp_norm_gain, ("seq", "band"), axis=0, tiled=True),
        lax.all_gather(mlp_norm_bias, ("seq", "band"), axis=0, tiled=True),
        lax.all_gather(mlp_in_weight, ("seq", "band"), axis=0, tiled=True),
        lax.all_gather(mlp_in_bias, ("seq", "band"), axis=0, tiled=True),
        lax.all_gather(mlp_out_weight, ("seq", "band"), axis=0, tiled=True),
        lax.all_gather(mlp_out_bias, ("seq", "band"), axis=0, tiled=True),
    )
    (
        gain_one,
        shift_one,
        joint_weight,
        bias_query,
        bias_value,
        proj_weight,
        proj_bias,
        gain_two,
        shift_two,
        up_weight,
        up_bias,
        down_weight,
        down_bias,
    ) = gathered
    inputs = block_in[0].astype(float_type)
    normed_float, norm_pull_one = jax.vjp(
        layer_norm, inputs, gain_one.astype(float_type), shift_one.astype(float_type)
    )
    normed_one = normed_float.astype(half_type)
    mixed_all = jnp.dot(normed_one, joint_weight, preferred_element_type=float_type)
    queries = (mixed_all[:, :D] + bias_query.astype(float_type)).astype(half_type)
    keys_local = mixed_all[:, D : 2 * D].astype(half_type)
    values_local = (mixed_all[:, 2 * D :] + bias_value.astype(float_type)).astype(half_type)
    keys_seq, values_seq, codes_seq = (
        lax.all_gather(keys_local, "band", axis=0, tiled=True),
        lax.all_gather(values_local, "band", axis=0, tiled=True),
        lax.all_gather(key_codes, "band", axis=0, tiled=True),
    )
    query_heads = queries.reshape(rows_local, HEADS, HEAD_DIM)
    key_blocks = split_blocks(keys_seq.reshape(seq_length, HEADS, HEAD_DIM), block_rows)
    value_blocks = split_blocks(values_seq.reshape(seq_length, HEADS, HEAD_DIM), block_rows)
    code_blocks = split_blocks(codes_seq, block_rows)

    def stats_step(running, block_items):
        top_now, total_now = running
        key_part, code_part = block_items
        scores, allowed = block_scores(query_heads, key_part, seg_local, code_part, scale_factor)
        top_new = jnp.maximum(top_now, jnp.max(scores, axis=-1))
        exp_terms = jnp.where(allowed, jnp.exp(scores - top_new[..., None]), 0.0)
        return (
            (top_new, total_now * jnp.exp(top_now - top_new) + jnp.sum(exp_terms, axis=-1)),
            None,
        )

    start_stats = (
        jnp.full((HEADS, rows_local), NEGATIVE, float_type),
        jnp.zeros((HEADS, rows_local), float_type),
    )
    (top_final, total_final), unused_stats = lax.scan(
        stats_step, start_stats, (key_blocks, code_blocks)
    )
    log_total = top_final + jnp.log(total_final)

    def value_step(accum_out, block_items):
        key_part, value_part, code_part = block_items
        scores, allowed = block_scores(query_heads, key_part, seg_local, code_part, scale_factor)
        soft_probs = jnp.where(allowed, jnp.exp(scores - log_total[..., None]), 0.0).astype(
            half_type
        )
        return (
            accum_out
            + jnp.einsum("hqk,khe->qhe", soft_probs, value_part, preferred_element_type=float_type),
            None,
        )

    attended, unused_values = lax.scan(
        value_step,
        jnp.zeros((rows_local, HEADS, HEAD_DIM), float_type),
        (key_blocks, value_blocks, code_blocks),
    )
    attended_low = attended.reshape(rows_local, D).astype(half_type)
    residual = (
        inputs
        + jnp.dot(attended_low, proj_weight, preferred_element_type=float_type)
        + proj_bias.astype(float_type)
    )
    normed_float_two, norm_pull_two = jax.vjp(
        layer_norm, residual, gain_two.astype(float_type), shift_two.astype(float_type)
    )
    normed_two = normed_float_two.astype(half_type)
    hidden_pre = jnp.dot(normed_two, up_weight, preferred_element_type=float_type) + up_bias.astype(
        float_type
    )
    hidden_value, gelu_pull = jax.vjp(gelu_exact, hidden_pre)
    hidden_act = hidden_value.astype(half_type)
    block_result = (
        residual
        + jnp.dot(hidden_act, down_weight, preferred_element_type=float_type)
        + down_bias.astype(float_type)
    )
    gathered_back = (
        lax.all_gather(attention_norm_gain, ("seq", "band"), axis=0, tiled=True),
        lax.all_gather(attention_norm_bias, ("seq", "band"), axis=0, tiled=True),
        lax.all_gather(query_key_value, ("seq", "band"), axis=0, tiled=True),
        lax.all_gather(query_bias, ("seq", "band"), axis=0, tiled=True),
        lax.all_gather(value_bias, ("seq", "band"), axis=0, tiled=True),
        lax.all_gather(output_weight, ("seq", "band"), axis=0, tiled=True),
        lax.all_gather(output_bias, ("seq", "band"), axis=0, tiled=True),
        lax.all_gather(mlp_norm_gain, ("seq", "band"), axis=0, tiled=True),
        lax.all_gather(mlp_norm_bias, ("seq", "band"), axis=0, tiled=True),
        lax.all_gather(mlp_in_weight, ("seq", "band"), axis=0, tiled=True),
        lax.all_gather(mlp_in_bias, ("seq", "band"), axis=0, tiled=True),
        lax.all_gather(mlp_out_weight, ("seq", "band"), axis=0, tiled=True),
        lax.all_gather(mlp_out_bias, ("seq", "band"), axis=0, tiled=True),
    )
    joint_back = gathered_back[2]
    proj_back = gathered_back[5]
    up_back = gathered_back[9]
    down_back = gathered_back[11]
    grad_out = cotangent[0].astype(float_type) * realness[:, None].astype(float_type)
    grad_mlp = grad_out.astype(half_type)
    grad_down_weight = jnp.einsum(
        "rf,rd->fd", hidden_act, grad_mlp, preferred_element_type=float_type
    )
    grad_down_bias = jnp.sum(grad_mlp.astype(float_type), axis=0)
    grad_act = jnp.einsum("rd,fd->rf", grad_mlp, down_back, preferred_element_type=float_type)
    grad_pre = gelu_pull(grad_act)[0].astype(half_type)
    grad_up_weight = jnp.einsum(
        "rd,rf->df", normed_two, grad_pre, preferred_element_type=float_type
    )
    grad_up_bias = jnp.sum(grad_pre.astype(float_type), axis=0)
    grad_normed_two = jnp.einsum("rf,df->rd", grad_pre, up_back, preferred_element_type=float_type)
    grad_resid_part, grad_gain_two, grad_shift_two = norm_pull_two(grad_normed_two)
    grad_residual = grad_out + grad_resid_part
    grad_branch = grad_residual.astype(half_type)
    grad_proj_weight = jnp.einsum(
        "rd,re->de", attended_low, grad_branch, preferred_element_type=float_type
    )
    grad_proj_bias = jnp.sum(grad_branch.astype(float_type), axis=0)
    grad_attended = jnp.einsum(
        "re,de->rd", grad_branch, proj_back, preferred_element_type=float_type
    ).astype(half_type)
    grad_heads = grad_attended.reshape(rows_local, HEADS, HEAD_DIM)
    row_delta = jnp.sum(grad_heads.astype(float_type) * attended, axis=-1).T
    keys_back = lax.all_gather(keys_local, "band", axis=0, tiled=True)
    values_back = lax.all_gather(values_local, "band", axis=0, tiled=True)
    codes_back = lax.all_gather(key_codes, "band", axis=0, tiled=True)
    key_back_blocks = split_blocks(keys_back.reshape(seq_length, HEADS, HEAD_DIM), block_rows)
    value_back_blocks = split_blocks(values_back.reshape(seq_length, HEADS, HEAD_DIM), block_rows)
    code_back_blocks = split_blocks(codes_back, block_rows)

    def key_step(query_accum, block_items):
        key_part, value_part, code_part = block_items
        scores, allowed = block_scores(query_heads, key_part, seg_local, code_part, scale_factor)
        soft_probs = jnp.where(allowed, jnp.exp(scores - log_total[..., None]), 0.0)
        grad_probs = jnp.einsum(
            "qhe,khe->hqk", grad_heads, value_part, preferred_element_type=float_type
        )
        grad_scores = (soft_probs * (grad_probs - row_delta[..., None])).astype(half_type)
        query_accum = query_accum + jnp.einsum(
            "hqk,khe->qhe", grad_scores, key_part, preferred_element_type=float_type
        )
        return (query_accum, None)

    query_total, joined_blocks = lax.scan(
        key_step,
        jnp.zeros((rows_local, HEADS, HEAD_DIM), float_type),
        (key_back_blocks, value_back_blocks, code_back_blocks),
    )
    grad_query = (query_total * scale_factor).reshape(rows_local, D)
    query_seq = lax.all_gather(queries, "band", axis=0, tiled=True)
    grad_seq = lax.all_gather(grad_attended, "band", axis=0, tiled=True)
    total_seq = lax.all_gather(log_total, "band", axis=1, tiled=True)
    delta_seq = lax.all_gather(row_delta, "band", axis=1, tiled=True)
    seg_seq = lax.all_gather(seg_local, "band", axis=0, tiled=True)
    block_count = seq_length // block_rows
    key_heads_local = keys_local.reshape(rows_local, HEADS, HEAD_DIM)
    value_heads_local = values_local.reshape(rows_local, HEADS, HEAD_DIM)

    def query_step(running, block_items):
        key_accum, value_accum = running
        query_part, grad_part, total_part, delta_part, seg_part = block_items
        scores, allowed = block_scores(
            query_part, key_heads_local, seg_part, key_codes, scale_factor
        )
        soft_probs = jnp.where(allowed, jnp.exp(scores - total_part[..., None]), 0.0)
        grad_probs = jnp.einsum(
            "qhe,khe->hqk", grad_part, value_heads_local, preferred_element_type=float_type
        )
        grad_scores = (soft_probs * (grad_probs - delta_part[..., None])).astype(half_type)
        key_accum = key_accum + jnp.einsum(
            "hqk,qhe->khe", grad_scores, query_part, preferred_element_type=float_type
        )
        value_accum = value_accum + jnp.einsum(
            "hqk,qhe->khe",
            soft_probs.astype(half_type),
            grad_part,
            preferred_element_type=float_type,
        )
        return ((key_accum, value_accum), None)

    zero_heads = jnp.zeros((rows_local, HEADS, HEAD_DIM), float_type)
    (key_total, value_total), query_blocks = lax.scan(
        query_step,
        (zero_heads, zero_heads),
        (
            split_blocks(query_seq.reshape(seq_length, HEADS, HEAD_DIM), block_rows),
            split_blocks(grad_seq.reshape(seq_length, HEADS, HEAD_DIM), block_rows),
            total_seq.reshape(HEADS, block_count, block_rows).transpose(1, 0, 2),
            delta_seq.reshape(HEADS, block_count, block_rows).transpose(1, 0, 2),
            split_blocks(seg_seq, block_rows),
        ),
    )
    grad_key = (key_total * scale_factor).reshape(rows_local, D)
    grad_value = value_total.reshape(rows_local, D)
    grad_query_low = grad_query.astype(half_type)
    grad_value_low = grad_value.astype(half_type)
    grad_mixed = jnp.concatenate(
        [grad_query_low, grad_key.astype(half_type), grad_value_low], axis=1
    )
    grad_joint_weight = jnp.einsum(
        "rd,rm->dm", normed_one, grad_mixed, preferred_element_type=float_type
    )
    grad_bias_query = jnp.sum(grad_query_low.astype(float_type), axis=0)
    grad_bias_value = jnp.sum(grad_value_low.astype(float_type), axis=0)
    grad_normed_one = jnp.einsum(
        "rm,dm->rd", grad_mixed, joint_back, preferred_element_type=float_type
    )
    grad_input_part, grad_gain_one, grad_shift_one = norm_pull_one(grad_normed_one)
    input_grad = (grad_residual + grad_input_part).astype(half_type)
    shard_grads = (
        lax.psum_scatter(grad_gain_one, ("seq", "band"), scatter_dimension=0, tiled=True),
        lax.psum_scatter(grad_shift_one, ("seq", "band"), scatter_dimension=0, tiled=True),
        lax.psum_scatter(grad_joint_weight, ("seq", "band"), scatter_dimension=0, tiled=True),
        lax.psum_scatter(grad_bias_query, ("seq", "band"), scatter_dimension=0, tiled=True),
        lax.psum_scatter(grad_bias_value, ("seq", "band"), scatter_dimension=0, tiled=True),
        lax.psum_scatter(grad_proj_weight, ("seq", "band"), scatter_dimension=0, tiled=True),
        lax.psum_scatter(grad_proj_bias, ("seq", "band"), scatter_dimension=0, tiled=True),
        lax.psum_scatter(grad_gain_two, ("seq", "band"), scatter_dimension=0, tiled=True),
        lax.psum_scatter(grad_shift_two, ("seq", "band"), scatter_dimension=0, tiled=True),
        lax.psum_scatter(grad_up_weight, ("seq", "band"), scatter_dimension=0, tiled=True),
        lax.psum_scatter(grad_up_bias, ("seq", "band"), scatter_dimension=0, tiled=True),
        lax.psum_scatter(grad_down_weight, ("seq", "band"), scatter_dimension=0, tiled=True),
        lax.psum_scatter(grad_down_bias, ("seq", "band"), scatter_dimension=0, tiled=True),
    )
    return (
        block_result.astype(half_type)[None],
        input_grad[None],
        shard_grads[0],
        shard_grads[1],
        shard_grads[2],
        shard_grads[3],
        shard_grads[4],
        shard_grads[5],
        shard_grads[6],
        shard_grads[7],
        shard_grads[8],
        shard_grads[9],
        shard_grads[10],
        shard_grads[11],
        shard_grads[12],
    )


F32 = jnp.float32
BF16 = jnp.bfloat16
MESH_ID = pl.DeviceIdType.MESH
ROWS = 128
LANES = 128
COPIES = 240


def dot(lhs, rhs):
    return jnp.dot(lhs, rhs, preferred_element_type=F32)


def dot_nt(lhs, rhs):
    return lax.dot_general(lhs, rhs, (((1,), (1,)), ((), ())), preferred_element_type=F32)


def dot_tn(lhs, rhs):
    return lax.dot_general(lhs, rhs, (((0,), (0,)), ((), ())), preferred_element_type=F32)


def flat_column(jj, ch):
    return (ch // 2) * 16 + (jj // 4) * 8 + (ch % 2) * 4 + jj % 4


def shard_place(i):
    return (i // 16) * 2 + (i // 4) % 2, ((i // 8) % 2) * 4 + i % 4


def fused_kernel(copies, *refs):
    (
        xin, cin, seg_in, len_in, wq, wo, wi, wd,
        p0, p1, p2, p3, p4, p5, p6, p7, pb,
        out_block, out_input, out_q, out_o, out_i, out_d, out_small,
        X, N0, N1, N2, GM, GB, SGI, SG, PK, SP, FULL, PV,
        WQI, WSQ, RQ, WQ, WO, WII, WSI, RI, WI, WD,
        QS, KK, VV, QT, KT, VT, CODE, SC, PT, INV, OT, OL,
        PA, CS, PB, CSB, SB, RV, XO, N2F, HAT, HA, GP, GA,
        DK, DV, DQ, GMX,
        GQ, GI, GD, XQ, XI, XD, HQ, HI, HD, ZQ, ZI, ZD, TQ, TI, TD,
        GO, GOF, XGO, TGO,
        VG, VR, SL, SLR, SLF, RS_, BG, BO, BI,
        ssem, rsem, lsem,
    ) = refs
    s = lax.axis_index("seq")
    b = lax.axis_index("band")
    x, c = lax.div(s, 2), lax.rem(s, 2)
    zh, l = lax.div(b, 4), lax.rem(b, 4)
    zl, y = lax.div(l, 2), lax.rem(l, 2)
    t, j = x * 2 + zh, c * 4 + l

    def flip(v, d):
        return 1 - v if d else v

    def flip_l(d):
        return flip(zl, d // 2) * 2 + flip(y, d % 2)

    def dev(dx=0, dc=0, dzh=0, dl=0):
        return (flip(x, dx) * 2 + flip(c, dc), flip(zh, dzh) * 4 + flip_l(dl))

    roles = (l, flip_l(2), flip_l(1), flip_l(3))

    counter = [0]
    pending = []

    def slots(n=1):
        first = counter[0]
        counter[0] += n
        assert counter[0] <= copies
        return first

    def send(src, dst, device, sem):
        copy = pltpu.make_async_remote_copy(
            src_ref=src, dst_ref=dst, send_sem=ssem.at[sem], recv_sem=rsem.at[sem],
            device_id=device, device_id_type=MESH_ID)
        copy.start()
        return copy

    def push(src, dst, device, sem):
        copy = send(src, dst, device, sem)
        pending.append(copy)
        return copy

    def arrive(dst, sem):
        pltpu.make_async_remote_copy(
            src_ref=dst, dst_ref=dst, send_sem=ssem.at[sem], recv_sem=rsem.at[sem],
            device_id=dev(dc=1), device_id_type=MESH_ID).wait_recv()

    def left(src, sem):
        pltpu.make_async_remote_copy(
            src_ref=src, dst_ref=src, send_sem=ssem.at[sem], recv_sem=rsem.at[sem],
            device_id=dev(dc=1), device_id_type=MESH_ID).wait_send()

    def move(src, dst, sem):
        return pltpu.make_async_copy(src, dst, lsem.at[sem])

    group_masks = [(dc, dl) for dl in (3, 1, 2, 0) for dc in (0, 1) if (dc, dl) != (0, 0)]
    line_masks = [(dx, dc, dzh) for dx in (1, 0) for dc in (0, 1) for dzh in (1, 0) if dx + dc + dzh]

    def group(dc, dl):
        return flip(c, dc) * 4 + flip_l(dl)

    native = c == zh
    foreign = jnp.logical_not(native)
    partner = dev(dc=1, dzh=1)
    their_block = (1 - c) * 4 + l

    barrier = pltpu.get_barrier_semaphore()
    peers = [dict(dc=dc, dl=dl) for dc, dl in group_masks]
    peers += [dict(dx=a, dc=e, dzh=f) for a, e, f in line_masks if (a, e, f) != (0, 1, 0)]
    for peer in peers:
        pl.semaphore_signal(barrier, inc=1, device_id=dev(**peer), device_id_type=MESH_ID)
    get_q, get_i, get_d = move(wq, WQI, 0), move(wi, WII, 1), move(wd, WD.at[t], 2)
    get_x, get_c = move(xin.at[0], X.at[j], 3), move(cin.at[0], GM.at[j], 4)
    get_q.start()
    get_i.start()
    get_d.start()

    @pl.when(native)
    def _():
        get_x.start()
        get_c.start()

    lane_group = lax.broadcasted_iota(jnp.int32, (1, LANES), 1) // 32
    PK[...] = jnp.zeros_like(PK)
    for p, ref in enumerate((p0, p1, p2, p3, p4, p5, p6, p7)):
        value = ref[...].astype(F32).reshape(1, 32)
        PK[p : p + 1] = jnp.where(lane_group == l, jnp.concatenate([value] * 4, axis=1), 0.0)
    own_bias = pb[...].astype(F32).reshape(1, LANES)
    for r in range(4):
        PK[8 + r : 9 + r] = jnp.where(l == r, own_bias, jnp.zeros_like(own_bias))
    SGI[...] = jnp.zeros_like(SGI)
    SGI[0:1] = seg_in[...].astype(F32)
    SGI[1:2, 0:SUBGRIDS] = len_in[...].astype(F32)
    get_q.wait()
    for jj in range(8):
        for ch in range(3):
            WSQ[jj, ch] = WQI[:, ch * D + jj * LANES : ch * D + (jj + 1) * LANES]
    for ch in range(3):
        RQ[ch, t, j] = WSQ[j, ch]
    pl.semaphore_wait(barrier, len(peers))

    sem_px, sem_pc, sem_ps = slots(), slots(), slots()
    sem_wq, sem_s1 = slots(8), slots(4)
    for dl in (1, 2, 3):
        push(PK, SP.at[dl], dev(dl=dl), sem_s1 + dl)

    @pl.when(native)
    def _():
        SG[j] = SGI[...]

    @pl.when(foreign)
    def _():
        send(SGI, SG.at[their_block], partner, sem_ps)
        send(xin.at[0], X.at[their_block], partner, sem_px)

    for dc, dl in group_masks:
        push(WSQ.at[group(dc, dl)], RQ.at[:, t, j], dev(dc=dc, dl=dl), sem_wq + dc * 4 + dl)

    class Gather:
        def __init__(self, buf):
            self.buf, self.far, self.near = buf, slots(4), slots(4)

        def start(self):
            block = self.buf.at[j]
            copies_out = [
                send(block, block, (s, zh * 4 + roles[1]), self.far + 1),
                send(block, block, (s, zh * 4 + roles[2]), self.far + 2),
                send(block, block, dev(dc=1), self.near),
            ]
            return copies_out

        def begin(self):
            pending.extend(self.start())

        def forward(self, k):
            block = self.buf.at[c * 4 + roles[k]]
            arrive(block, self.far + k)
            if k == 1:
                push(block, block, (s, zh * 4 + roles[2]), self.far + 3)
            push(block, block, dev(dc=1), self.near + k)

        def sibling(self, k):
            arrive(self.buf.at[(1 - c) * 4 + roles[k]], self.near + k)

    gather_x = Gather(X)
    gather_g = Gather(GM)

    @pl.when(native)
    def _():
        get_x.wait()
        gather_x.start()

    sem_wo, sem_wt = slots(4), slots(4)
    pair_l = c * 2 + zh
    to_self = jnp.logical_and(x == c, l == pair_l)
    is_root = jnp.logical_and(x == c, zh == y)
    root_mask = jnp.abs(x - c) * 2 + jnp.abs(zh - y)
    get_o = move(wo, WO.at[l], 5)

    @pl.when(to_self)
    def _():
        get_o.start()

    @pl.when(jnp.logical_not(to_self))
    def _():
        send(wo, WO.at[l], (x * 2 + x, zh * 4 + pair_l), sem_wo + l)

    q_own = x * 4 + c * 2 + zh
    slab = PK[...]
    for dl in (1, 2, 3):
        arrive(SP.at[dl], sem_s1 + dl)
        slab += SP[dl]
    FULL[q_own] = slab
    sem_s2 = slots(8)
    for dx, dc, dzh in line_masks:
        push(FULL.at[q_own], FULL.at[q_own], dev(dx=dx, dc=dc, dzh=dzh), sem_s2 + dx * 4 + dc * 2 + dzh)

    class Spread:
        def __init__(self, buf):
            self.buf, self.sem = buf, slots(3)

        def start_z(self, keep=True):
            block = self.buf.at[t]
            copy = send(block, block, dev(dzh=1), self.sem)
            if keep:
                pending.append(copy)

        def start_x(self):
            block = self.buf.at[t]
            push(block, block, dev(dx=1), self.sem + 1)

        def sent_z(self):
            left(self.buf.at[t], self.sem)

        def start(self):
            self.start_z()
            self.start_x()

        def forward(self):
            block = self.buf.at[x * 2 + 1 - zh]
            arrive(block, self.sem)
            push(block, block, dev(dx=1), self.sem + 2)

        def finish(self):
            arrive(self.buf.at[(1 - x) * 2 + zh], self.sem + 1)
            arrive(self.buf.at[(1 - x) * 2 + 1 - zh], self.sem + 2)

    spread_q = [Spread(RQ.at[ch]) for ch in range(3)]
    for dc, dl in group_masks:
        arrive(RQ.at[:, t, group(dc, dl)], sem_wq + dc * 4 + dl)
    for ch in range(3):
        spread_q[ch].start()

    sem_sg = slots(8)

    @pl.when(foreign)
    def _():
        arrive(SG.at[j], sem_ps)

    for dc, dl in group_masks:
        push(SG.at[j], SG.at[j], dev(dc=dc, dl=dl), sem_sg + dc * 4 + dl)
    @pl.when(foreign)
    def _():
        arrive(X.at[j], sem_px)
        gather_x.start()

    for slot in range(4):
        @pl.when(jnp.logical_and(is_root, jnp.logical_not(jnp.logical_and(zl == c, l == slot))))
        def _():
            arrive(WO.at[slot], sem_wo + slot)

    @pl.when(to_self)
    def _():
        get_o.wait()

    @pl.when(is_root)
    def _():
        send(WO, WO, dev(dzh=1), sem_wt + 1)
        send(WO, WO, dev(dx=1), sem_wt + 2)


    @pl.when(foreign)
    def _():
        send(cin.at[0], GM.at[their_block], partner, sem_pc)

    for dx, dc, dzh in line_masks:
        arrive(FULL.at[flip(x, dx) * 4 + flip(c, dc) * 2 + flip(zh, dzh)], sem_s2 + dx * 4 + dc * 2 + dzh)
    for q in range(8):
        PV[:, q * LANES : (q + 1) * LANES] = FULL[q]
    gain1, shift1 = PV[0:1, :], PV[1:2, :]

    def norm_rows(value, gain, shift):
        average = jnp.mean(value, axis=-1, keepdims=True)
        centered = value - average
        root = lax.rsqrt(jnp.mean(centered * centered, axis=-1, keepdims=True) + EPSILON)
        normal = centered * root
        return normal, root, normal * gain + shift

    def norm_one(block):
        for r in range(2):
            rows = pl.ds(r * 64, 64)
            normal, _, value = norm_rows(X[block, rows].astype(F32), gain1, shift1)
            N0[block, rows] = normal.astype(BF16)
            N1[block, rows] = value.astype(BF16)

    norm_one(j)

    gather_x.sibling(0)
    norm_one((1 - c) * 4 + l)
    gather_x.forward(1)
    gather_x.forward(2)
    norm_one(c * 4 + roles[1])
    norm_one(c * 4 + roles[2])
    spread_q[0].forward()
    get_i.wait()
    for jj in range(8):
        for ch in range(4):
            flat = flat_column(jj, ch)
            WSI[jj, ch] = WII[:, flat * LANES : (flat + 1) * LANES]
    sem_wi = slots(8)
    for dc, dl in group_masks:
        push(WSI.at[group(dc, dl)], RI.at[t, j], dev(dc=dc, dl=dl), sem_wi + dc * 4 + dl)
    RI[t, j] = WSI[j]
    for k in (1, 2):
        gather_x.sibling(k)
    gather_x.forward(3)
    norm_one((1 - c) * 4 + roles[1])
    spread_q[1].forward()
    norm_one((1 - c) * 4 + roles[2])
    norm_one(c * 4 + roles[3])
    spread_q[2].forward()
    gather_x.sibling(3)
    norm_one((1 - c) * 4 + roles[3])

    get_d.wait()
    spread_i, spread_d = Spread(RI), Spread(WD)

    for dc, dl in group_masks:
        arrive(SG.at[group(dc, dl)], sem_sg + dc * 4 + dl)
    lens = SG[j, 1:2, :]
    row_ids = lax.broadcasted_iota(jnp.int32, (LANES, LANES), 0)
    lane_ids = lax.broadcasted_iota(jnp.int32, (LANES, LANES), 1)
    label_row = lane_ids.astype(F32)
    label_col = row_ids.astype(F32)
    earlier = (lane_ids < row_ids).astype(BF16)
    running = jnp.zeros((1, LANES), F32)
    for blk in range(8):
        onehot = (label_col == SG[blk, 0:1, :]).astype(F32).T
        before = dot(earlier, onehot.astype(BF16)) + running
        running = running + jnp.sum(onehot, axis=0, keepdims=True)
        rank = jnp.sum(before * onehot, axis=1, keepdims=True)
        limit = jnp.sum(onehot * lens, axis=1, keepdims=True)
        ident = jnp.sum(label_row * onehot, axis=1, keepdims=True)
        CODE[blk] = jnp.broadcast_to(jnp.where(rank < limit, ident, -1.0), (ROWS, LANES))

    @pl.when(native)
    def _():
        get_c.wait()

    @pl.when(foreign)
    def _():
        arrive(GM.at[j], sem_pc)

    is_real = CODE[j][:, 0:1] >= 0.0
    GM[j] = jnp.where(is_real, GM[j].astype(F32), 0.0).astype(BF16)
    gather_g.begin()

    @pl.when(jnp.logical_not(is_root))
    def _():
        arrive(WO, sem_wt + root_mask)

    @pl.when(root_mask == 1)
    def _():
        send(WO, WO, dev(dx=1), sem_wt + 3)

    for dc, dl in group_masks:
        arrive(RI.at[t, group(dc, dl)], sem_wi + dc * 4 + dl)
    spread_i.start_z()
    spread_i.start_x()
    spread_d.start_x()
    for ch in range(3):
        spread_q[ch].finish()
        for i in range(32):
            tt, jj = shard_place(i)
            WQ[i * 32 : (i + 1) * 32, ch * LANES : (ch + 1) * LANES] = RQ[ch, tt, jj]
    bias_q, bias_v = FULL[j][2:3, :], FULL[j][3:4, :]
    for k in range(4):
        rows = pl.ds(k * 256, 256)
        normed = N1[2 * k : 2 * k + 2].reshape(256, D)
        mixed = dot(normed, WQ[...])
        queries = (mixed[:, :LANES] + bias_q).astype(BF16).astype(F32) * (HEAD_DIM ** -0.5)
        keys = mixed[:, LANES : 2 * LANES]
        values = mixed[:, 2 * LANES :] + bias_v
        QS[rows] = queries.astype(BF16)
        KK[rows] = keys.astype(BF16)
        VV[rows] = values.astype(BF16)
        QT[:, rows] = queries.T.astype(BF16)
        KT[:, rows] = keys.T.astype(BF16)
        VT[:, rows] = values.T.astype(BF16)


    def pair_lanes(lp):
        return (pl.ds(pl.multiple_of(lp * LANES, LANES), LANES), pl.ds(pl.multiple_of(512 + lp * LANES, LANES), LANES))

    def cat_lanes(ref, lp):
        first, second = pair_lanes(lp)
        return jnp.concatenate([ref[:, first], ref[:, second]], axis=1)

    def cat_rows(ref, lp):
        return jnp.concatenate([ref[lp], ref[4 + lp]], axis=0)

    class Scatter:
        def __init__(self, part, chip, number, before=None, tree=True):
            self.part, self.chip, self.number, self.before, self.tree = part, chip, number, before, tree
            self.near, self.far = slots(4), slots(8)

        def emit(self, m, value):
            if self.before is not None:
                left(self.part.at[m, 1 - c], self.before.near + m)
            low = value.astype(BF16)
            self.part[m, 0] = low[:ROWS]
            self.part[m, 1] = low[ROWS:]
            send(self.part.at[m, 1 - c], SB.at[self.number, m], dev(dc=1), self.near + m)

        def pieces(self, m):
            if self.tree and m > 1:
                return ((pl.ds(0, 64), self.far + m), (pl.ds(64, 64), self.far + 4 + m))
            return ((pl.ds(0, ROWS), self.far + m),)

        def chip_left(self, m):
            for rows, sem in self.pieces(m):
                left(self.chip.at[m, rows], sem)

        def reduce(self, m):
            arrive(SB.at[self.number, m], self.near + m)
            if m == 0:
                return
            if self.before is not None:
                self.before.chip_left(m)
            for k, (rows, sem) in enumerate(self.pieces(m)):
                total = self.part[m, c, rows].astype(F32) + SB[self.number, m, rows].astype(F32)
                if self.tree and m == 2:
                    across = RV.at[self.number, 3, rows]
                    arrive(across, self.pieces(3)[k][1])
                    total += across[...].astype(F32)
                self.chip[m, rows] = total.astype(BF16)
                device = dev(dl=1) if self.tree and m == 3 else dev(dl=m)
                send(self.chip.at[m, rows], RV.at[self.number, m, rows], device, sem)

        def finish(self):
            for m in (1, 2) if self.tree else (1, 2, 3):
                for rows, sem in self.pieces(m):
                    arrive(RV.at[self.number, m, rows], sem)

        def rows(self, rows):
            total = self.part[0, c, rows].astype(F32) + SB[self.number, 0, rows].astype(F32)
            for m in (1, 2) if self.tree else (1, 2, 3):
                total += RV[self.number, m, rows].astype(F32)
            return total

        def close(self):
            for m in range(4):
                left(self.part.at[m, 1 - c], self.near + m)
                if m:
                    self.chip_left(m)

    head_rows = lax.broadcasted_iota(jnp.int32, (LANES, 256), 0)
    head_lanes = lax.broadcasted_iota(jnp.int32, (256, LANES), 1)

    def only_rows(value, h):
        return jnp.where((head_rows >= h * 64) & (head_rows < (h + 1) * 64), value, jnp.zeros_like(value))

    def only_lanes(value, h):
        return jnp.where((head_lanes >= h * 64) & (head_lanes < (h + 1) * 64), value, jnp.zeros_like(value))

    scatter_a = Scatter(PA, CS, 0)
    attend_order = (3, 1, 2, 0)
    for k, m in enumerate(attend_order):
        lp = flip_l(m)
        queries_t = cat_lanes(QT, lp)
        seg_q = jnp.concatenate([SG[lp, 0:1, :], SG[4 + lp, 0:1, :]], axis=1)
        for h in range(2):
            masked_t = only_rows(queries_t.astype(F32), h).astype(BF16)
            top = jnp.full((8, 256), NEGATIVE, F32)
            for i in range(8):
                rows = pl.ds(i * ROWS, ROWS)
                value = dot(KK[rows], masked_t)
                code = CODE[i]
                allowed = jnp.concatenate([code, code], axis=1) == seg_q
                value = jnp.where(allowed, value, NEGATIVE)
                SC[h, rows] = value
                top = jnp.maximum(top, jnp.max(value.reshape(16, 8, 256), axis=0))
            top = jnp.max(top, axis=0, keepdims=True)
            total = jnp.zeros((8, 256), F32)
            for i in range(8):
                rows = pl.ds(i * ROWS, ROWS)
                value = jnp.exp(SC[h, rows] - top)
                PT[m, h, rows] = value.astype(BF16)
                total = total + jnp.sum(value.reshape(16, 8, 256), axis=0)
            inverse = 1.0 / jnp.sum(total, axis=0, keepdims=True)
            INV[m, h] = jnp.broadcast_to(inverse, (8, 256))
            OT[m, h * 64 : (h + 1) * 64] = dot(VT[h * 64 : (h + 1) * 64, :], PT[m, h]) * inverse
            if k and h == 0:
                scatter_a.reduce(attend_order[k - 1])
            if k == 1 and h == 1:
                spread_d.start_z()
            if k == 2 and h == 0:
                gather_g.forward(2)
            if k == 3 and h == 1:
                gather_g.forward(1)
        joined = OT[m]
        OL[m] = joined.astype(BF16)
        scatter_a.emit(m, dot(joined.T.astype(BF16), WO[...].reshape(LANES, D)))
    spread_i.forward()
    scatter_a.reduce(0)
    scatter_a.finish()

    gain2, shift2, bias_o = PV[5:6, :], PV[6:7, :], PV[4:5, :]
    for r in range(4):
        rows = pl.ds(r * 32, 32)
        residual = X[j, rows].astype(F32) + scatter_a.rows(rows) + bias_o
        XO[rows] = residual
        normal, root, value = norm_rows(residual, gain2, shift2)
        N2F[rows] = normal
        RS_[rows] = jnp.broadcast_to(root, (32, LANES))
        N2[j, rows] = value.astype(BF16)
    gather_n = Gather(N2)
    gather_n.begin()

    spread_i.finish()
    for i in range(32):
        tt, jj = shard_place(i)
        for ch in range(4):
            WI[i * 32 : (i + 1) * 32, ch * LANES : (ch + 1) * LANES] = RI[tt, jj, ch]
    pick = lax.broadcasted_iota(jnp.int32, (16, LANES), 0) == 8 + l
    bias_in = jnp.concatenate(
        [
            jnp.sum(jnp.where(pick, FULL[(ch // 2) * 4 + c * 2 + ch % 2], 0.0), axis=0, keepdims=True)
            for ch in range(4)
        ],
        axis=1,
    )
    scatter_m = Scatter(PA, CS, 1, scatter_a, tree=False)
    scatter_b = Scatter(PB, CSB, 2)
    BG[0:1] = jnp.zeros((1, 512), F32)

    def hidden_part(m):
        lp = flip_l(m)
        first, second = pair_lanes(lp)
        hidden = dot(cat_rows(N2, lp), WI[...]) + bias_in
        phi_cap = 0.5 * (1.0 + lax.erf(hidden * 0.7071067811865476))
        phi = jnp.exp(-0.5 * hidden * hidden) * 0.3989422804014327
        act = hidden * phi_cap
        GA[m] = phi_cap + hidden * phi
        HA[m] = act.astype(BF16)
        act_t = act.T.astype(BF16)
        HAT[:, first] = act_t[:, :ROWS]
        HAT[:, second] = act_t[:, ROWS:]

    def hidden_back(m):
        lp = flip_l(m)
        grad_act = dot_nt(cat_rows(GM, lp), WD[...].reshape(512, D))
        grad_pre = (grad_act * GA[m]).astype(BF16)
        GP[lp] = grad_pre[:ROWS]
        GP[4 + lp] = grad_pre[ROWS:]
        BG[0:1] += jnp.sum(grad_pre.astype(F32), axis=0, keepdims=True)
        scatter_m.emit(m, dot_nt(grad_pre, WI[...]))

    gather_n.sibling(0)
    hidden_part(0)
    spread_d.forward()
    gather_n.forward(2)
    gather_n.forward(1)
    gather_g.forward(3)
    gather_g.sibling(0)
    spread_d.finish()
    hidden_back(0)
    gather_n.sibling(2)
    hidden_part(1)
    gather_g.sibling(2)
    hidden_back(1)
    scatter_m.reduce(0)
    gather_n.sibling(1)
    hidden_part(2)
    gather_g.sibling(1)
    hidden_back(2)
    gather_n.forward(3)
    scatter_m.reduce(1)
    gather_n.sibling(3)
    hidden_part(3)
    gather_g.sibling(3)
    scatter_m.reduce(2)
    hidden_back(3)
    scatter_m.reduce(3)

    class Total:
        def __init__(self, part, from_x, middle, from_z):
            self.part, self.from_x, self.middle, self.from_z = part, from_x, middle, from_z
            self.sem = slots(3)

        def start_cross(self):
            push(self.part.at[(1 - x) * 2 + 1 - zh], self.from_x.at[1 - zh], dev(dx=1), self.sem)

        def start_keep(self):
            push(self.part.at[(1 - x) * 2 + zh], self.from_x.at[zh], dev(dx=1), self.sem + 2)

        def second(self):
            arrive(self.from_x.at[1 - zh], self.sem)
            self.middle[...] = (
                self.part[x * 2 + 1 - zh].astype(F32) + self.from_x[1 - zh].astype(F32)
            ).astype(BF16)
            push(self.middle, self.from_z, dev(dzh=1), self.sem + 1)

        def result(self):
            arrive(self.from_x.at[zh], self.sem + 2)
            arrive(self.from_z, self.sem + 1)
            return self.part[t].astype(F32) + self.from_x[zh].astype(F32) + self.from_z[...].astype(F32)

    total_d = Total(GD, XD, HD, ZD)
    total_i = Total(GI, XI, HI, ZI)
    total_q = [Total(GQ.at[ch], XQ.at[ch], HQ.at[ch], ZQ.at[ch]) for ch in range(3)]
    for ch in range(4):
        GD[ch] = dot(HAT[ch * LANES : (ch + 1) * LANES, :], GM[...].reshape(8 * ROWS, D)).astype(BF16)
    total_d.start_cross()
    all_pre = GP[...].reshape(8 * ROWS, 512)
    for blk in range(8):
        product = dot_tn(N2[:, :, blk * LANES : (blk + 1) * LANES].reshape(8 * ROWS, LANES), all_pre).astype(BF16)
        for r in range(4):
            tt, jj = shard_place(blk * 4 + r)
            for ch in range(4):
                GI[tt, jj, ch] = product[r * 32 : (r + 1) * 32, ch * LANES : (ch + 1) * LANES]
    total_i.start_cross()
    total_d.start_keep()
    total_i.start_keep()

    def norm_back(grad, normal, root, gain):
        scaled = grad * gain
        return root * (scaled - jnp.mean(scaled, axis=-1, keepdims=True)
                       - normal * jnp.mean(scaled * normal, axis=-1, keepdims=True))

    def forward_out(m):
        scatter_b.emit(m, dot(HA[m], WD[...].reshape(512, D)))

    for m in attend_order:
        forward_out(m)
    scatter_m.finish()
    sums = [jnp.zeros((1, D), F32) for _ in range(4)]
    for r in range(4):
        rows = pl.ds(r * 32, 32)
        grad = scatter_m.rows(rows)
        normal = N2F[rows]
        top_grad = GM[j, rows].astype(F32)
        grad_residual = top_grad + norm_back(grad, normal, RS_[rows][:, 0:1], gain2)
        low = grad_residual.astype(BF16)
        GB[j, rows] = low
        N2F[rows] = grad_residual
        for i, value in enumerate((grad * normal, grad, low.astype(F32), top_grad)):
            sums[i] += jnp.sum(value, axis=0, keepdims=True)
    vectors = {5: sums[0], 6: sums[1], 4: sums[2], 7: sums[3]}
    gather_b = Gather(GB)
    gather_b.begin()

    DK[...] = jnp.zeros_like(DK)
    DV[...] = jnp.zeros_like(DV)
    GOF[...] = jnp.zeros_like(GOF)

    def attend_back(m):
        lp = flip_l(m)
        first, second = pair_lanes(lp)
        branch = cat_rows(GB, lp)
        grad_att = dot_nt(branch, WO[...].reshape(LANES, D)).astype(BF16).astype(F32)
        GOF[...] += dot(OL[m], branch)
        grad_att_t = grad_att.T
        both = grad_att_t * OT[m]
        queries = jnp.concatenate([QS[first], QS[second]], axis=0).astype(F32)
        for h in range(2):
            inverse = INV[m, h][0:1]
            delta = jnp.sum(both[h * 64 : (h + 1) * 64], axis=0, keepdims=True) * inverse
            scaled_t = only_rows(grad_att_t * inverse, h)
            scaled_low_t = scaled_t.astype(BF16)
            scaled_low = scaled_t.T.astype(BF16)
            queries_h = only_lanes(queries, h).astype(BF16)
            for i in range(8):
                rows = pl.ds(i * ROWS, ROWS)
                probs = PT[m, h, rows]
                value = dot(VV[rows], scaled_low_t)
                grad_scores = (probs.astype(F32) * (value - delta)).astype(BF16)
                DV[rows] += dot(probs, scaled_low)
                DK[rows] += dot(grad_scores, queries_h)
                PT[m, h, rows] = grad_scores
            DQ[h * 64 : (h + 1) * 64, :] = dot(KT[h * 64 : (h + 1) * 64, :], PT[m, h]) * (HEAD_DIM ** -0.5)
        dq_rows = DQ[...].T.astype(BF16)
        GMX[lp, :, 0:LANES] = dq_rows[:ROWS]
        GMX[4 + lp, :, 0:LANES] = dq_rows[ROWS:]

    total_d.second()
    gather_b.sibling(0)
    attend_back(0)
    gather_b.forward(2)
    gather_b.forward(1)
    scatter_b.reduce(3)
    gather_b.sibling(2)
    attend_back(1)
    total_i.second()
    gather_b.sibling(1)
    attend_back(2)
    gather_b.forward(3)
    scatter_b.reduce(1)
    scatter_b.reduce(0)
    gather_b.sibling(3)
    attend_back(3)
    scatter_b.reduce(2)

    for blk in range(8):
        rows = pl.ds(blk * ROWS, ROWS)
        GMX[blk, :, LANES : 2 * LANES] = DK[rows].astype(BF16)
        GMX[blk, :, 2 * LANES :] = DV[rows].astype(BF16)
    all_mixed = GMX[...].reshape(8 * ROWS, 3 * LANES)
    scatter_n = Scatter(PA, CS, 3, scatter_m)

    def back_out(m):
        scatter_n.emit(m, dot_nt(cat_rows(GMX, flip_l(m)), WQ[...]))

    def joint_grad(blk):
        product = dot_tn(N1[:, :, blk * LANES : (blk + 1) * LANES].reshape(8 * ROWS, LANES), all_mixed).astype(BF16)
        for r in range(4):
            tt, jj = shard_place(blk * 4 + r)
            for ch in range(3):
                GQ[ch, tt, jj] = product[r * 32 : (r + 1) * 32, ch * LANES : (ch + 1) * LANES]

    back_out(3)
    for blk in range(4):
        joint_grad(blk)
    scatter_n.reduce(3)
    for blk in range(4, 8):
        joint_grad(blk)
    for ch in range(3):
        total_q[ch].start_cross()
    for ch in range(3):
        total_q[ch].start_keep()

    back_out(1)
    back_out(2)
    scatter_n.reduce(1)
    back_out(0)
    GO[...] = GOF[...].astype(BF16)
    sem_go, sem_gs = slots(4), slots(4)

    @pl.when(jnp.logical_not(is_root))
    def _():
        send(GO, XGO.at[root_mask], (c * 2 + c, y * 4 + l), sem_go + root_mask)

    scatter_n.reduce(0)

    sums = [jnp.zeros((1, D), F32) for _ in range(2)]
    for m in range(4):
        lp = flip_l(m)
        for half in range(2):
            value = PA[m, half].astype(F32)
            sums[0] += jnp.sum(value * N0[half * 4 + lp].astype(F32), axis=0, keepdims=True)
            sums[1] += jnp.sum(value, axis=0, keepdims=True)
    vectors[0], vectors[1] = sums
    scatter_n.reduce(2)
    mixed_sums = jnp.sum(all_mixed.astype(F32), axis=0, keepdims=True)
    for q in range(8):
        VG[q] = jnp.zeros((16, LANES), F32)
        for p in (0, 1, 4, 5, 6, 7):
            VG[q, p : p + 1] = vectors[p][:, q * LANES : (q + 1) * LANES]
        for p, ch in ((2, 0), (3, 2)):
            VG[q, p : p + 1] = jnp.where(j == q, mixed_sums[:, ch * LANES : (ch + 1) * LANES], 0.0)
        ch = (q // 4) * 2 + q % 2
        for r in range(4):
            here = jnp.logical_and(c == (q // 2) % 2, l == r)
            VG[q, 8 + r : 9 + r] = jnp.where(here, BG[0:1, ch * LANES : (ch + 1) * LANES], 0.0)
    sem_v1, sem_v2 = slots(8), slots(4)
    for dx, dc, dzh in line_masks:
        mask = dx * 4 + dc * 2 + dzh
        push(VG.at[flip(x, dx) * 4 + flip(c, dc) * 2 + flip(zh, dzh)], VR.at[mask], dev(dx=dx, dc=dc, dzh=dzh), sem_v1 + mask)

    for ch in range(3):
        total_q[ch].second()

    bias_d = PV[7:8, :]
    sem_out, sem_in = slots(), slots()
    scatter_b.finish()
    for r in range(4):
        rows = pl.ds(r * 32, 32)
        BO[rows] = (XO[rows] + scatter_b.rows(rows) + bias_d).astype(BF16)
    put_block = move(BO, out_block.at[0], 6)

    @pl.when(native)
    def _():
        put_block.start()

    @pl.when(foreign)
    def _():
        send(BO, out_block.at[0], partner, sem_out)

    scatter_n.finish()
    for r in range(4):
        rows = pl.ds(r * 32, 32)
        grad = scatter_n.rows(rows)
        normal, root, _ = norm_rows(X[j, rows].astype(F32), gain1, shift1)
        BI[rows] = (N2F[rows] + norm_back(grad, normal, root, gain1)).astype(BF16)
    put_input = move(BI, out_input.at[0], 9)

    @pl.when(native)
    def _():
        put_input.start()

    @pl.when(foreign)
    def _():
        send(BI, out_input.at[0], partner, sem_in)

    slab = VG[q_own]
    for dx, dc, dzh in line_masks:
        mask = dx * 4 + dc * 2 + dzh
        arrive(VR.at[mask], sem_v1 + mask)
        slab += VR[mask]
    SL[...] = slab
    for dl in (1, 2, 3):
        push(SL, SLR.at[dl], dev(dl=dl), sem_v2 + dl)

    TD[...] = total_d.result().astype(BF16)
    put_d = move(TD, out_d, 7)
    put_d.start()
    TI[...] = total_i.result().astype(BF16)
    sem_ti, sem_tq = slots(8), slots(8 * 3)
    for dc, dl in group_masks:
        push(TI.at[group(dc, dl)], out_i.at[j], dev(dc=dc, dl=dl), sem_ti + dc * 4 + dl)
    put_i = move(TI.at[j], out_i.at[j], 8)
    put_i.start()

    put_o = move(TGO.at[l], out_o, 10)

    @pl.when(is_root)
    def _():
        total = GOF[...]
        for mask in (1, 2, 3):
            arrive(XGO.at[mask], sem_go + mask)
            total += XGO[mask].astype(F32)
        TGO[...] = total.astype(BF16).reshape(4, 32, D)
        for slot in range(4):
            mine = jnp.logical_and(zl == c, l == slot)

            @pl.when(mine)
            def _():
                put_o.start()

            @pl.when(jnp.logical_not(mine))
            def _():
                send(TGO.at[slot], out_o, (x * 2 + zl, zh * 4 + slot), sem_gs + slot)

    for ch in range(3):
        TQ[ch] = total_q[ch].result().astype(BF16)
        for dc, dl in group_masks:
            push(TQ.at[ch, group(dc, dl)], out_q.at[ch, j], dev(dc=dc, dl=dl), sem_tq + ch * 8 + dc * 4 + dl)
    put_q = [move(TQ.at[ch, j], out_q.at[ch, j], 11 + ch) for ch in range(3)]
    for ch in range(3):
        put_q[ch].start()

    for dl in (1, 2, 3):
        arrive(SLR.at[dl], sem_v2 + dl)
        slab += SLR[dl]
    SLF[...] = slab
    put_small = move(SLF, out_small, 14)
    put_small.start()

    for dc, dl in group_masks:
        arrive(out_i.at[group(dc, dl)], sem_ti + dc * 4 + dl)
        for ch in range(3):
            arrive(out_q.at[ch, group(dc, dl)], sem_tq + ch * 8 + dc * 4 + dl)

    put_d.wait()
    put_i.wait()
    put_small.wait()
    for ch in range(3):
        put_q[ch].wait()

    @pl.when(native)
    def _():
        put_block.wait()
        put_input.wait()

    @pl.when(foreign)
    def _():
        left(SGI, sem_ps)
        left(xin.at[0], sem_px)
        left(cin.at[0], sem_pc)
        left(BO, sem_out)
        left(BI, sem_in)
        arrive(out_block.at[0], sem_out)
        arrive(out_input.at[0], sem_in)

    @pl.when(to_self)
    def _():
        put_o.wait()

    @pl.when(jnp.logical_not(to_self))
    def _():
        left(wo, sem_wo + l)
        arrive(out_o, sem_gs + l)

    @pl.when(jnp.logical_not(is_root))
    def _():
        left(GO, sem_go + root_mask)

    @pl.when(root_mask == 1)
    def _():
        left(WO, sem_wt + 3)

    @pl.when(is_root)
    def _():
        for mask in (1, 2):
            left(WO, sem_wt + mask)
        for slot in range(4):
            @pl.when(jnp.logical_not(jnp.logical_and(zl == c, l == slot)))
            def _():
                left(TGO.at[slot], sem_gs + slot)

    scatter_n.close()
    scatter_b.close()
    for k in (1, 2):
        left(X.at[j], gather_x.far + k)
    left(X.at[j], gather_x.near)
    for copy in pending:
        copy.wait_send()


def fused_scratch():
    def v(*shape):
        return pltpu.VMEM(shape, BF16)

    def f(*shape):
        return pltpu.VMEM(shape, F32)

    blocks = (8, ROWS, D)
    return [
        v(*blocks), v(*blocks), v(*blocks), v(*blocks), v(*blocks), v(*blocks),
        f(8, LANES), f(8, 8, LANES), f(16, LANES), f(4, 16, LANES), f(8, 16, LANES), f(16, D),
        v(32, 3 * D), v(8, 3, 32, LANES), v(3, 4, 8, 32, LANES), v(D, 3 * LANES), v(4, 32, D),
        v(32, 4 * D), v(8, 4, 32, LANES), v(4, 8, 4, 32, LANES), v(D, 512), v(4, LANES, D),
        v(D, LANES), v(D, LANES), v(D, LANES), v(LANES, D), v(LANES, D), v(LANES, D),
        f(8, ROWS, LANES), f(2, D, 256), v(4, 2, D, 256), f(4, 2, 8, 256),
        f(4, LANES, 256), v(4, LANES, 256),
        v(4, 2, ROWS, D), v(4, ROWS, D), v(4, 2, ROWS, D), v(4, ROWS, D),
        v(4, 4, ROWS, D), v(4, 4, ROWS, D), f(ROWS, D), f(ROWS, D),
        v(512, D), v(4, 256, 512), v(8, ROWS, 512), f(4, 256, 512),
        f(D, LANES), f(D, LANES), f(LANES, 256), v(8, ROWS, 3 * LANES),
        v(3, 4, 8, 32, LANES), v(4, 8, 4, 32, LANES), v(4, LANES, D),
        v(3, 2, 8, 32, LANES), v(2, 8, 4, 32, LANES), v(2, LANES, D),
        v(3, 8, 32, LANES), v(8, 4, 32, LANES), v(LANES, D),
        v(3, 8, 32, LANES), v(8, 4, 32, LANES), v(LANES, D),
        v(3, 8, 32, LANES), v(8, 4, 32, LANES), v(LANES, D),
        v(LANES, D), f(LANES, D), v(4, LANES, D), v(4, 32, D),
        f(8, 16, LANES), f(8, 16, LANES), f(16, LANES), f(4, 16, LANES), f(16, LANES),
        f(ROWS, LANES), f(8, 512), v(ROWS, D), v(ROWS, D),
        pltpu.SemaphoreType.DMA((COPIES,)),
        pltpu.SemaphoreType.DMA((COPIES,)),
        pltpu.SemaphoreType.DMA((16,)),
    ]


def finish_kernel(
    block, grad_in, grad_q, grad_o, grad_i, grad_d, small,
    out_block, out_input, o0, o1, out_q, o2, o3, out_o, o4, o5, o6, out_i, ob, out_d, o7,
):
    place = lax.rem(lax.axis_index("band"), 4)
    out_block[...] = block[...]
    out_input[...] = grad_in[...]
    for jj in range(8):
        for ch in range(3):
            out_q[:, ch * D + jj * LANES : ch * D + (jj + 1) * LANES] = grad_q[ch, jj].astype(F32)
        for ch in range(4):
            flat = flat_column(jj, ch)
            out_i[:, flat * LANES : (flat + 1) * LANES] = grad_i[jj, ch].astype(F32)
    out_o[...] = grad_o[...].astype(F32)
    out_d[...] = grad_d[...].astype(F32)
    slab = small[...]
    mine = jnp.zeros((16, 32), F32)
    for k in range(4):
        mine = jnp.where(place == k, slab[:, k * 32 : (k + 1) * 32], mine)
    for p, ref in enumerate((o0, o1, o2, o3, o4, o5, o6, o7)):
        ref[...] = mine[p : p + 1].reshape(32)
    pick = lax.broadcasted_iota(jnp.int32, (16, LANES), 0) == 8 + place
    ob[...] = jnp.sum(jnp.where(pick, slab, 0.0), axis=0, keepdims=True).reshape(LANES)


def fused_shards(
    block_in,
    attention_norm_gain,
    attention_norm_bias,
    query_key_value,
    query_bias,
    value_bias,
    output_weight,
    output_bias,
    mlp_norm_gain,
    mlp_norm_bias,
    mlp_in_weight,
    mlp_in_bias,
    mlp_out_weight,
    mlp_out_bias,
    cotangent,
    segment_ids,
    sub_lengths,
):
    vmem = pl.BlockSpec(memory_space=pltpu.VMEM)
    hbm = pl.BlockSpec(memory_space=pl.ANY)

    def shape(dims, kind):
        return jax.ShapeDtypeStruct(dims, kind)

    parts = pl.pallas_call(
        functools.partial(fused_kernel, COPIES),
        out_shape=(
            shape((1, ROWS, D), BF16),
            shape((1, ROWS, D), BF16),
            shape((3, 8, 32, LANES), BF16),
            shape((32, D), BF16),
            shape((8, 4, 32, LANES), BF16),
            shape((LANES, D), BF16),
            shape((16, LANES), F32),
        ),
        in_specs=[hbm, hbm, vmem, vmem, hbm, hbm, hbm, hbm] + [vmem] * 9,
        out_specs=(hbm,) * 7,
        scratch_shapes=fused_scratch(),
        compiler_params=pltpu.CompilerParams(
            collective_id=0, has_side_effects=True, vmem_limit_bytes=63 * 2**20
        ),
    )(
        block_in, cotangent, segment_ids, sub_lengths,
        query_key_value, output_weight, mlp_in_weight, mlp_out_weight,
        attention_norm_gain, attention_norm_bias, query_bias, value_bias,
        output_bias, mlp_norm_gain, mlp_norm_bias, mlp_out_bias, mlp_in_bias,
    )
    vector = shape((32,), F32)
    return pl.pallas_call(
        finish_kernel,
        out_shape=(
            shape((1, ROWS, D), BF16), shape((1, ROWS, D), BF16), vector, vector,
            shape((32, 3 * D), F32), vector, vector, shape((32, D), F32), vector, vector, vector,
            shape((32, 4 * D), F32), shape((LANES,), F32), shape((LANES, D), F32), vector,
        ),
        in_specs=[vmem] * 7,
        out_specs=(vmem,) * 15,
    )(*parts)


def solution(mesh):
    small_slice = dict(mesh.shape) == {"seq": 4, "band": 8}
    return jax.shard_map(
        fused_shards if small_slice else shards,
        mesh=mesh,
        in_specs=(
            P("seq", "band", None),
            P(("seq", "band")),
            P(("seq", "band")),
            P(("seq", "band"), None),
            P(("seq", "band")),
            P(("seq", "band")),
            P(("seq", "band"), None),
            P(("seq", "band")),
            P(("seq", "band")),
            P(("seq", "band")),
            P(("seq", "band"), None),
            P(("seq", "band")),
            P(("seq", "band"), None),
            P(("seq", "band")),
            P("seq", "band", None),
            P("seq", "band"),
            P("seq", None),
        ),
        out_specs=(
            P("seq", "band", None),
            P("seq", "band", None),
            P(("seq", "band")),
            P(("seq", "band")),
            P(("seq", "band"), None),
            P(("seq", "band")),
            P(("seq", "band")),
            P(("seq", "band"), None),
            P(("seq", "band")),
            P(("seq", "band")),
            P(("seq", "band")),
            P(("seq", "band"), None),
            P(("seq", "band")),
            P(("seq", "band"), None),
            P(("seq", "band")),
        ),
        check_vma=False,
    )
```

```python
import functools
import math

import jax
import jax.numpy as jnp
from jax import lax
from jax.experimental import pallas as pl
from jax.experimental.pallas import tpu as pltpu
from jax.sharding import PartitionSpec as P

D = 1024
HEADS = 16
HEAD_DIM = 64
SUBGRIDS = 8


EPSILON = 1e-05
NEGATIVE = -1e30


def prefix(part, axis, combine, identity):
    place = lax.axis_index(axis)
    gathered = lax.all_gather(part, axis)
    state = jnp.zeros_like(part) + jnp.asarray(identity, part.dtype)

    def one(lap, state):
        return combine(state, lax.dynamic_index_in_dim(gathered, lap, 0, False))

    return lax.fori_loop(0, place, one, state)


def layer_norm(values_in, norm_gain, norm_shift):
    average = jnp.mean(values_in, axis=-1, keepdims=True)
    centered = values_in - average
    variance = jnp.mean(centered * centered, axis=-1, keepdims=True)
    return centered * lax.rsqrt(variance + EPSILON) * norm_gain + norm_shift


def gelu_exact(values_in):
    return jax.nn.gelu(values_in, approximate=False)


def add_counts(first_part, second_part):
    return first_part + second_part


def block_scores(query_part, key_part, seg_part, code_part, scale_factor):
    scores = (
        jnp.einsum("qhe,khe->hqk", query_part, key_part, preferred_element_type=jnp.float32)
        * scale_factor
    )
    allowed = (seg_part[:, None] == code_part[None, :])[None]
    return (jnp.where(allowed, scores, NEGATIVE), allowed)


def split_blocks(array_in, block_rows):
    return array_in.reshape((array_in.shape[0] // block_rows, block_rows) + array_in.shape[1:])


def shards(
    block_in,
    attention_norm_gain,
    attention_norm_bias,
    query_key_value,
    query_bias,
    value_bias,
    output_weight,
    output_bias,
    mlp_norm_gain,
    mlp_norm_bias,
    mlp_in_weight,
    mlp_in_bias,
    mlp_out_weight,
    mlp_out_bias,
    cotangent,
    segment_ids,
    sub_lengths,
):
    float_type = jnp.float32
    half_type = jnp.bfloat16
    rows_local = block_in.shape[1]
    seq_length = rows_local * lax.axis_size("band")
    scale_factor = HEAD_DIM ** (-0.5)
    block_rows = math.gcd(seq_length, 1024)
    seg_local = segment_ids[0]
    labels = jnp.arange(SUBGRIDS, dtype=jnp.int32)
    onehot_ids = (seg_local[:, None] == labels[None, :]).astype(jnp.int32)
    earlier_counts = prefix(
        jnp.sum(onehot_ids, axis=0), "band", add_counts, jnp.zeros((SUBGRIDS,), jnp.int32)
    )
    slots = jnp.arange(rows_local)
    earlier = (slots[None, :] < slots[:, None]).astype(float_type)
    before = (
        jnp.dot(earlier, onehot_ids.astype(float_type), precision=lax.Precision.HIGHEST).astype(
            jnp.int32
        )
        + earlier_counts[None, :]
    )
    patch_rank = jnp.sum(before * onehot_ids, axis=1)
    limits = jnp.sum(onehot_ids * sub_lengths[0][None, :], axis=1)
    realness = patch_rank < limits
    key_codes = jnp.where(realness, seg_local, -1)
    gathered = (
        lax.all_gather(attention_norm_gain, ("seq", "band"), axis=0, tiled=True),
        lax.all_gather(attention_norm_bias, ("seq", "band"), axis=0, tiled=True),
        lax.all_gather(query_key_value, ("seq", "band"), axis=0, tiled=True),
        lax.all_gather(query_bias, ("seq", "band"), axis=0, tiled=True),
        lax.all_gather(value_bias, ("seq", "band"), axis=0, tiled=True),
        lax.all_gather(output_weight, ("seq", "band"), axis=0, tiled=True),
        lax.all_gather(output_bias, ("seq", "band"), axis=0, tiled=True),
        lax.all_gather(mlp_norm_gain, ("seq", "band"), axis=0, tiled=True),
        lax.all_gather(mlp_norm_bias, ("seq", "band"), axis=0, tiled=True),
        lax.all_gather(mlp_in_weight, ("seq", "band"), axis=0, tiled=True),
        lax.all_gather(mlp_in_bias, ("seq", "band"), axis=0, tiled=True),
        lax.all_gather(mlp_out_weight, ("seq", "band"), axis=0, tiled=True),
        lax.all_gather(mlp_out_bias, ("seq", "band"), axis=0, tiled=True),
    )
    (
        gain_one,
        shift_one,
        joint_weight,
        bias_query,
        bias_value,
        proj_weight,
        proj_bias,
        gain_two,
        shift_two,
        up_weight,
        up_bias,
        down_weight,
        down_bias,
    ) = gathered
    inputs = block_in[0].astype(float_type)
    normed_float, norm_pull_one = jax.vjp(
        layer_norm, inputs, gain_one.astype(float_type), shift_one.astype(float_type)
    )
    normed_one = normed_float.astype(half_type)
    mixed_all = jnp.dot(normed_one, joint_weight, preferred_element_type=float_type)
    queries = (mixed_all[:, :D] + bias_query.astype(float_type)).astype(half_type)
    keys_local = mixed_all[:, D : 2 * D].astype(half_type)
    values_local = (mixed_all[:, 2 * D :] + bias_value.astype(float_type)).astype(half_type)
    keys_seq, values_seq, codes_seq = (
        lax.all_gather(keys_local, "band", axis=0, tiled=True),
        lax.all_gather(values_local, "band", axis=0, tiled=True),
        lax.all_gather(key_codes, "band", axis=0, tiled=True),
    )
    query_heads = queries.reshape(rows_local, HEADS, HEAD_DIM)
    key_blocks = split_blocks(keys_seq.reshape(seq_length, HEADS, HEAD_DIM), block_rows)
    value_blocks = split_blocks(values_seq.reshape(seq_length, HEADS, HEAD_DIM), block_rows)
    code_blocks = split_blocks(codes_seq, block_rows)

    def stats_step(running, block_items):
        top_now, total_now = running
        key_part, code_part = block_items
        scores, allowed = block_scores(query_heads, key_part, seg_local, code_part, scale_factor)
        top_new = jnp.maximum(top_now, jnp.max(scores, axis=-1))
        exp_terms = jnp.where(allowed, jnp.exp(scores - top_new[..., None]), 0.0)
        return (
            (top_new, total_now * jnp.exp(top_now - top_new) + jnp.sum(exp_terms, axis=-1)),
            None,
        )

    start_stats = (
        jnp.full((HEADS, rows_local), NEGATIVE, float_type),
        jnp.zeros((HEADS, rows_local), float_type),
    )
    (top_final, total_final), unused_stats = lax.scan(
        stats_step, start_stats, (key_blocks, code_blocks)
    )
    log_total = top_final + jnp.log(total_final)

    def value_step(accum_out, block_items):
        key_part, value_part, code_part = block_items
        scores, allowed = block_scores(query_heads, key_part, seg_local, code_part, scale_factor)
        soft_probs = jnp.where(allowed, jnp.exp(scores - log_total[..., None]), 0.0).astype(
            half_type
        )
        return (
            accum_out
            + jnp.einsum("hqk,khe->qhe", soft_probs, value_part, preferred_element_type=float_type),
            None,
        )

    attended, unused_values = lax.scan(
        value_step,
        jnp.zeros((rows_local, HEADS, HEAD_DIM), float_type),
        (key_blocks, value_blocks, code_blocks),
    )
    attended_low = attended.reshape(rows_local, D).astype(half_type)
    residual = (
        inputs
        + jnp.dot(attended_low, proj_weight, preferred_element_type=float_type)
        + proj_bias.astype(float_type)
    )
    normed_float_two, norm_pull_two = jax.vjp(
        layer_norm, residual, gain_two.astype(float_type), shift_two.astype(float_type)
    )
    normed_two = normed_float_two.astype(half_type)
    hidden_pre = jnp.dot(normed_two, up_weight, preferred_element_type=float_type) + up_bias.astype(
        float_type
    )
    hidden_value, gelu_pull = jax.vjp(gelu_exact, hidden_pre)
    hidden_act = hidden_value.astype(half_type)
    block_result = (
        residual
        + jnp.dot(hidden_act, down_weight, preferred_element_type=float_type)
        + down_bias.astype(float_type)
    )
    gathered_back = (
        lax.all_gather(attention_norm_gain, ("seq", "band"), axis=0, tiled=True),
        lax.all_gather(attention_norm_bias, ("seq", "band"), axis=0, tiled=True),
        lax.all_gather(query_key_value, ("seq", "band"), axis=0, tiled=True),
        lax.all_gather(query_bias, ("seq", "band"), axis=0, tiled=True),
        lax.all_gather(value_bias, ("seq", "band"), axis=0, tiled=True),
        lax.all_gather(output_weight, ("seq", "band"), axis=0, tiled=True),
        lax.all_gather(output_bias, ("seq", "band"), axis=0, tiled=True),
        lax.all_gather(mlp_norm_gain, ("seq", "band"), axis=0, tiled=True),
        lax.all_gather(mlp_norm_bias, ("seq", "band"), axis=0, tiled=True),
        lax.all_gather(mlp_in_weight, ("seq", "band"), axis=0, tiled=True),
        lax.all_gather(mlp_in_bias, ("seq", "band"), axis=0, tiled=True),
        lax.all_gather(mlp_out_weight, ("seq", "band"), axis=0, tiled=True),
        lax.all_gather(mlp_out_bias, ("seq", "band"), axis=0, tiled=True),
    )
    joint_back = gathered_back[2]
    proj_back = gathered_back[5]
    up_back = gathered_back[9]
    down_back = gathered_back[11]
    grad_out = cotangent[0].astype(float_type) * realness[:, None].astype(float_type)
    grad_mlp = grad_out.astype(half_type)
    grad_down_weight = jnp.einsum(
        "rf,rd->fd", hidden_act, grad_mlp, preferred_element_type=float_type
    )
    grad_down_bias = jnp.sum(grad_mlp.astype(float_type), axis=0)
    grad_act = jnp.einsum("rd,fd->rf", grad_mlp, down_back, preferred_element_type=float_type)
    grad_pre = gelu_pull(grad_act)[0].astype(half_type)
    grad_up_weight = jnp.einsum(
        "rd,rf->df", normed_two, grad_pre, preferred_element_type=float_type
    )
    grad_up_bias = jnp.sum(grad_pre.astype(float_type), axis=0)
    grad_normed_two = jnp.einsum("rf,df->rd", grad_pre, up_back, preferred_element_type=float_type)
    grad_resid_part, grad_gain_two, grad_shift_two = norm_pull_two(grad_normed_two)
    grad_residual = grad_out + grad_resid_part
    grad_branch = grad_residual.astype(half_type)
    grad_proj_weight = jnp.einsum(
        "rd,re->de", attended_low, grad_branch, preferred_element_type=float_type
    )
    grad_proj_bias = jnp.sum(grad_branch.astype(float_type), axis=0)
    grad_attended = jnp.einsum(
        "re,de->rd", grad_branch, proj_back, preferred_element_type=float_type
    ).astype(half_type)
    grad_heads = grad_attended.reshape(rows_local, HEADS, HEAD_DIM)
    row_delta = jnp.sum(grad_heads.astype(float_type) * attended, axis=-1).T
    keys_back = lax.all_gather(keys_local, "band", axis=0, tiled=True)
    values_back = lax.all_gather(values_local, "band", axis=0, tiled=True)
    codes_back = lax.all_gather(key_codes, "band", axis=0, tiled=True)
    key_back_blocks = split_blocks(keys_back.reshape(seq_length, HEADS, HEAD_DIM), block_rows)
    value_back_blocks = split_blocks(values_back.reshape(seq_length, HEADS, HEAD_DIM), block_rows)
    code_back_blocks = split_blocks(codes_back, block_rows)

    def key_step(query_accum, block_items):
        key_part, value_part, code_part = block_items
        scores, allowed = block_scores(query_heads, key_part, seg_local, code_part, scale_factor)
        soft_probs = jnp.where(allowed, jnp.exp(scores - log_total[..., None]), 0.0)
        grad_probs = jnp.einsum(
            "qhe,khe->hqk", grad_heads, value_part, preferred_element_type=float_type
        )
        grad_scores = (soft_probs * (grad_probs - row_delta[..., None])).astype(half_type)
        query_accum = query_accum + jnp.einsum(
            "hqk,khe->qhe", grad_scores, key_part, preferred_element_type=float_type
        )
        return (query_accum, None)

    query_total, joined_blocks = lax.scan(
        key_step,
        jnp.zeros((rows_local, HEADS, HEAD_DIM), float_type),
        (key_back_blocks, value_back_blocks, code_back_blocks),
    )
    grad_query = (query_total * scale_factor).reshape(rows_local, D)
    query_seq = lax.all_gather(queries, "band", axis=0, tiled=True)
    grad_seq = lax.all_gather(grad_attended, "band", axis=0, tiled=True)
    total_seq = lax.all_gather(log_total, "band", axis=1, tiled=True)
    delta_seq = lax.all_gather(row_delta, "band", axis=1, tiled=True)
    seg_seq = lax.all_gather(seg_local, "band", axis=0, tiled=True)
    block_count = seq_length // block_rows
    key_heads_local = keys_local.reshape(rows_local, HEADS, HEAD_DIM)
    value_heads_local = values_local.reshape(rows_local, HEADS, HEAD_DIM)

    def query_step(running, block_items):
        key_accum, value_accum = running
        query_part, grad_part, total_part, delta_part, seg_part = block_items
        scores, allowed = block_scores(
            query_part, key_heads_local, seg_part, key_codes, scale_factor
        )
        soft_probs = jnp.where(allowed, jnp.exp(scores - total_part[..., None]), 0.0)
        grad_probs = jnp.einsum(
            "qhe,khe->hqk", grad_part, value_heads_local, preferred_element_type=float_type
        )
        grad_scores = (soft_probs * (grad_probs - delta_part[..., None])).astype(half_type)
        key_accum = key_accum + jnp.einsum(
            "hqk,qhe->khe", grad_scores, query_part, preferred_element_type=float_type
        )
        value_accum = value_accum + jnp.einsum(
            "hqk,qhe->khe",
            soft_probs.astype(half_type),
            grad_part,
            preferred_element_type=float_type,
        )
        return ((key_accum, value_accum), None)

    zero_heads = jnp.zeros((rows_local, HEADS, HEAD_DIM), float_type)
    (key_total, value_total), query_blocks = lax.scan(
        query_step,
        (zero_heads, zero_heads),
        (
            split_blocks(query_seq.reshape(seq_length, HEADS, HEAD_DIM), block_rows),
            split_blocks(grad_seq.reshape(seq_length, HEADS, HEAD_DIM), block_rows),
            total_seq.reshape(HEADS, block_count, block_rows).transpose(1, 0, 2),
            delta_seq.reshape(HEADS, block_count, block_rows).transpose(1, 0, 2),
            split_blocks(seg_seq, block_rows),
        ),
    )
    grad_key = (key_total * scale_factor).reshape(rows_local, D)
    grad_value = value_total.reshape(rows_local, D)
    grad_query_low = grad_query.astype(half_type)
    grad_value_low = grad_value.astype(half_type)
    grad_mixed = jnp.concatenate(
        [grad_query_low, grad_key.astype(half_type), grad_value_low], axis=1
    )
    grad_joint_weight = jnp.einsum(
        "rd,rm->dm", normed_one, grad_mixed, preferred_element_type=float_type
    )
    grad_bias_query = jnp.sum(grad_query_low.astype(float_type), axis=0)
    grad_bias_value = jnp.sum(grad_value_low.astype(float_type), axis=0)
    grad_normed_one = jnp.einsum(
        "rm,dm->rd", grad_mixed, joint_back, preferred_element_type=float_type
    )
    grad_input_part, grad_gain_one, grad_shift_one = norm_pull_one(grad_normed_one)
    input_grad = (grad_residual + grad_input_part).astype(half_type)
    shard_grads = (
        lax.psum_scatter(grad_gain_one, ("seq", "band"), scatter_dimension=0, tiled=True),
        lax.psum_scatter(grad_shift_one, ("seq", "band"), scatter_dimension=0, tiled=True),
        lax.psum_scatter(grad_joint_weight, ("seq", "band"), scatter_dimension=0, tiled=True),
        lax.psum_scatter(grad_bias_query, ("seq", "band"), scatter_dimension=0, tiled=True),
        lax.psum_scatter(grad_bias_value, ("seq", "band"), scatter_dimension=0, tiled=True),
        lax.psum_scatter(grad_proj_weight, ("seq", "band"), scatter_dimension=0, tiled=True),
        lax.psum_scatter(grad_proj_bias, ("seq", "band"), scatter_dimension=0, tiled=True),
        lax.psum_scatter(grad_gain_two, ("seq", "band"), scatter_dimension=0, tiled=True),
        lax.psum_scatter(grad_shift_two, ("seq", "band"), scatter_dimension=0, tiled=True),
        lax.psum_scatter(grad_up_weight, ("seq", "band"), scatter_dimension=0, tiled=True),
        lax.psum_scatter(grad_up_bias, ("seq", "band"), scatter_dimension=0, tiled=True),
        lax.psum_scatter(grad_down_weight, ("seq", "band"), scatter_dimension=0, tiled=True),
        lax.psum_scatter(grad_down_bias, ("seq", "band"), scatter_dimension=0, tiled=True),
    )
    return (
        block_result.astype(half_type)[None],
        input_grad[None],
        shard_grads[0],
        shard_grads[1],
        shard_grads[2],
        shard_grads[3],
        shard_grads[4],
        shard_grads[5],
        shard_grads[6],
        shard_grads[7],
        shard_grads[8],
        shard_grads[9],
        shard_grads[10],
        shard_grads[11],
        shard_grads[12],
    )


F32 = jnp.float32
BF16 = jnp.bfloat16
MESH_ID = pl.DeviceIdType.MESH
ROWS = 128
LANES = 128
COPIES = 240


def dot(lhs, rhs):
    return jnp.dot(lhs, rhs, preferred_element_type=F32)


def dot_nt(lhs, rhs):
    return lax.dot_general(lhs, rhs, (((1,), (1,)), ((), ())), preferred_element_type=F32)


def dot_tn(lhs, rhs):
    return lax.dot_general(lhs, rhs, (((0,), (0,)), ((), ())), preferred_element_type=F32)


def pair_of(jj):
    return (jj // 4) * 4 + (jj % 2) * 2 + (jj // 2) % 2


def flat_column(jj, ch):
    return (ch // 2) * 16 + (jj // 4) * 8 + (ch % 2) * 4 + jj % 4


def shard_place(i):
    return (i // 16) * 2 + (i // 4) % 2, ((i // 8) % 2) * 4 + i % 4


def fused_kernel(copies, *refs):
    (
        xin, cin, seg_in, len_in, wq, wo, wi, wd,
        p0, p1, p2, p3, p4, p5, p6, p7, pb,
        out_block, out_input, out_q, out_o, out_i, out_d, out_small,
        X, N0, N1, N2, GM, GB, SGI, SG, PK, SP, FULL, PV,
        WQI, WSQ, RQ, WQ, WO, WII, WSI, RI, WI, WD,
        QS, KK, VV, QT, KT, VT, CODE, SC, PT, INV, OT, OL,
        PA, CS, PB, CSB, SB, RV, XO, N2F, HAT, HA, GP, GA,
        DK, DV, DQ, GMX,
        GQ, GI, GD, XQ, XI, XD, HQ, HI, HD, ZQ, ZI, ZD, TQ, TI, TD,
        GO, GOF, XGO, TGO,
        VG, VR, SL, SLR, SLF, RS_, BG, BO, BI,
        ssem, rsem, lsem,
    ) = refs
    s = lax.axis_index("seq")
    b = lax.axis_index("band")
    x, c = lax.div(s, 2), lax.rem(s, 2)
    zh, l = lax.div(b, 4), lax.rem(b, 4)
    zl, y = lax.div(l, 2), lax.rem(l, 2)
    t, j = x * 2 + zh, c * 4 + l

    def flip(v, d):
        return 1 - v if d else v

    def flip_l(d):
        return flip(zl, d // 2) * 2 + flip(y, d % 2)

    def dev(dx=0, dc=0, dzh=0, dl=0):
        return (flip(x, dx) * 2 + flip(c, dc), flip(zh, dzh) * 4 + flip_l(dl))

    roles = (l, flip_l(2), flip_l(1), flip_l(3))

    counter = [0]
    pending = []

    def slots(n=1):
        first = counter[0]
        counter[0] += n
        assert counter[0] <= copies
        return first

    def send(src, dst, device, sem):
        copy = pltpu.make_async_remote_copy(
            src_ref=src, dst_ref=dst, send_sem=ssem.at[sem], recv_sem=rsem.at[sem],
            device_id=device, device_id_type=MESH_ID)
        copy.start()
        return copy

    def push(src, dst, device, sem):
        copy = send(src, dst, device, sem)
        pending.append(copy)
        return copy

    def arrive(dst, sem):
        pltpu.make_async_remote_copy(
            src_ref=dst, dst_ref=dst, send_sem=ssem.at[sem], recv_sem=rsem.at[sem],
            device_id=dev(dc=1), device_id_type=MESH_ID).wait_recv()

    def left(src, sem):
        pltpu.make_async_remote_copy(
            src_ref=src, dst_ref=src, send_sem=ssem.at[sem], recv_sem=rsem.at[sem],
            device_id=dev(dc=1), device_id_type=MESH_ID).wait_send()

    def move(src, dst, sem):
        return pltpu.make_async_copy(src, dst, lsem.at[sem])

    group_masks = [(dc, dl) for dl in (3, 1, 2, 0) for dc in (0, 1) if (dc, dl) != (0, 0)]
    line_masks = [(dx, dc, dzh) for dx in (1, 0) for dc in (0, 1) for dzh in (1, 0) if dx + dc + dzh]

    def group(dc, dl):
        return flip(c, dc) * 4 + flip_l(dl)

    native = c == zh
    foreign = jnp.logical_not(native)
    partner = dev(dc=1, dzh=1)
    their_block = (1 - c) * 4 + l

    barrier = pltpu.get_barrier_semaphore()
    peers = [dict(dc=dc, dl=dl) for dc, dl in group_masks]
    peers += [dict(dx=a, dc=e, dzh=f) for a, e, f in line_masks if (a, e, f) != (0, 1, 0)]
    for peer in peers:
        pl.semaphore_signal(barrier, inc=1, device_id=dev(**peer), device_id_type=MESH_ID)
    get_q, get_i, get_d = move(wq, WQI, 0), move(wi, WII, 1), move(wd, WD.at[t], 2)
    get_x, get_c = move(xin.at[0], X.at[j], 3), move(cin.at[0], GM.at[j], 4)
    get_q.start()
    get_i.start()
    get_d.start()

    @pl.when(native)
    def _():
        get_x.start()
        get_c.start()

    lane_group = lax.broadcasted_iota(jnp.int32, (1, LANES), 1) // 32
    PK[...] = jnp.zeros_like(PK)
    for p, ref in enumerate((p0, p1, p2, p3, p4, p5, p6, p7)):
        value = ref[...].astype(F32).reshape(1, 32)
        PK[p : p + 1] = jnp.where(lane_group == l, jnp.concatenate([value] * 4, axis=1), 0.0)
    own_bias = pb[...].astype(F32).reshape(1, LANES)
    for r in range(4):
        PK[8 + r : 9 + r] = jnp.where(l == r, own_bias, jnp.zeros_like(own_bias))
    SGI[...] = jnp.zeros_like(SGI)
    SGI[0:1] = seg_in[...].astype(F32)
    SGI[1:2, 0:SUBGRIDS] = len_in[...].astype(F32)
    get_q.wait()
    for jj in range(8):
        for ch in range(3):
            WSQ[jj, ch] = WQI[:, ch * D + pair_of(jj) * LANES : ch * D + (pair_of(jj) + 1) * LANES]
    for ch in range(3):
        RQ[ch, t, j] = WSQ[j, ch]
    pl.semaphore_wait(barrier, len(peers))

    sem_px, sem_pc, sem_ps = slots(), slots(), slots()
    sem_wq, sem_s1 = slots(8), slots(4)
    for dl in (1, 2, 3):
        push(PK, SP.at[dl], dev(dl=dl), sem_s1 + dl)

    @pl.when(native)
    def _():
        SG[j] = SGI[...]

    @pl.when(foreign)
    def _():
        send(SGI, SG.at[their_block], partner, sem_ps)
        send(xin.at[0], X.at[their_block], partner, sem_px)

    for dc, dl in group_masks:
        push(WSQ.at[group(dc, dl)], RQ.at[:, t, j], dev(dc=dc, dl=dl), sem_wq + dc * 4 + dl)

    class Gather:
        def __init__(self, buf):
            self.buf, self.far, self.near = buf, slots(4), slots(4)

        def start(self):
            block = self.buf.at[j]
            copies_out = [
                send(block, block, (s, zh * 4 + roles[1]), self.far + 1),
                send(block, block, (s, zh * 4 + roles[2]), self.far + 2),
                send(block, block, dev(dc=1), self.near),
            ]
            return copies_out

        def begin(self):
            pending.extend(self.start())

        def forward(self, k):
            block = self.buf.at[c * 4 + roles[k]]
            arrive(block, self.far + k)
            if k == 1:
                push(block, block, (s, zh * 4 + roles[2]), self.far + 3)
            push(block, block, dev(dc=1), self.near + k)

        def sibling(self, k):
            arrive(self.buf.at[(1 - c) * 4 + roles[k]], self.near + k)

    gather_x = Gather(X)
    gather_g = Gather(GM)

    @pl.when(native)
    def _():
        get_x.wait()
        gather_x.start()

    sem_wo, sem_wt = slots(4), slots(4)
    own_pair = c * 4 + y * 2 + zl
    pair_l = zh * 2 + c
    to_self = jnp.logical_and(x == c, l == pair_l)
    is_root = jnp.logical_and(x == c, zh == zl)
    root_mask = jnp.abs(x - c) * 2 + jnp.abs(zh - zl)
    get_o = move(wo, WO.at[l], 5)

    @pl.when(to_self)
    def _():
        get_o.start()

    @pl.when(jnp.logical_not(to_self))
    def _():
        send(wo, WO.at[l], (x * 2 + x, zh * 4 + pair_l), sem_wo + l)

    q_own = x * 4 + c * 2 + zh
    slab = PK[...]
    for dl in (1, 2, 3):
        arrive(SP.at[dl], sem_s1 + dl)
        slab += SP[dl]
    FULL[q_own] = slab
    sem_s2 = slots(8)
    for dx, dc, dzh in line_masks:
        push(FULL.at[q_own], FULL.at[q_own], dev(dx=dx, dc=dc, dzh=dzh), sem_s2 + dx * 4 + dc * 2 + dzh)

    class Spread:
        def __init__(self, buf):
            self.buf, self.sem = buf, slots(3)

        def start_z(self, keep=True):
            block = self.buf.at[t]
            copy = send(block, block, dev(dzh=1), self.sem)
            if keep:
                pending.append(copy)

        def start_x(self):
            block = self.buf.at[t]
            push(block, block, dev(dx=1), self.sem + 1)

        def sent_z(self):
            left(self.buf.at[t], self.sem)

        def start(self):
            self.start_z()
            self.start_x()

        def forward(self):
            block = self.buf.at[x * 2 + 1 - zh]
            arrive(block, self.sem)
            push(block, block, dev(dx=1), self.sem + 2)

        def finish(self):
            arrive(self.buf.at[(1 - x) * 2 + zh], self.sem + 1)
            arrive(self.buf.at[(1 - x) * 2 + 1 - zh], self.sem + 2)

    spread_q = [Spread(RQ.at[ch]) for ch in range(3)]
    for dc, dl in group_masks:
        arrive(RQ.at[:, t, group(dc, dl)], sem_wq + dc * 4 + dl)
    for ch in range(3):
        spread_q[ch].start()

    sem_sg = slots(8)

    @pl.when(foreign)
    def _():
        arrive(SG.at[j], sem_ps)

    for dc, dl in group_masks:
        push(SG.at[j], SG.at[j], dev(dc=dc, dl=dl), sem_sg + dc * 4 + dl)
    @pl.when(foreign)
    def _():
        arrive(X.at[j], sem_px)
        gather_x.start()

    for slot in range(4):
        @pl.when(jnp.logical_and(is_root, jnp.logical_not(jnp.logical_and(y == c, l == slot))))
        def _():
            arrive(WO.at[slot], sem_wo + slot)

    @pl.when(to_self)
    def _():
        get_o.wait()

    @pl.when(is_root)
    def _():
        send(WO, WO, dev(dzh=1), sem_wt + 1)
        send(WO, WO, dev(dx=1), sem_wt + 2)


    @pl.when(foreign)
    def _():
        send(cin.at[0], GM.at[their_block], partner, sem_pc)

    for dx, dc, dzh in line_masks:
        arrive(FULL.at[flip(x, dx) * 4 + flip(c, dc) * 2 + flip(zh, dzh)], sem_s2 + dx * 4 + dc * 2 + dzh)
    for q in range(8):
        PV[:, q * LANES : (q + 1) * LANES] = FULL[q]
    gain1, shift1 = PV[0:1, :], PV[1:2, :]

    def norm_rows(value, gain, shift):
        average = jnp.mean(value, axis=-1, keepdims=True)
        centered = value - average
        root = lax.rsqrt(jnp.mean(centered * centered, axis=-1, keepdims=True) + EPSILON)
        normal = centered * root
        return normal, root, normal * gain + shift

    def norm_one(block):
        for r in range(2):
            rows = pl.ds(r * 64, 64)
            normal, _, value = norm_rows(X[block, rows].astype(F32), gain1, shift1)
            N0[block, rows] = normal.astype(BF16)
            N1[block, rows] = value.astype(BF16)

    norm_one(j)

    gather_x.sibling(0)
    norm_one((1 - c) * 4 + l)
    gather_x.forward(1)
    gather_x.forward(2)
    norm_one(c * 4 + roles[1])
    norm_one(c * 4 + roles[2])
    spread_q[0].forward()
    get_i.wait()
    for jj in range(8):
        for ch in range(4):
            flat = flat_column(jj, ch)
            WSI[jj, ch] = WII[:, flat * LANES : (flat + 1) * LANES]
    sem_wi = slots(8)
    for dc, dl in group_masks:
        push(WSI.at[group(dc, dl)], RI.at[t, j], dev(dc=dc, dl=dl), sem_wi + dc * 4 + dl)
    RI[t, j] = WSI[j]
    for k in (1, 2):
        gather_x.sibling(k)
    gather_x.forward(3)
    norm_one((1 - c) * 4 + roles[1])
    spread_q[1].forward()
    norm_one((1 - c) * 4 + roles[2])
    norm_one(c * 4 + roles[3])
    spread_q[2].forward()
    gather_x.sibling(3)
    norm_one((1 - c) * 4 + roles[3])

    get_d.wait()
    spread_i, spread_d = Spread(RI), Spread(WD)

    for dc, dl in group_masks:
        arrive(SG.at[group(dc, dl)], sem_sg + dc * 4 + dl)
    lens = SG[j, 1:2, :]
    row_ids = lax.broadcasted_iota(jnp.int32, (LANES, LANES), 0)
    lane_ids = lax.broadcasted_iota(jnp.int32, (LANES, LANES), 1)
    label_row = lane_ids.astype(F32)
    label_col = row_ids.astype(F32)
    earlier = (lane_ids < row_ids).astype(BF16)
    running = jnp.zeros((1, LANES), F32)
    for blk in range(8):
        onehot = (label_col == SG[blk, 0:1, :]).astype(F32).T
        before = dot(earlier, onehot.astype(BF16)) + running
        running = running + jnp.sum(onehot, axis=0, keepdims=True)
        rank = jnp.sum(before * onehot, axis=1, keepdims=True)
        limit = jnp.sum(onehot * lens, axis=1, keepdims=True)
        ident = jnp.sum(label_row * onehot, axis=1, keepdims=True)
        CODE[blk] = jnp.broadcast_to(jnp.where(rank < limit, ident, -1.0), (ROWS, LANES))

    @pl.when(native)
    def _():
        get_c.wait()

    @pl.when(foreign)
    def _():
        arrive(GM.at[j], sem_pc)

    is_real = CODE[j][:, 0:1] >= 0.0
    GM[j] = jnp.where(is_real, GM[j].astype(F32), 0.0).astype(BF16)
    gather_g.begin()

    @pl.when(jnp.logical_not(is_root))
    def _():
        arrive(WO, sem_wt + root_mask)

    @pl.when(root_mask == 1)
    def _():
        send(WO, WO, dev(dx=1), sem_wt + 3)

    for dc, dl in group_masks:
        arrive(RI.at[t, group(dc, dl)], sem_wi + dc * 4 + dl)
    spread_i.start_z()
    spread_i.start_x()
    spread_d.start_x()
    for ch in range(3):
        spread_q[ch].finish()
        for i in range(32):
            tt, jj = shard_place(i)
            WQ[i * 32 : (i + 1) * 32, ch * LANES : (ch + 1) * LANES] = RQ[ch, tt, jj]
    bias_q, bias_v = FULL[own_pair][2:3, :], FULL[own_pair][3:4, :]
    for k in range(4):
        rows = pl.ds(k * 256, 256)
        normed = N1[2 * k : 2 * k + 2].reshape(256, D)
        mixed = dot(normed, WQ[...])
        queries = (mixed[:, :LANES] + bias_q).astype(BF16).astype(F32) * (HEAD_DIM ** -0.5)
        keys = mixed[:, LANES : 2 * LANES]
        values = mixed[:, 2 * LANES :] + bias_v
        QS[rows] = queries.astype(BF16)
        KK[rows] = keys.astype(BF16)
        VV[rows] = values.astype(BF16)
        QT[:, rows] = queries.T.astype(BF16)
        KT[:, rows] = keys.T.astype(BF16)
        VT[:, rows] = values.T.astype(BF16)


    def pair_lanes(lp):
        return (pl.ds(pl.multiple_of(lp * LANES, LANES), LANES), pl.ds(pl.multiple_of(512 + lp * LANES, LANES), LANES))

    def cat_lanes(ref, lp):
        first, second = pair_lanes(lp)
        return jnp.concatenate([ref[:, first], ref[:, second]], axis=1)

    def cat_rows(ref, lp):
        return jnp.concatenate([ref[lp], ref[4 + lp]], axis=0)

    class Scatter:
        def __init__(self, part, chip, number, before=None, tree=True):
            self.part, self.chip, self.number, self.before, self.tree = part, chip, number, before, tree
            self.near, self.far = slots(4), slots(8)

        def emit(self, m, value):
            if self.before is not None:
                left(self.part.at[m, 1 - c], self.before.near + m)
            low = value.astype(BF16)
            self.part[m, 0] = low[:ROWS]
            self.part[m, 1] = low[ROWS:]
            send(self.part.at[m, 1 - c], SB.at[self.number, m], dev(dc=1), self.near + m)

        def pieces(self, m):
            if self.tree and m > 1:
                return ((pl.ds(0, 64), self.far + m), (pl.ds(64, 64), self.far + 4 + m))
            return ((pl.ds(0, ROWS), self.far + m),)

        def chip_left(self, m):
            for rows, sem in self.pieces(m):
                left(self.chip.at[m, rows], sem)

        def reduce(self, m):
            arrive(SB.at[self.number, m], self.near + m)
            if m == 0:
                return
            if self.before is not None:
                self.before.chip_left(m)
            for k, (rows, sem) in enumerate(self.pieces(m)):
                total = self.part[m, c, rows].astype(F32) + SB[self.number, m, rows].astype(F32)
                if self.tree and m == 2:
                    across = RV.at[self.number, 3, rows]
                    arrive(across, self.pieces(3)[k][1])
                    total += across[...].astype(F32)
                self.chip[m, rows] = total.astype(BF16)
                device = dev(dl=1) if self.tree and m == 3 else dev(dl=m)
                send(self.chip.at[m, rows], RV.at[self.number, m, rows], device, sem)

        def finish(self):
            for m in (1, 2) if self.tree else (1, 2, 3):
                for rows, sem in self.pieces(m):
                    arrive(RV.at[self.number, m, rows], sem)

        def rows(self, rows):
            total = self.part[0, c, rows].astype(F32) + SB[self.number, 0, rows].astype(F32)
            for m in (1, 2) if self.tree else (1, 2, 3):
                total += RV[self.number, m, rows].astype(F32)
            return total

        def close(self):
            for m in range(4):
                left(self.part.at[m, 1 - c], self.near + m)
                if m:
                    self.chip_left(m)

    head_rows = lax.broadcasted_iota(jnp.int32, (LANES, 256), 0)
    head_lanes = lax.broadcasted_iota(jnp.int32, (256, LANES), 1)

    def only_rows(value, h):
        return jnp.where((head_rows >= h * 64) & (head_rows < (h + 1) * 64), value, jnp.zeros_like(value))

    def only_lanes(value, h):
        return jnp.where((head_lanes >= h * 64) & (head_lanes < (h + 1) * 64), value, jnp.zeros_like(value))

    scatter_a = Scatter(PA, CS, 0)
    attend_order = (3, 1, 2, 0)
    for k, m in enumerate(attend_order):
        lp = flip_l(m)
        queries_t = cat_lanes(QT, lp)
        seg_q = jnp.concatenate([SG[lp, 0:1, :], SG[4 + lp, 0:1, :]], axis=1)
        for h in range(2):
            masked_t = only_rows(queries_t.astype(F32), h).astype(BF16)
            top = jnp.full((8, 256), NEGATIVE, F32)
            for i in range(8):
                rows = pl.ds(i * ROWS, ROWS)
                value = dot(KK[rows], masked_t)
                code = CODE[i]
                allowed = jnp.concatenate([code, code], axis=1) == seg_q
                value = jnp.where(allowed, value, NEGATIVE)
                SC[h, rows] = value
                top = jnp.maximum(top, jnp.max(value.reshape(16, 8, 256), axis=0))
            top = jnp.max(top, axis=0, keepdims=True)
            total = jnp.zeros((8, 256), F32)
            for i in range(8):
                rows = pl.ds(i * ROWS, ROWS)
                value = jnp.exp(SC[h, rows] - top)
                PT[m, h, rows] = value.astype(BF16)
                total = total + jnp.sum(value.reshape(16, 8, 256), axis=0)
            inverse = 1.0 / jnp.sum(total, axis=0, keepdims=True)
            INV[m, h] = jnp.broadcast_to(inverse, (8, 256))
            OT[m, h * 64 : (h + 1) * 64] = dot(VT[h * 64 : (h + 1) * 64, :], PT[m, h]) * inverse
            if k and h == 0:
                scatter_a.reduce(attend_order[k - 1])
            if k == 1 and h == 1:
                spread_d.start_z()
            if k == 2 and h == 0:
                gather_g.forward(2)
            if k == 3 and h == 1:
                gather_g.forward(1)
        joined = OT[m]
        OL[m] = joined.astype(BF16)
        scatter_a.emit(m, dot(joined.T.astype(BF16), WO[...].reshape(LANES, D)))
    spread_i.forward()
    scatter_a.reduce(0)
    scatter_a.finish()

    gain2, shift2, bias_o = PV[5:6, :], PV[6:7, :], PV[4:5, :]
    for r in range(4):
        rows = pl.ds(r * 32, 32)
        residual = X[j, rows].astype(F32) + scatter_a.rows(rows) + bias_o
        XO[rows] = residual
        normal, root, value = norm_rows(residual, gain2, shift2)
        N2F[rows] = normal
        RS_[rows] = jnp.broadcast_to(root, (32, LANES))
        N2[j, rows] = value.astype(BF16)
    gather_n = Gather(N2)
    gather_n.begin()

    spread_i.finish()
    for i in range(32):
        tt, jj = shard_place(i)
        for ch in range(4):
            WI[i * 32 : (i + 1) * 32, ch * LANES : (ch + 1) * LANES] = RI[tt, jj, ch]
    pick = lax.broadcasted_iota(jnp.int32, (16, LANES), 0) == 8 + l
    bias_in = jnp.concatenate(
        [
            jnp.sum(jnp.where(pick, FULL[(ch // 2) * 4 + c * 2 + ch % 2], 0.0), axis=0, keepdims=True)
            for ch in range(4)
        ],
        axis=1,
    )
    scatter_m = Scatter(PA, CS, 1, scatter_a, tree=False)
    scatter_b = Scatter(PB, CSB, 2)
    BG[0:1] = jnp.zeros((1, 512), F32)

    def hidden_part(m):
        lp = flip_l(m)
        first, second = pair_lanes(lp)
        hidden = dot(cat_rows(N2, lp), WI[...]) + bias_in
        phi_cap = 0.5 * (1.0 + lax.erf(hidden * 0.7071067811865476))
        phi = jnp.exp(-0.5 * hidden * hidden) * 0.3989422804014327
        act = hidden * phi_cap
        GA[m] = phi_cap + hidden * phi
        HA[m] = act.astype(BF16)
        act_t = act.T.astype(BF16)
        HAT[:, first] = act_t[:, :ROWS]
        HAT[:, second] = act_t[:, ROWS:]

    def hidden_back(m):
        lp = flip_l(m)
        grad_act = dot_nt(cat_rows(GM, lp), WD[...].reshape(512, D))
        grad_pre = (grad_act * GA[m]).astype(BF16)
        GP[lp] = grad_pre[:ROWS]
        GP[4 + lp] = grad_pre[ROWS:]
        BG[0:1] += jnp.sum(grad_pre.astype(F32), axis=0, keepdims=True)
        scatter_m.emit(m, dot_nt(grad_pre, WI[...]))

    gather_n.sibling(0)
    hidden_part(0)
    spread_d.forward()
    gather_n.forward(2)
    gather_n.forward(1)
    gather_g.forward(3)
    gather_g.sibling(0)
    spread_d.finish()
    hidden_back(0)
    gather_n.sibling(2)
    hidden_part(1)
    gather_g.sibling(2)
    hidden_back(1)
    scatter_m.reduce(0)
    gather_n.sibling(1)
    hidden_part(2)
    gather_g.sibling(1)
    hidden_back(2)
    gather_n.forward(3)
    scatter_m.reduce(1)
    gather_n.sibling(3)
    hidden_part(3)
    gather_g.sibling(3)
    scatter_m.reduce(2)
    hidden_back(3)
    scatter_m.reduce(3)

    class Total:
        def __init__(self, part, from_x, middle, from_z):
            self.part, self.from_x, self.middle, self.from_z = part, from_x, middle, from_z
            self.sem = slots(3)

        def start_cross(self):
            push(self.part.at[(1 - x) * 2 + 1 - zh], self.from_x.at[1 - zh], dev(dx=1), self.sem)

        def start_keep(self):
            push(self.part.at[(1 - x) * 2 + zh], self.from_x.at[zh], dev(dx=1), self.sem + 2)

        def second(self):
            arrive(self.from_x.at[1 - zh], self.sem)
            self.middle[...] = (
                self.part[x * 2 + 1 - zh].astype(F32) + self.from_x[1 - zh].astype(F32)
            ).astype(BF16)
            push(self.middle, self.from_z, dev(dzh=1), self.sem + 1)

        def result(self):
            arrive(self.from_x.at[zh], self.sem + 2)
            arrive(self.from_z, self.sem + 1)
            return self.part[t].astype(F32) + self.from_x[zh].astype(F32) + self.from_z[...].astype(F32)

    total_d = Total(GD, XD, HD, ZD)
    total_i = Total(GI, XI, HI, ZI)
    total_q = [Total(GQ.at[ch], XQ.at[ch], HQ.at[ch], ZQ.at[ch]) for ch in range(3)]
    for ch in range(4):
        GD[ch] = dot(HAT[ch * LANES : (ch + 1) * LANES, :], GM[...].reshape(8 * ROWS, D)).astype(BF16)
    total_d.start_cross()
    all_pre = GP[...].reshape(8 * ROWS, 512)
    for blk in range(8):
        product = dot_tn(N2[:, :, blk * LANES : (blk + 1) * LANES].reshape(8 * ROWS, LANES), all_pre).astype(BF16)
        for r in range(4):
            tt, jj = shard_place(blk * 4 + r)
            for ch in range(4):
                GI[tt, jj, ch] = product[r * 32 : (r + 1) * 32, ch * LANES : (ch + 1) * LANES]
    total_i.start_cross()
    total_d.start_keep()
    total_i.start_keep()

    def norm_back(grad, normal, root, gain):
        scaled = grad * gain
        return root * (scaled - jnp.mean(scaled, axis=-1, keepdims=True)
                       - normal * jnp.mean(scaled * normal, axis=-1, keepdims=True))

    def forward_out(m):
        scatter_b.emit(m, dot(HA[m], WD[...].reshape(512, D)))

    for m in attend_order:
        forward_out(m)
    scatter_m.finish()
    sums = [jnp.zeros((1, D), F32) for _ in range(4)]
    for r in range(4):
        rows = pl.ds(r * 32, 32)
        grad = scatter_m.rows(rows)
        normal = N2F[rows]
        top_grad = GM[j, rows].astype(F32)
        grad_residual = top_grad + norm_back(grad, normal, RS_[rows][:, 0:1], gain2)
        low = grad_residual.astype(BF16)
        GB[j, rows] = low
        N2F[rows] = grad_residual
        for i, value in enumerate((grad * normal, grad, low.astype(F32), top_grad)):
            sums[i] += jnp.sum(value, axis=0, keepdims=True)
    vectors = {5: sums[0], 6: sums[1], 4: sums[2], 7: sums[3]}
    gather_b = Gather(GB)
    gather_b.begin()

    DK[...] = jnp.zeros_like(DK)
    DV[...] = jnp.zeros_like(DV)
    GOF[...] = jnp.zeros_like(GOF)

    def attend_back(m):
        lp = flip_l(m)
        first, second = pair_lanes(lp)
        branch = cat_rows(GB, lp)
        grad_att = dot_nt(branch, WO[...].reshape(LANES, D)).astype(BF16).astype(F32)
        GOF[...] += dot(OL[m], branch)
        grad_att_t = grad_att.T
        both = grad_att_t * OT[m]
        queries = jnp.concatenate([QS[first], QS[second]], axis=0).astype(F32)
        for h in range(2):
            inverse = INV[m, h][0:1]
            delta = jnp.sum(both[h * 64 : (h + 1) * 64], axis=0, keepdims=True) * inverse
            scaled_t = only_rows(grad_att_t * inverse, h)
            scaled_low_t = scaled_t.astype(BF16)
            scaled_low = scaled_t.T.astype(BF16)
            queries_h = only_lanes(queries, h).astype(BF16)
            for i in range(8):
                rows = pl.ds(i * ROWS, ROWS)
                probs = PT[m, h, rows]
                value = dot(VV[rows], scaled_low_t)
                grad_scores = (probs.astype(F32) * (value - delta)).astype(BF16)
                DV[rows] += dot(probs, scaled_low)
                DK[rows] += dot(grad_scores, queries_h)
                PT[m, h, rows] = grad_scores
            DQ[h * 64 : (h + 1) * 64, :] = dot(KT[h * 64 : (h + 1) * 64, :], PT[m, h]) * (HEAD_DIM ** -0.5)
        dq_rows = DQ[...].T.astype(BF16)
        GMX[lp, :, 0:LANES] = dq_rows[:ROWS]
        GMX[4 + lp, :, 0:LANES] = dq_rows[ROWS:]

    total_d.second()
    gather_b.sibling(0)
    attend_back(0)
    gather_b.forward(2)
    gather_b.forward(1)
    scatter_b.reduce(3)
    gather_b.sibling(2)
    attend_back(1)
    total_i.second()
    gather_b.sibling(1)
    attend_back(2)
    gather_b.forward(3)
    scatter_b.reduce(1)
    scatter_b.reduce(0)
    gather_b.sibling(3)
    attend_back(3)
    scatter_b.reduce(2)

    for blk in range(8):
        rows = pl.ds(blk * ROWS, ROWS)
        GMX[blk, :, LANES : 2 * LANES] = DK[rows].astype(BF16)
        GMX[blk, :, 2 * LANES :] = DV[rows].astype(BF16)
    all_mixed = GMX[...].reshape(8 * ROWS, 3 * LANES)
    scatter_n = Scatter(PA, CS, 3, scatter_m)

    def back_out(m):
        scatter_n.emit(m, dot_nt(cat_rows(GMX, flip_l(m)), WQ[...]))

    def joint_grad(blk):
        product = dot_tn(N1[:, :, blk * LANES : (blk + 1) * LANES].reshape(8 * ROWS, LANES), all_mixed).astype(BF16)
        for r in range(4):
            tt, jj = shard_place(blk * 4 + r)
            for ch in range(3):
                GQ[ch, tt, jj] = product[r * 32 : (r + 1) * 32, ch * LANES : (ch + 1) * LANES]

    for blk in range(8):
        joint_grad(blk)
    for ch in range(3):
        total_q[ch].start_cross()
    for ch in range(3):
        total_q[ch].start_keep()

    back_out(3)
    back_out(1)
    scatter_n.reduce(3)
    back_out(2)
    scatter_n.reduce(1)
    back_out(0)
    GO[...] = GOF[...].astype(BF16)
    sem_go, sem_gs = slots(4), slots(4)

    @pl.when(x != c)
    def _():
        send(GO, XGO.at[0], dev(dx=1), sem_go)

    scatter_n.reduce(0)

    sums = [jnp.zeros((1, D), F32) for _ in range(2)]
    for m in range(4):
        lp = flip_l(m)
        for half in range(2):
            value = PA[m, half].astype(F32)
            sums[0] += jnp.sum(value * N0[half * 4 + lp].astype(F32), axis=0, keepdims=True)
            sums[1] += jnp.sum(value, axis=0, keepdims=True)
    vectors[0], vectors[1] = sums
    scatter_n.reduce(2)
    mixed_sums = jnp.sum(all_mixed.astype(F32), axis=0, keepdims=True)
    for q in range(8):
        VG[q] = jnp.zeros((16, LANES), F32)
        for p in (0, 1, 4, 5, 6, 7):
            VG[q, p : p + 1] = vectors[p][:, q * LANES : (q + 1) * LANES]
        for p, ch in ((2, 0), (3, 2)):
            VG[q, p : p + 1] = jnp.where(own_pair == q, mixed_sums[:, ch * LANES : (ch + 1) * LANES], 0.0)
        ch = (q // 4) * 2 + q % 2
        for r in range(4):
            here = jnp.logical_and(c == (q // 2) % 2, l == r)
            VG[q, 8 + r : 9 + r] = jnp.where(here, BG[0:1, ch * LANES : (ch + 1) * LANES], 0.0)
    sem_v1, sem_v2 = slots(8), slots(4)
    for dx, dc, dzh in line_masks:
        mask = dx * 4 + dc * 2 + dzh
        push(VG.at[flip(x, dx) * 4 + flip(c, dc) * 2 + flip(zh, dzh)], VR.at[mask], dev(dx=dx, dc=dc, dzh=dzh), sem_v1 + mask)

    @pl.when(x == c)
    def _():
        arrive(XGO.at[0], sem_go)
        GOF[...] += XGO[0].astype(F32)

    @pl.when(root_mask == 1)
    def _():
        GO[...] = GOF[...].astype(BF16)
        send(GO, XGO.at[1], dev(dzh=1), sem_go + 1)

    for ch in range(3):
        total_q[ch].second()

    bias_d = PV[7:8, :]
    sem_out, sem_in = slots(), slots()
    scatter_b.finish()
    for r in range(4):
        rows = pl.ds(r * 32, 32)
        BO[rows] = (XO[rows] + scatter_b.rows(rows) + bias_d).astype(BF16)
    put_block = move(BO, out_block.at[0], 6)

    @pl.when(native)
    def _():
        put_block.start()

    @pl.when(foreign)
    def _():
        send(BO, out_block.at[0], partner, sem_out)

    TD[...] = total_d.result().astype(BF16)
    put_d = move(TD, out_d, 7)
    put_d.start()
    TI[...] = total_i.result().astype(BF16)
    sem_ti, sem_tq = slots(8), slots(8 * 3)
    for dc, dl in group_masks:
        push(TI.at[group(dc, dl)], out_i.at[j], dev(dc=dc, dl=dl), sem_ti + dc * 4 + dl)
    put_i = move(TI.at[j], out_i.at[j], 8)
    put_i.start()

    slab = VG[q_own]
    for dx, dc, dzh in line_masks:
        mask = dx * 4 + dc * 2 + dzh
        arrive(VR.at[mask], sem_v1 + mask)
        slab += VR[mask]
    SL[...] = slab
    for dl in (1, 2, 3):
        push(SL, SLR.at[dl], dev(dl=dl), sem_v2 + dl)

    put_o = move(TGO.at[l], out_o, 10)

    @pl.when(is_root)
    def _():
        arrive(XGO.at[1], sem_go + 1)
        TGO[...] = (GOF[...] + XGO[1].astype(F32)).astype(BF16).reshape(4, 32, D)
        for slot in range(4):
            mine = jnp.logical_and(y == c, l == slot)

            @pl.when(mine)
            def _():
                put_o.start()

            @pl.when(jnp.logical_not(mine))
            def _():
                send(TGO.at[slot], out_o, (x * 2 + y, zh * 4 + slot), sem_gs + slot)

    scatter_n.finish()
    for r in range(4):
        rows = pl.ds(r * 32, 32)
        grad = scatter_n.rows(rows)
        normal, root, _ = norm_rows(X[j, rows].astype(F32), gain1, shift1)
        BI[rows] = (N2F[rows] + norm_back(grad, normal, root, gain1)).astype(BF16)
    put_input = move(BI, out_input.at[0], 9)

    @pl.when(native)
    def _():
        put_input.start()

    @pl.when(foreign)
    def _():
        send(BI, out_input.at[0], partner, sem_in)

    for ch in range(3):
        TQ[ch] = total_q[ch].result().astype(BF16)
        for dc, dl in group_masks:
            push(TQ.at[ch, group(dc, dl)], out_q.at[ch, j], dev(dc=dc, dl=dl), sem_tq + ch * 8 + dc * 4 + dl)
    put_q = [move(TQ.at[ch, j], out_q.at[ch, j], 11 + ch) for ch in range(3)]
    for ch in range(3):
        put_q[ch].start()

    for dl in (1, 2, 3):
        arrive(SLR.at[dl], sem_v2 + dl)
        slab += SLR[dl]
    SLF[...] = slab
    put_small = move(SLF, out_small, 14)
    put_small.start()

    for dc, dl in group_masks:
        arrive(out_i.at[group(dc, dl)], sem_ti + dc * 4 + dl)
        for ch in range(3):
            arrive(out_q.at[ch, group(dc, dl)], sem_tq + ch * 8 + dc * 4 + dl)

    put_d.wait()
    put_i.wait()
    put_small.wait()
    for ch in range(3):
        put_q[ch].wait()

    @pl.when(native)
    def _():
        put_block.wait()
        put_input.wait()

    @pl.when(foreign)
    def _():
        left(SGI, sem_ps)
        left(xin.at[0], sem_px)
        left(cin.at[0], sem_pc)
        left(BO, sem_out)
        left(BI, sem_in)
        arrive(out_block.at[0], sem_out)
        arrive(out_input.at[0], sem_in)

    @pl.when(to_self)
    def _():
        put_o.wait()

    @pl.when(jnp.logical_not(to_self))
    def _():
        left(wo, sem_wo + l)
        arrive(out_o, sem_gs + l)

    @pl.when(x != c)
    def _():
        left(GO, sem_go)

    @pl.when(root_mask == 1)
    def _():
        left(GO, sem_go + 1)

    @pl.when(root_mask == 1)
    def _():
        left(WO, sem_wt + 3)

    @pl.when(is_root)
    def _():
        for mask in (1, 2):
            left(WO, sem_wt + mask)
        for slot in range(4):
            @pl.when(jnp.logical_not(jnp.logical_and(y == c, l == slot)))
            def _():
                left(TGO.at[slot], sem_gs + slot)

    scatter_n.close()
    scatter_b.close()
    for k in (1, 2):
        left(X.at[j], gather_x.far + k)
    left(X.at[j], gather_x.near)
    for copy in pending:
        copy.wait_send()


def fused_scratch():
    def v(*shape):
        return pltpu.VMEM(shape, BF16)

    def f(*shape):
        return pltpu.VMEM(shape, F32)

    blocks = (8, ROWS, D)
    return [
        v(*blocks), v(*blocks), v(*blocks), v(*blocks), v(*blocks), v(*blocks),
        f(8, LANES), f(8, 8, LANES), f(16, LANES), f(4, 16, LANES), f(8, 16, LANES), f(16, D),
        v(32, 3 * D), v(8, 3, 32, LANES), v(3, 4, 8, 32, LANES), v(D, 3 * LANES), v(4, 32, D),
        v(32, 4 * D), v(8, 4, 32, LANES), v(4, 8, 4, 32, LANES), v(D, 512), v(4, LANES, D),
        v(D, LANES), v(D, LANES), v(D, LANES), v(LANES, D), v(LANES, D), v(LANES, D),
        f(8, ROWS, LANES), f(2, D, 256), v(4, 2, D, 256), f(4, 2, 8, 256),
        f(4, LANES, 256), v(4, LANES, 256),
        v(4, 2, ROWS, D), v(4, ROWS, D), v(4, 2, ROWS, D), v(4, ROWS, D),
        v(4, 4, ROWS, D), v(4, 4, ROWS, D), f(ROWS, D), f(ROWS, D),
        v(512, D), v(4, 256, 512), v(8, ROWS, 512), f(4, 256, 512),
        f(D, LANES), f(D, LANES), f(LANES, 256), v(8, ROWS, 3 * LANES),
        v(3, 4, 8, 32, LANES), v(4, 8, 4, 32, LANES), v(4, LANES, D),
        v(3, 2, 8, 32, LANES), v(2, 8, 4, 32, LANES), v(2, LANES, D),
        v(3, 8, 32, LANES), v(8, 4, 32, LANES), v(LANES, D),
        v(3, 8, 32, LANES), v(8, 4, 32, LANES), v(LANES, D),
        v(3, 8, 32, LANES), v(8, 4, 32, LANES), v(LANES, D),
        v(LANES, D), f(LANES, D), v(4, LANES, D), v(4, 32, D),
        f(8, 16, LANES), f(8, 16, LANES), f(16, LANES), f(4, 16, LANES), f(16, LANES),
        f(ROWS, LANES), f(8, 512), v(ROWS, D), v(ROWS, D),
        pltpu.SemaphoreType.DMA((COPIES,)),
        pltpu.SemaphoreType.DMA((COPIES,)),
        pltpu.SemaphoreType.DMA((16,)),
    ]


def finish_kernel(
    block, grad_in, grad_q, grad_o, grad_i, grad_d, small,
    out_block, out_input, o0, o1, out_q, o2, o3, out_o, o4, o5, o6, out_i, ob, out_d, o7,
):
    place = lax.rem(lax.axis_index("band"), 4)
    out_block[...] = block[...]
    out_input[...] = grad_in[...]
    for jj in range(8):
        for ch in range(3):
            out_q[:, ch * D + pair_of(jj) * LANES : ch * D + (pair_of(jj) + 1) * LANES] = grad_q[ch, jj].astype(F32)
        for ch in range(4):
            flat = flat_column(jj, ch)
            out_i[:, flat * LANES : (flat + 1) * LANES] = grad_i[jj, ch].astype(F32)
    out_o[...] = grad_o[...].astype(F32)
    out_d[...] = grad_d[...].astype(F32)
    slab = small[...]
    mine = jnp.zeros((16, 32), F32)
    for k in range(4):
        mine = jnp.where(place == k, slab[:, k * 32 : (k + 1) * 32], mine)
    for p, ref in enumerate((o0, o1, o2, o3, o4, o5, o6, o7)):
        ref[...] = mine[p : p + 1].reshape(32)
    pick = lax.broadcasted_iota(jnp.int32, (16, LANES), 0) == 8 + place
    ob[...] = jnp.sum(jnp.where(pick, slab, 0.0), axis=0, keepdims=True).reshape(LANES)


def fused_shards(
    block_in,
    attention_norm_gain,
    attention_norm_bias,
    query_key_value,
    query_bias,
    value_bias,
    output_weight,
    output_bias,
    mlp_norm_gain,
    mlp_norm_bias,
    mlp_in_weight,
    mlp_in_bias,
    mlp_out_weight,
    mlp_out_bias,
    cotangent,
    segment_ids,
    sub_lengths,
):
    vmem = pl.BlockSpec(memory_space=pltpu.VMEM)
    hbm = pl.BlockSpec(memory_space=pl.ANY)

    def shape(dims, kind):
        return jax.ShapeDtypeStruct(dims, kind)

    parts = pl.pallas_call(
        functools.partial(fused_kernel, COPIES),
        out_shape=(
            shape((1, ROWS, D), BF16),
            shape((1, ROWS, D), BF16),
            shape((3, 8, 32, LANES), BF16),
            shape((32, D), BF16),
            shape((8, 4, 32, LANES), BF16),
            shape((LANES, D), BF16),
            shape((16, LANES), F32),
        ),
        in_specs=[hbm, hbm, vmem, vmem, hbm, hbm, hbm, hbm] + [vmem] * 9,
        out_specs=(hbm,) * 7,
        scratch_shapes=fused_scratch(),
        compiler_params=pltpu.CompilerParams(
            collective_id=0, has_side_effects=True, vmem_limit_bytes=63 * 2**20
        ),
    )(
        block_in, cotangent, segment_ids, sub_lengths,
        query_key_value, output_weight, mlp_in_weight, mlp_out_weight,
        attention_norm_gain, attention_norm_bias, query_bias, value_bias,
        output_bias, mlp_norm_gain, mlp_norm_bias, mlp_out_bias, mlp_in_bias,
    )
    vector = shape((32,), F32)
    return pl.pallas_call(
        finish_kernel,
        out_shape=(
            shape((1, ROWS, D), BF16), shape((1, ROWS, D), BF16), vector, vector,
            shape((32, 3 * D), F32), vector, vector, shape((32, D), F32), vector, vector, vector,
            shape((32, 4 * D), F32), shape((LANES,), F32), shape((LANES, D), F32), vector,
        ),
        in_specs=[vmem] * 7,
        out_specs=(vmem,) * 15,
    )(*parts)


def solution(mesh):
    small_slice = dict(mesh.shape) == {"seq": 4, "band": 8}
    return jax.shard_map(
        fused_shards if small_slice else shards,
        mesh=mesh,
        in_specs=(
            P("seq", "band", None),
            P(("seq", "band")),
            P(("seq", "band")),
            P(("seq", "band"), None),
            P(("seq", "band")),
            P(("seq", "band")),
            P(("seq", "band"), None),
            P(("seq", "band")),
            P(("seq", "band")),
            P(("seq", "band")),
            P(("seq", "band"), None),
            P(("seq", "band")),
            P(("seq", "band"), None),
            P(("seq", "band")),
            P("seq", "band", None),
            P("seq", "band"),
            P("seq", None),
        ),
        out_specs=(
            P("seq", "band", None),
            P("seq", "band", None),
            P(("seq", "band")),
            P(("seq", "band")),
            P(("seq", "band"), None),
            P(("seq", "band")),
            P(("seq", "band")),
            P(("seq", "band"), None),
            P(("seq", "band")),
            P(("seq", "band")),
            P(("seq", "band")),
            P(("seq", "band"), None),
            P(("seq", "band")),
            P(("seq", "band"), None),
            P(("seq", "band")),
        ),
        check_vma=False,
    )
```

```python
import functools
import math

import jax
import jax.numpy as jnp
from jax import lax
from jax.experimental import pallas as pl
from jax.experimental.pallas import tpu as pltpu
from jax.sharding import PartitionSpec as P

D = 1024
HEADS = 16
HEAD_DIM = 64
SUBGRIDS = 8


EPSILON = 1e-05
NEGATIVE = -1e30


def prefix(part, axis, combine, identity):
    place = lax.axis_index(axis)
    gathered = lax.all_gather(part, axis)
    state = jnp.zeros_like(part) + jnp.asarray(identity, part.dtype)

    def one(lap, state):
        return combine(state, lax.dynamic_index_in_dim(gathered, lap, 0, False))

    return lax.fori_loop(0, place, one, state)


def layer_norm(values_in, norm_gain, norm_shift):
    average = jnp.mean(values_in, axis=-1, keepdims=True)
    centered = values_in - average
    variance = jnp.mean(centered * centered, axis=-1, keepdims=True)
    return centered * lax.rsqrt(variance + EPSILON) * norm_gain + norm_shift


def gelu_exact(values_in):
    return jax.nn.gelu(values_in, approximate=False)


def add_counts(first_part, second_part):
    return first_part + second_part


def block_scores(query_part, key_part, seg_part, code_part, scale_factor):
    scores = (
        jnp.einsum("qhe,khe->hqk", query_part, key_part, preferred_element_type=jnp.float32)
        * scale_factor
    )
    allowed = (seg_part[:, None] == code_part[None, :])[None]
    return (jnp.where(allowed, scores, NEGATIVE), allowed)


def split_blocks(array_in, block_rows):
    return array_in.reshape((array_in.shape[0] // block_rows, block_rows) + array_in.shape[1:])


def shards(
    block_in,
    attention_norm_gain,
    attention_norm_bias,
    query_key_value,
    query_bias,
    value_bias,
    output_weight,
    output_bias,
    mlp_norm_gain,
    mlp_norm_bias,
    mlp_in_weight,
    mlp_in_bias,
    mlp_out_weight,
    mlp_out_bias,
    cotangent,
    segment_ids,
    sub_lengths,
):
    float_type = jnp.float32
    half_type = jnp.bfloat16
    rows_local = block_in.shape[1]
    seq_length = rows_local * lax.axis_size("band")
    scale_factor = HEAD_DIM ** (-0.5)
    block_rows = math.gcd(seq_length, 1024)
    seg_local = segment_ids[0]
    labels = jnp.arange(SUBGRIDS, dtype=jnp.int32)
    onehot_ids = (seg_local[:, None] == labels[None, :]).astype(jnp.int32)
    earlier_counts = prefix(
        jnp.sum(onehot_ids, axis=0), "band", add_counts, jnp.zeros((SUBGRIDS,), jnp.int32)
    )
    slots = jnp.arange(rows_local)
    earlier = (slots[None, :] < slots[:, None]).astype(float_type)
    before = (
        jnp.dot(earlier, onehot_ids.astype(float_type), precision=lax.Precision.HIGHEST).astype(
            jnp.int32
        )
        + earlier_counts[None, :]
    )
    patch_rank = jnp.sum(before * onehot_ids, axis=1)
    limits = jnp.sum(onehot_ids * sub_lengths[0][None, :], axis=1)
    realness = patch_rank < limits
    key_codes = jnp.where(realness, seg_local, -1)
    gathered = (
        lax.all_gather(attention_norm_gain, ("seq", "band"), axis=0, tiled=True),
        lax.all_gather(attention_norm_bias, ("seq", "band"), axis=0, tiled=True),
        lax.all_gather(query_key_value, ("seq", "band"), axis=0, tiled=True),
        lax.all_gather(query_bias, ("seq", "band"), axis=0, tiled=True),
        lax.all_gather(value_bias, ("seq", "band"), axis=0, tiled=True),
        lax.all_gather(output_weight, ("seq", "band"), axis=0, tiled=True),
        lax.all_gather(output_bias, ("seq", "band"), axis=0, tiled=True),
        lax.all_gather(mlp_norm_gain, ("seq", "band"), axis=0, tiled=True),
        lax.all_gather(mlp_norm_bias, ("seq", "band"), axis=0, tiled=True),
        lax.all_gather(mlp_in_weight, ("seq", "band"), axis=0, tiled=True),
        lax.all_gather(mlp_in_bias, ("seq", "band"), axis=0, tiled=True),
        lax.all_gather(mlp_out_weight, ("seq", "band"), axis=0, tiled=True),
        lax.all_gather(mlp_out_bias, ("seq", "band"), axis=0, tiled=True),
    )
    (
        gain_one,
        shift_one,
        joint_weight,
        bias_query,
        bias_value,
        proj_weight,
        proj_bias,
        gain_two,
        shift_two,
        up_weight,
        up_bias,
        down_weight,
        down_bias,
    ) = gathered
    inputs = block_in[0].astype(float_type)
    normed_float, norm_pull_one = jax.vjp(
        layer_norm, inputs, gain_one.astype(float_type), shift_one.astype(float_type)
    )
    normed_one = normed_float.astype(half_type)
    mixed_all = jnp.dot(normed_one, joint_weight, preferred_element_type=float_type)
    queries = (mixed_all[:, :D] + bias_query.astype(float_type)).astype(half_type)
    keys_local = mixed_all[:, D : 2 * D].astype(half_type)
    values_local = (mixed_all[:, 2 * D :] + bias_value.astype(float_type)).astype(half_type)
    keys_seq, values_seq, codes_seq = (
        lax.all_gather(keys_local, "band", axis=0, tiled=True),
        lax.all_gather(values_local, "band", axis=0, tiled=True),
        lax.all_gather(key_codes, "band", axis=0, tiled=True),
    )
    query_heads = queries.reshape(rows_local, HEADS, HEAD_DIM)
    key_blocks = split_blocks(keys_seq.reshape(seq_length, HEADS, HEAD_DIM), block_rows)
    value_blocks = split_blocks(values_seq.reshape(seq_length, HEADS, HEAD_DIM), block_rows)
    code_blocks = split_blocks(codes_seq, block_rows)

    def stats_step(running, block_items):
        top_now, total_now = running
        key_part, code_part = block_items
        scores, allowed = block_scores(query_heads, key_part, seg_local, code_part, scale_factor)
        top_new = jnp.maximum(top_now, jnp.max(scores, axis=-1))
        exp_terms = jnp.where(allowed, jnp.exp(scores - top_new[..., None]), 0.0)
        return (
            (top_new, total_now * jnp.exp(top_now - top_new) + jnp.sum(exp_terms, axis=-1)),
            None,
        )

    start_stats = (
        jnp.full((HEADS, rows_local), NEGATIVE, float_type),
        jnp.zeros((HEADS, rows_local), float_type),
    )
    (top_final, total_final), unused_stats = lax.scan(
        stats_step, start_stats, (key_blocks, code_blocks)
    )
    log_total = top_final + jnp.log(total_final)

    def value_step(accum_out, block_items):
        key_part, value_part, code_part = block_items
        scores, allowed = block_scores(query_heads, key_part, seg_local, code_part, scale_factor)
        soft_probs = jnp.where(allowed, jnp.exp(scores - log_total[..., None]), 0.0).astype(
            half_type
        )
        return (
            accum_out
            + jnp.einsum("hqk,khe->qhe", soft_probs, value_part, preferred_element_type=float_type),
            None,
        )

    attended, unused_values = lax.scan(
        value_step,
        jnp.zeros((rows_local, HEADS, HEAD_DIM), float_type),
        (key_blocks, value_blocks, code_blocks),
    )
    attended_low = attended.reshape(rows_local, D).astype(half_type)
    residual = (
        inputs
        + jnp.dot(attended_low, proj_weight, preferred_element_type=float_type)
        + proj_bias.astype(float_type)
    )
    normed_float_two, norm_pull_two = jax.vjp(
        layer_norm, residual, gain_two.astype(float_type), shift_two.astype(float_type)
    )
    normed_two = normed_float_two.astype(half_type)
    hidden_pre = jnp.dot(normed_two, up_weight, preferred_element_type=float_type) + up_bias.astype(
        float_type
    )
    hidden_value, gelu_pull = jax.vjp(gelu_exact, hidden_pre)
    hidden_act = hidden_value.astype(half_type)
    block_result = (
        residual
        + jnp.dot(hidden_act, down_weight, preferred_element_type=float_type)
        + down_bias.astype(float_type)
    )
    gathered_back = (
        lax.all_gather(attention_norm_gain, ("seq", "band"), axis=0, tiled=True),
        lax.all_gather(attention_norm_bias, ("seq", "band"), axis=0, tiled=True),
        lax.all_gather(query_key_value, ("seq", "band"), axis=0, tiled=True),
        lax.all_gather(query_bias, ("seq", "band"), axis=0, tiled=True),
        lax.all_gather(value_bias, ("seq", "band"), axis=0, tiled=True),
        lax.all_gather(output_weight, ("seq", "band"), axis=0, tiled=True),
        lax.all_gather(output_bias, ("seq", "band"), axis=0, tiled=True),
        lax.all_gather(mlp_norm_gain, ("seq", "band"), axis=0, tiled=True),
        lax.all_gather(mlp_norm_bias, ("seq", "band"), axis=0, tiled=True),
        lax.all_gather(mlp_in_weight, ("seq", "band"), axis=0, tiled=True),
        lax.all_gather(mlp_in_bias, ("seq", "band"), axis=0, tiled=True),
        lax.all_gather(mlp_out_weight, ("seq", "band"), axis=0, tiled=True),
        lax.all_gather(mlp_out_bias, ("seq", "band"), axis=0, tiled=True),
    )
    joint_back = gathered_back[2]
    proj_back = gathered_back[5]
    up_back = gathered_back[9]
    down_back = gathered_back[11]
    grad_out = cotangent[0].astype(float_type) * realness[:, None].astype(float_type)
    grad_mlp = grad_out.astype(half_type)
    grad_down_weight = jnp.einsum(
        "rf,rd->fd", hidden_act, grad_mlp, preferred_element_type=float_type
    )
    grad_down_bias = jnp.sum(grad_mlp.astype(float_type), axis=0)
    grad_act = jnp.einsum("rd,fd->rf", grad_mlp, down_back, preferred_element_type=float_type)
    grad_pre = gelu_pull(grad_act)[0].astype(half_type)
    grad_up_weight = jnp.einsum(
        "rd,rf->df", normed_two, grad_pre, preferred_element_type=float_type
    )
    grad_up_bias = jnp.sum(grad_pre.astype(float_type), axis=0)
    grad_normed_two = jnp.einsum("rf,df->rd", grad_pre, up_back, preferred_element_type=float_type)
    grad_resid_part, grad_gain_two, grad_shift_two = norm_pull_two(grad_normed_two)
    grad_residual = grad_out + grad_resid_part
    grad_branch = grad_residual.astype(half_type)
    grad_proj_weight = jnp.einsum(
        "rd,re->de", attended_low, grad_branch, preferred_element_type=float_type
    )
    grad_proj_bias = jnp.sum(grad_branch.astype(float_type), axis=0)
    grad_attended = jnp.einsum(
        "re,de->rd", grad_branch, proj_back, preferred_element_type=float_type
    ).astype(half_type)
    grad_heads = grad_attended.reshape(rows_local, HEADS, HEAD_DIM)
    row_delta = jnp.sum(grad_heads.astype(float_type) * attended, axis=-1).T
    keys_back = lax.all_gather(keys_local, "band", axis=0, tiled=True)
    values_back = lax.all_gather(values_local, "band", axis=0, tiled=True)
    codes_back = lax.all_gather(key_codes, "band", axis=0, tiled=True)
    key_back_blocks = split_blocks(keys_back.reshape(seq_length, HEADS, HEAD_DIM), block_rows)
    value_back_blocks = split_blocks(values_back.reshape(seq_length, HEADS, HEAD_DIM), block_rows)
    code_back_blocks = split_blocks(codes_back, block_rows)

    def key_step(query_accum, block_items):
        key_part, value_part, code_part = block_items
        scores, allowed = block_scores(query_heads, key_part, seg_local, code_part, scale_factor)
        soft_probs = jnp.where(allowed, jnp.exp(scores - log_total[..., None]), 0.0)
        grad_probs = jnp.einsum(
            "qhe,khe->hqk", grad_heads, value_part, preferred_element_type=float_type
        )
        grad_scores = (soft_probs * (grad_probs - row_delta[..., None])).astype(half_type)
        query_accum = query_accum + jnp.einsum(
            "hqk,khe->qhe", grad_scores, key_part, preferred_element_type=float_type
        )
        return (query_accum, None)

    query_total, joined_blocks = lax.scan(
        key_step,
        jnp.zeros((rows_local, HEADS, HEAD_DIM), float_type),
        (key_back_blocks, value_back_blocks, code_back_blocks),
    )
    grad_query = (query_total * scale_factor).reshape(rows_local, D)
    query_seq = lax.all_gather(queries, "band", axis=0, tiled=True)
    grad_seq = lax.all_gather(grad_attended, "band", axis=0, tiled=True)
    total_seq = lax.all_gather(log_total, "band", axis=1, tiled=True)
    delta_seq = lax.all_gather(row_delta, "band", axis=1, tiled=True)
    seg_seq = lax.all_gather(seg_local, "band", axis=0, tiled=True)
    block_count = seq_length // block_rows
    key_heads_local = keys_local.reshape(rows_local, HEADS, HEAD_DIM)
    value_heads_local = values_local.reshape(rows_local, HEADS, HEAD_DIM)

    def query_step(running, block_items):
        key_accum, value_accum = running
        query_part, grad_part, total_part, delta_part, seg_part = block_items
        scores, allowed = block_scores(
            query_part, key_heads_local, seg_part, key_codes, scale_factor
        )
        soft_probs = jnp.where(allowed, jnp.exp(scores - total_part[..., None]), 0.0)
        grad_probs = jnp.einsum(
            "qhe,khe->hqk", grad_part, value_heads_local, preferred_element_type=float_type
        )
        grad_scores = (soft_probs * (grad_probs - delta_part[..., None])).astype(half_type)
        key_accum = key_accum + jnp.einsum(
            "hqk,qhe->khe", grad_scores, query_part, preferred_element_type=float_type
        )
        value_accum = value_accum + jnp.einsum(
            "hqk,qhe->khe",
            soft_probs.astype(half_type),
            grad_part,
            preferred_element_type=float_type,
        )
        return ((key_accum, value_accum), None)

    zero_heads = jnp.zeros((rows_local, HEADS, HEAD_DIM), float_type)
    (key_total, value_total), query_blocks = lax.scan(
        query_step,
        (zero_heads, zero_heads),
        (
            split_blocks(query_seq.reshape(seq_length, HEADS, HEAD_DIM), block_rows),
            split_blocks(grad_seq.reshape(seq_length, HEADS, HEAD_DIM), block_rows),
            total_seq.reshape(HEADS, block_count, block_rows).transpose(1, 0, 2),
            delta_seq.reshape(HEADS, block_count, block_rows).transpose(1, 0, 2),
            split_blocks(seg_seq, block_rows),
        ),
    )
    grad_key = (key_total * scale_factor).reshape(rows_local, D)
    grad_value = value_total.reshape(rows_local, D)
    grad_query_low = grad_query.astype(half_type)
    grad_value_low = grad_value.astype(half_type)
    grad_mixed = jnp.concatenate(
        [grad_query_low, grad_key.astype(half_type), grad_value_low], axis=1
    )
    grad_joint_weight = jnp.einsum(
        "rd,rm->dm", normed_one, grad_mixed, preferred_element_type=float_type
    )
    grad_bias_query = jnp.sum(grad_query_low.astype(float_type), axis=0)
    grad_bias_value = jnp.sum(grad_value_low.astype(float_type), axis=0)
    grad_normed_one = jnp.einsum(
        "rm,dm->rd", grad_mixed, joint_back, preferred_element_type=float_type
    )
    grad_input_part, grad_gain_one, grad_shift_one = norm_pull_one(grad_normed_one)
    input_grad = (grad_residual + grad_input_part).astype(half_type)
    shard_grads = (
        lax.psum_scatter(grad_gain_one, ("seq", "band"), scatter_dimension=0, tiled=True),
        lax.psum_scatter(grad_shift_one, ("seq", "band"), scatter_dimension=0, tiled=True),
        lax.psum_scatter(grad_joint_weight, ("seq", "band"), scatter_dimension=0, tiled=True),
        lax.psum_scatter(grad_bias_query, ("seq", "band"), scatter_dimension=0, tiled=True),
        lax.psum_scatter(grad_bias_value, ("seq", "band"), scatter_dimension=0, tiled=True),
        lax.psum_scatter(grad_proj_weight, ("seq", "band"), scatter_dimension=0, tiled=True),
        lax.psum_scatter(grad_proj_bias, ("seq", "band"), scatter_dimension=0, tiled=True),
        lax.psum_scatter(grad_gain_two, ("seq", "band"), scatter_dimension=0, tiled=True),
        lax.psum_scatter(grad_shift_two, ("seq", "band"), scatter_dimension=0, tiled=True),
        lax.psum_scatter(grad_up_weight, ("seq", "band"), scatter_dimension=0, tiled=True),
        lax.psum_scatter(grad_up_bias, ("seq", "band"), scatter_dimension=0, tiled=True),
        lax.psum_scatter(grad_down_weight, ("seq", "band"), scatter_dimension=0, tiled=True),
        lax.psum_scatter(grad_down_bias, ("seq", "band"), scatter_dimension=0, tiled=True),
    )
    return (
        block_result.astype(half_type)[None],
        input_grad[None],
        shard_grads[0],
        shard_grads[1],
        shard_grads[2],
        shard_grads[3],
        shard_grads[4],
        shard_grads[5],
        shard_grads[6],
        shard_grads[7],
        shard_grads[8],
        shard_grads[9],
        shard_grads[10],
        shard_grads[11],
        shard_grads[12],
    )


F32 = jnp.float32
BF16 = jnp.bfloat16
MESH_ID = pl.DeviceIdType.MESH
ROWS = 128
LANES = 128
COPIES = 240


def dot(lhs, rhs):
    return jnp.dot(lhs, rhs, preferred_element_type=F32)


def dot_nt(lhs, rhs):
    return lax.dot_general(lhs, rhs, (((1,), (1,)), ((), ())), preferred_element_type=F32)


def dot_tn(lhs, rhs):
    return lax.dot_general(lhs, rhs, (((0,), (0,)), ((), ())), preferred_element_type=F32)


def pair_of(jj):
    return (jj // 4) * 4 + (jj % 2) * 2 + (jj // 2) % 2


def flat_column(jj, ch):
    return (ch // 2) * 16 + (jj // 4) * 8 + (ch % 2) * 4 + jj % 4


def shard_place(i):
    return (i // 16) * 2 + (i // 4) % 2, ((i // 8) % 2) * 4 + i % 4


def fused_kernel(copies, *refs):
    (
        xin, cin, seg_in, len_in, wq, wo, wi, wd,
        p0, p1, p2, p3, p4, p5, p6, p7, pb,
        out_block, out_input, out_q, out_o, out_i, out_d, out_small,
        X, N0, N1, N2, GM, GB, SGI, SG, PK, SP, FULL, PV,
        WQI, WSQ, RQ, WQ, WO, WII, WSI, RI, WI, WD,
        QS, KK, VV, QT, KT, VT, CODE, SC, PT, INV, OT, OL,
        PA, CS, PB, CSB, SB, RV, XO, N2F, HAT, HA, GP, GA,
        DK, DV, DQ, GMX,
        GQ, GI, GD, XQ, XI, XD, HQ, HI, HD, ZQ, ZI, ZD, TQ, TI, TD,
        GO, GOF, XGO, TGO,
        VG, VR, SL, SLR, SLF, RS_, BG, BO, BI,
        ssem, rsem, lsem,
    ) = refs
    s = lax.axis_index("seq")
    b = lax.axis_index("band")
    x, c = lax.div(s, 2), lax.rem(s, 2)
    zh, l = lax.div(b, 4), lax.rem(b, 4)
    zl, y = lax.div(l, 2), lax.rem(l, 2)
    t, j = x * 2 + zh, c * 4 + l

    def flip(v, d):
        return 1 - v if d else v

    def flip_l(d):
        return flip(zl, d // 2) * 2 + flip(y, d % 2)

    def dev(dx=0, dc=0, dzh=0, dl=0):
        return (flip(x, dx) * 2 + flip(c, dc), flip(zh, dzh) * 4 + flip_l(dl))

    roles = (l, flip_l(2), flip_l(1), flip_l(3))

    counter = [0]
    pending = []

    def slots(n=1):
        first = counter[0]
        counter[0] += n
        assert counter[0] <= copies
        return first

    def send(src, dst, device, sem):
        copy = pltpu.make_async_remote_copy(
            src_ref=src, dst_ref=dst, send_sem=ssem.at[sem], recv_sem=rsem.at[sem],
            device_id=device, device_id_type=MESH_ID)
        copy.start()
        return copy

    def push(src, dst, device, sem):
        copy = send(src, dst, device, sem)
        pending.append(copy)
        return copy

    def arrive(dst, sem):
        pltpu.make_async_remote_copy(
            src_ref=dst, dst_ref=dst, send_sem=ssem.at[sem], recv_sem=rsem.at[sem],
            device_id=dev(dc=1), device_id_type=MESH_ID).wait_recv()

    def left(src, sem):
        pltpu.make_async_remote_copy(
            src_ref=src, dst_ref=src, send_sem=ssem.at[sem], recv_sem=rsem.at[sem],
            device_id=dev(dc=1), device_id_type=MESH_ID).wait_send()

    def move(src, dst, sem):
        return pltpu.make_async_copy(src, dst, lsem.at[sem])

    group_masks = [(dc, dl) for dl in (3, 1, 2, 0) for dc in (0, 1) if (dc, dl) != (0, 0)]
    line_masks = [(dx, dc, dzh) for dx in (1, 0) for dc in (0, 1) for dzh in (1, 0) if dx + dc + dzh]

    def group(dc, dl):
        return flip(c, dc) * 4 + flip_l(dl)

    native = c == zh
    foreign = jnp.logical_not(native)
    partner = dev(dc=1, dzh=1)
    their_block = (1 - c) * 4 + l

    barrier = pltpu.get_barrier_semaphore()
    peers = [dict(dc=dc, dl=dl) for dc, dl in group_masks]
    peers += [dict(dx=a, dc=e, dzh=f) for a, e, f in line_masks if (a, e, f) != (0, 1, 0)]
    for peer in peers:
        pl.semaphore_signal(barrier, inc=1, device_id=dev(**peer), device_id_type=MESH_ID)
    get_q, get_i, get_d = move(wq, WQI, 0), move(wi, WII, 1), move(wd, WD.at[t], 2)
    get_x, get_c = move(xin.at[0], X.at[j], 3), move(cin.at[0], GM.at[j], 4)
    get_q.start()
    get_i.start()
    get_d.start()

    @pl.when(native)
    def _():
        get_x.start()
        get_c.start()

    lane_group = lax.broadcasted_iota(jnp.int32, (1, LANES), 1) // 32
    PK[...] = jnp.zeros_like(PK)
    for p, ref in enumerate((p0, p1, p2, p3, p4, p5, p6, p7)):
        value = ref[...].astype(F32).reshape(1, 32)
        PK[p : p + 1] = jnp.where(lane_group == l, jnp.concatenate([value] * 4, axis=1), 0.0)
    own_bias = pb[...].astype(F32).reshape(1, LANES)
    for r in range(4):
        PK[8 + r : 9 + r] = jnp.where(l == r, own_bias, jnp.zeros_like(own_bias))
    SGI[...] = jnp.zeros_like(SGI)
    SGI[0:1] = seg_in[...].astype(F32)
    SGI[1:2, 0:SUBGRIDS] = len_in[...].astype(F32)
    get_q.wait()
    for jj in range(8):
        for ch in range(3):
            WSQ[jj, ch] = WQI[:, ch * D + pair_of(jj) * LANES : ch * D + (pair_of(jj) + 1) * LANES]
    for ch in range(3):
        RQ[ch, t, j] = WSQ[j, ch]
    pl.semaphore_wait(barrier, len(peers))

    sem_px, sem_pc, sem_ps = slots(), slots(), slots()
    sem_wq, sem_s1 = slots(8), slots(4)
    for dl in (1, 2, 3):
        push(PK, SP.at[dl], dev(dl=dl), sem_s1 + dl)

    @pl.when(native)
    def _():
        SG[j] = SGI[...]

    @pl.when(foreign)
    def _():
        send(SGI, SG.at[their_block], partner, sem_ps)
        send(xin.at[0], X.at[their_block], partner, sem_px)

    for dc, dl in group_masks:
        push(WSQ.at[group(dc, dl)], RQ.at[:, t, j], dev(dc=dc, dl=dl), sem_wq + dc * 4 + dl)

    class Gather:
        def __init__(self, buf):
            self.buf, self.far, self.near = buf, slots(4), slots(4)

        def start(self):
            block = self.buf.at[j]
            copies_out = [
                send(block, block, dev(dc=1), self.near),
                send(block, block, (s, zh * 4 + roles[1]), self.far + 1),
                send(block, block, (s, zh * 4 + roles[2]), self.far + 2),
            ]
            return copies_out

        def begin(self):
            pending.extend(self.start())

        def forward(self, k):
            block = self.buf.at[c * 4 + roles[k]]
            arrive(block, self.far + k)
            if k == 1:
                push(block, block, (s, zh * 4 + roles[2]), self.far + 3)
            push(block, block, dev(dc=1), self.near + k)

        def sibling(self, k):
            arrive(self.buf.at[(1 - c) * 4 + roles[k]], self.near + k)

    gather_x = Gather(X)
    gather_g = Gather(GM)

    @pl.when(native)
    def _():
        get_x.wait()
        gather_x.start()

    sem_wo, sem_wt = slots(4), slots(4)
    own_pair = c * 4 + y * 2 + zl
    pair_l = zh * 2 + c
    to_self = jnp.logical_and(x == c, l == pair_l)
    is_root = jnp.logical_and(x == c, zh == zl)
    root_mask = jnp.abs(x - c) * 2 + jnp.abs(zh - zl)
    get_o = move(wo, WO.at[l], 5)

    @pl.when(to_self)
    def _():
        get_o.start()

    @pl.when(jnp.logical_not(to_self))
    def _():
        send(wo, WO.at[l], (x * 2 + x, zh * 4 + pair_l), sem_wo + l)

    q_own = x * 4 + c * 2 + zh
    slab = PK[...]
    for dl in (1, 2, 3):
        arrive(SP.at[dl], sem_s1 + dl)
        slab += SP[dl]
    FULL[q_own] = slab
    sem_s2 = slots(8)
    for dx, dc, dzh in line_masks:
        push(FULL.at[q_own], FULL.at[q_own], dev(dx=dx, dc=dc, dzh=dzh), sem_s2 + dx * 4 + dc * 2 + dzh)

    class Spread:
        def __init__(self, buf):
            self.buf, self.sem = buf, slots(3)

        def start_z(self, keep=True):
            block = self.buf.at[t]
            copy = send(block, block, dev(dzh=1), self.sem)
            if keep:
                pending.append(copy)

        def start_x(self):
            block = self.buf.at[t]
            push(block, block, dev(dx=1), self.sem + 1)

        def sent_z(self):
            left(self.buf.at[t], self.sem)

        def start(self):
            self.start_z()
            self.start_x()

        def forward(self):
            block = self.buf.at[x * 2 + 1 - zh]
            arrive(block, self.sem)
            push(block, block, dev(dx=1), self.sem + 2)

        def finish(self):
            arrive(self.buf.at[(1 - x) * 2 + zh], self.sem + 1)
            arrive(self.buf.at[(1 - x) * 2 + 1 - zh], self.sem + 2)

    spread_q = [Spread(RQ.at[ch]) for ch in range(3)]
    for dc, dl in group_masks:
        arrive(RQ.at[:, t, group(dc, dl)], sem_wq + dc * 4 + dl)
    for ch in range(3):
        spread_q[ch].start()

    sem_sg = slots(8)

    @pl.when(foreign)
    def _():
        arrive(SG.at[j], sem_ps)

    for dc, dl in group_masks:
        push(SG.at[j], SG.at[j], dev(dc=dc, dl=dl), sem_sg + dc * 4 + dl)
    @pl.when(foreign)
    def _():
        arrive(X.at[j], sem_px)
        gather_x.start()

    for slot in range(4):
        @pl.when(jnp.logical_and(is_root, jnp.logical_not(jnp.logical_and(y == c, l == slot))))
        def _():
            arrive(WO.at[slot], sem_wo + slot)

    @pl.when(to_self)
    def _():
        get_o.wait()

    @pl.when(is_root)
    def _():
        send(WO, WO, dev(dzh=1), sem_wt + 1)
        send(WO, WO, dev(dx=1), sem_wt + 2)


    @pl.when(foreign)
    def _():
        send(cin.at[0], GM.at[their_block], partner, sem_pc)

    for dx, dc, dzh in line_masks:
        arrive(FULL.at[flip(x, dx) * 4 + flip(c, dc) * 2 + flip(zh, dzh)], sem_s2 + dx * 4 + dc * 2 + dzh)
    for q in range(8):
        PV[:, q * LANES : (q + 1) * LANES] = FULL[q]
    gain1, shift1 = PV[0:1, :], PV[1:2, :]

    def norm_rows(value, gain, shift):
        average = jnp.mean(value, axis=-1, keepdims=True)
        centered = value - average
        root = lax.rsqrt(jnp.mean(centered * centered, axis=-1, keepdims=True) + EPSILON)
        normal = centered * root
        return normal, root, normal * gain + shift

    def norm_one(block):
        for r in range(2):
            rows = pl.ds(r * 64, 64)
            normal, _, value = norm_rows(X[block, rows].astype(F32), gain1, shift1)
            N0[block, rows] = normal.astype(BF16)
            N1[block, rows] = value.astype(BF16)

    norm_one(j)

    gather_x.sibling(0)
    norm_one((1 - c) * 4 + l)
    gather_x.forward(1)
    gather_x.forward(2)
    norm_one(c * 4 + roles[1])
    norm_one(c * 4 + roles[2])
    spread_q[0].forward()
    get_i.wait()
    for jj in range(8):
        for ch in range(4):
            flat = flat_column(jj, ch)
            WSI[jj, ch] = WII[:, flat * LANES : (flat + 1) * LANES]
    sem_wi = slots(8)
    for dc, dl in group_masks:
        push(WSI.at[group(dc, dl)], RI.at[t, j], dev(dc=dc, dl=dl), sem_wi + dc * 4 + dl)
    RI[t, j] = WSI[j]
    for k in (1, 2):
        gather_x.sibling(k)
    gather_x.forward(3)
    norm_one((1 - c) * 4 + roles[1])
    spread_q[1].forward()
    norm_one((1 - c) * 4 + roles[2])
    norm_one(c * 4 + roles[3])
    spread_q[2].forward()
    gather_x.sibling(3)
    norm_one((1 - c) * 4 + roles[3])

    get_d.wait()
    spread_i, spread_d = Spread(RI), Spread(WD)

    for dc, dl in group_masks:
        arrive(SG.at[group(dc, dl)], sem_sg + dc * 4 + dl)
    lens = SG[j, 1:2, :]
    row_ids = lax.broadcasted_iota(jnp.int32, (LANES, LANES), 0)
    lane_ids = lax.broadcasted_iota(jnp.int32, (LANES, LANES), 1)
    label_row = lane_ids.astype(F32)
    label_col = row_ids.astype(F32)
    earlier = (lane_ids < row_ids).astype(BF16)
    running = jnp.zeros((1, LANES), F32)
    for blk in range(8):
        onehot = (label_col == SG[blk, 0:1, :]).astype(F32).T
        before = dot(earlier, onehot.astype(BF16)) + running
        running = running + jnp.sum(onehot, axis=0, keepdims=True)
        rank = jnp.sum(before * onehot, axis=1, keepdims=True)
        limit = jnp.sum(onehot * lens, axis=1, keepdims=True)
        ident = jnp.sum(label_row * onehot, axis=1, keepdims=True)
        CODE[blk] = jnp.broadcast_to(jnp.where(rank < limit, ident, -1.0), (ROWS, LANES))

    @pl.when(native)
    def _():
        get_c.wait()

    @pl.when(foreign)
    def _():
        arrive(GM.at[j], sem_pc)

    is_real = CODE[j][:, 0:1] >= 0.0
    GM[j] = jnp.where(is_real, GM[j].astype(F32), 0.0).astype(BF16)
    gather_g.begin()

    @pl.when(jnp.logical_not(is_root))
    def _():
        arrive(WO, sem_wt + root_mask)

    @pl.when(root_mask == 1)
    def _():
        send(WO, WO, dev(dx=1), sem_wt + 3)

    for dc, dl in group_masks:
        arrive(RI.at[t, group(dc, dl)], sem_wi + dc * 4 + dl)
    spread_i.start_z()
    spread_i.start_x()
    spread_d.start_x()
    for ch in range(3):
        spread_q[ch].finish()
        for i in range(32):
            tt, jj = shard_place(i)
            WQ[i * 32 : (i + 1) * 32, ch * LANES : (ch + 1) * LANES] = RQ[ch, tt, jj]
    bias_q, bias_v = FULL[own_pair][2:3, :], FULL[own_pair][3:4, :]
    for k in range(4):
        rows = pl.ds(k * 256, 256)
        normed = N1[2 * k : 2 * k + 2].reshape(256, D)
        mixed = dot(normed, WQ[...])
        queries = (mixed[:, :LANES] + bias_q).astype(BF16).astype(F32) * (HEAD_DIM ** -0.5)
        keys = mixed[:, LANES : 2 * LANES]
        values = mixed[:, 2 * LANES :] + bias_v
        QS[rows] = queries.astype(BF16)
        KK[rows] = keys.astype(BF16)
        VV[rows] = values.astype(BF16)
        QT[:, rows] = queries.T.astype(BF16)
        KT[:, rows] = keys.T.astype(BF16)
        VT[:, rows] = values.T.astype(BF16)


    def pair_lanes(lp):
        return (pl.ds(pl.multiple_of(lp * LANES, LANES), LANES), pl.ds(pl.multiple_of(512 + lp * LANES, LANES), LANES))

    def cat_lanes(ref, lp):
        first, second = pair_lanes(lp)
        return jnp.concatenate([ref[:, first], ref[:, second]], axis=1)

    def cat_rows(ref, lp):
        return jnp.concatenate([ref[lp], ref[4 + lp]], axis=0)

    class Scatter:
        def __init__(self, part, chip, number, before=None, tree=True):
            self.part, self.chip, self.number, self.before, self.tree = part, chip, number, before, tree
            self.near, self.far = slots(4), slots(8)

        def emit(self, m, value):
            if self.before is not None:
                left(self.part.at[m, 1 - c], self.before.near + m)
            low = value.astype(BF16)
            self.part[m, 0] = low[:ROWS]
            self.part[m, 1] = low[ROWS:]
            send(self.part.at[m, 1 - c], SB.at[self.number, m], dev(dc=1), self.near + m)

        def pieces(self, m):
            if self.tree and m > 1:
                return ((pl.ds(0, 64), self.far + m), (pl.ds(64, 64), self.far + 4 + m))
            return ((pl.ds(0, ROWS), self.far + m),)

        def chip_left(self, m):
            for rows, sem in self.pieces(m):
                left(self.chip.at[m, rows], sem)

        def reduce(self, m):
            arrive(SB.at[self.number, m], self.near + m)
            if m == 0:
                return
            if self.before is not None:
                self.before.chip_left(m)
            for k, (rows, sem) in enumerate(self.pieces(m)):
                total = self.part[m, c, rows].astype(F32) + SB[self.number, m, rows].astype(F32)
                if self.tree and m == 2:
                    across = RV.at[self.number, 3, rows]
                    arrive(across, self.pieces(3)[k][1])
                    total += across[...].astype(F32)
                self.chip[m, rows] = total.astype(BF16)
                device = dev(dl=1) if self.tree and m == 3 else dev(dl=m)
                send(self.chip.at[m, rows], RV.at[self.number, m, rows], device, sem)

        def finish(self):
            for m in (1, 2) if self.tree else (1, 2, 3):
                for rows, sem in self.pieces(m):
                    arrive(RV.at[self.number, m, rows], sem)

        def rows(self, rows):
            total = self.part[0, c, rows].astype(F32) + SB[self.number, 0, rows].astype(F32)
            for m in (1, 2) if self.tree else (1, 2, 3):
                total += RV[self.number, m, rows].astype(F32)
            return total

        def close(self):
            for m in range(4):
                left(self.part.at[m, 1 - c], self.near + m)
                if m:
                    self.chip_left(m)

    head_rows = lax.broadcasted_iota(jnp.int32, (LANES, 256), 0)
    head_lanes = lax.broadcasted_iota(jnp.int32, (256, LANES), 1)

    def only_rows(value, h):
        return jnp.where((head_rows >= h * 64) & (head_rows < (h + 1) * 64), value, jnp.zeros_like(value))

    def only_lanes(value, h):
        return jnp.where((head_lanes >= h * 64) & (head_lanes < (h + 1) * 64), value, jnp.zeros_like(value))

    scatter_a = Scatter(PA, CS, 0)
    attend_order = (3, 1, 2, 0)
    for k, m in enumerate(attend_order):
        lp = flip_l(m)
        queries_t = cat_lanes(QT, lp)
        seg_q = jnp.concatenate([SG[lp, 0:1, :], SG[4 + lp, 0:1, :]], axis=1)
        for h in range(2):
            masked_t = only_rows(queries_t.astype(F32), h).astype(BF16)
            top = jnp.full((8, 256), NEGATIVE, F32)
            for i in range(8):
                rows = pl.ds(i * ROWS, ROWS)
                value = dot(KK[rows], masked_t)
                code = CODE[i]
                allowed = jnp.concatenate([code, code], axis=1) == seg_q
                value = jnp.where(allowed, value, NEGATIVE)
                SC[h, rows] = value
                top = jnp.maximum(top, jnp.max(value.reshape(16, 8, 256), axis=0))
            top = jnp.max(top, axis=0, keepdims=True)
            total = jnp.zeros((8, 256), F32)
            for i in range(8):
                rows = pl.ds(i * ROWS, ROWS)
                value = jnp.exp(SC[h, rows] - top)
                PT[m, h, rows] = value.astype(BF16)
                total = total + jnp.sum(value.reshape(16, 8, 256), axis=0)
            inverse = 1.0 / jnp.sum(total, axis=0, keepdims=True)
            INV[m, h] = jnp.broadcast_to(inverse, (8, 256))
            OT[m, h * 64 : (h + 1) * 64] = dot(VT[h * 64 : (h + 1) * 64, :], PT[m, h]) * inverse
            if k and h == 0:
                scatter_a.reduce(attend_order[k - 1])
            if k == 1 and h == 1:
                spread_d.start_z()
            if k == 2 and h == 0:
                gather_g.forward(2)
            if k == 3 and h == 1:
                gather_g.forward(1)
        joined = OT[m]
        OL[m] = joined.astype(BF16)
        scatter_a.emit(m, dot(joined.T.astype(BF16), WO[...].reshape(LANES, D)))
    spread_i.forward()
    scatter_a.reduce(0)
    scatter_a.finish()

    gain2, shift2, bias_o = PV[5:6, :], PV[6:7, :], PV[4:5, :]
    for r in range(4):
        rows = pl.ds(r * 32, 32)
        residual = X[j, rows].astype(F32) + scatter_a.rows(rows) + bias_o
        XO[rows] = residual
        normal, root, value = norm_rows(residual, gain2, shift2)
        N2F[rows] = normal
        RS_[rows] = jnp.broadcast_to(root, (32, LANES))
        N2[j, rows] = value.astype(BF16)
    gather_n = Gather(N2)
    gather_n.begin()

    spread_i.finish()
    for i in range(32):
        tt, jj = shard_place(i)
        for ch in range(4):
            WI[i * 32 : (i + 1) * 32, ch * LANES : (ch + 1) * LANES] = RI[tt, jj, ch]
    pick = lax.broadcasted_iota(jnp.int32, (16, LANES), 0) == 8 + l
    bias_in = jnp.concatenate(
        [
            jnp.sum(jnp.where(pick, FULL[(ch // 2) * 4 + c * 2 + ch % 2], 0.0), axis=0, keepdims=True)
            for ch in range(4)
        ],
        axis=1,
    )
    scatter_m = Scatter(PA, CS, 1, scatter_a, tree=False)
    scatter_b = Scatter(PB, CSB, 2)
    BG[0:1] = jnp.zeros((1, 512), F32)

    def hidden_part(m):
        lp = flip_l(m)
        first, second = pair_lanes(lp)
        hidden = dot(cat_rows(N2, lp), WI[...]) + bias_in
        phi_cap = 0.5 * (1.0 + lax.erf(hidden * 0.7071067811865476))
        phi = jnp.exp(-0.5 * hidden * hidden) * 0.3989422804014327
        act = hidden * phi_cap
        GA[m] = phi_cap + hidden * phi
        HA[m] = act.astype(BF16)
        act_t = act.T.astype(BF16)
        HAT[:, first] = act_t[:, :ROWS]
        HAT[:, second] = act_t[:, ROWS:]

    def hidden_back(m):
        lp = flip_l(m)
        grad_act = dot_nt(cat_rows(GM, lp), WD[...].reshape(512, D))
        grad_pre = (grad_act * GA[m]).astype(BF16)
        GP[lp] = grad_pre[:ROWS]
        GP[4 + lp] = grad_pre[ROWS:]
        BG[0:1] += jnp.sum(grad_pre.astype(F32), axis=0, keepdims=True)
        scatter_m.emit(m, dot_nt(grad_pre, WI[...]))

    gather_n.sibling(0)
    hidden_part(0)
    spread_d.forward()
    gather_n.forward(2)
    gather_n.forward(1)
    gather_g.forward(3)
    gather_g.sibling(0)
    spread_d.finish()
    hidden_back(0)
    gather_n.sibling(2)
    hidden_part(1)
    gather_g.sibling(2)
    hidden_back(1)
    scatter_m.reduce(0)
    gather_n.sibling(1)
    hidden_part(2)
    gather_g.sibling(1)
    hidden_back(2)
    gather_n.forward(3)
    scatter_m.reduce(1)
    gather_n.sibling(3)
    hidden_part(3)
    gather_g.sibling(3)
    scatter_m.reduce(2)
    hidden_back(3)
    scatter_m.reduce(3)

    class Total:
        def __init__(self, part, from_x, middle, from_z):
            self.part, self.from_x, self.middle, self.from_z = part, from_x, middle, from_z
            self.sem = slots(3)

        def start_cross(self):
            push(self.part.at[(1 - x) * 2 + 1 - zh], self.from_x.at[1 - zh], dev(dx=1), self.sem)

        def start_keep(self):
            push(self.part.at[(1 - x) * 2 + zh], self.from_x.at[zh], dev(dx=1), self.sem + 2)

        def second(self):
            arrive(self.from_x.at[1 - zh], self.sem)
            self.middle[...] = (
                self.part[x * 2 + 1 - zh].astype(F32) + self.from_x[1 - zh].astype(F32)
            ).astype(BF16)
            push(self.middle, self.from_z, dev(dzh=1), self.sem + 1)

        def result(self):
            arrive(self.from_x.at[zh], self.sem + 2)
            arrive(self.from_z, self.sem + 1)
            return self.part[t].astype(F32) + self.from_x[zh].astype(F32) + self.from_z[...].astype(F32)

    total_d = Total(GD, XD, HD, ZD)
    total_i = Total(GI, XI, HI, ZI)
    total_q = [Total(GQ.at[ch], XQ.at[ch], HQ.at[ch], ZQ.at[ch]) for ch in range(3)]
    for ch in range(4):
        GD[ch] = dot(HAT[ch * LANES : (ch + 1) * LANES, :], GM[...].reshape(8 * ROWS, D)).astype(BF16)
    total_d.start_cross()
    all_pre = GP[...].reshape(8 * ROWS, 512)
    for blk in range(8):
        product = dot_tn(N2[:, :, blk * LANES : (blk + 1) * LANES].reshape(8 * ROWS, LANES), all_pre).astype(BF16)
        for r in range(4):
            tt, jj = shard_place(blk * 4 + r)
            for ch in range(4):
                GI[tt, jj, ch] = product[r * 32 : (r + 1) * 32, ch * LANES : (ch + 1) * LANES]
    total_i.start_cross()
    total_d.start_keep()
    total_i.start_keep()

    def norm_back(grad, normal, root, gain):
        scaled = grad * gain
        return root * (scaled - jnp.mean(scaled, axis=-1, keepdims=True)
                       - normal * jnp.mean(scaled * normal, axis=-1, keepdims=True))

    def forward_out(m):
        scatter_b.emit(m, dot(HA[m], WD[...].reshape(512, D)))

    for m in attend_order:
        forward_out(m)
    scatter_m.finish()
    sums = [jnp.zeros((1, D), F32) for _ in range(4)]
    for r in range(4):
        rows = pl.ds(r * 32, 32)
        grad = scatter_m.rows(rows)
        normal = N2F[rows]
        top_grad = GM[j, rows].astype(F32)
        grad_residual = top_grad + norm_back(grad, normal, RS_[rows][:, 0:1], gain2)
        low = grad_residual.astype(BF16)
        GB[j, rows] = low
        N2F[rows] = grad_residual
        for i, value in enumerate((grad * normal, grad, low.astype(F32), top_grad)):
            sums[i] += jnp.sum(value, axis=0, keepdims=True)
    vectors = {5: sums[0], 6: sums[1], 4: sums[2], 7: sums[3]}
    gather_b = Gather(GB)
    gather_b.begin()

    DK[...] = jnp.zeros_like(DK)
    DV[...] = jnp.zeros_like(DV)
    GOF[...] = jnp.zeros_like(GOF)

    def attend_back(m):
        lp = flip_l(m)
        first, second = pair_lanes(lp)
        branch = cat_rows(GB, lp)
        grad_att = dot_nt(branch, WO[...].reshape(LANES, D)).astype(BF16).astype(F32)
        GOF[...] += dot(OL[m], branch)
        grad_att_t = grad_att.T
        both = grad_att_t * OT[m]
        queries = jnp.concatenate([QS[first], QS[second]], axis=0).astype(F32)
        for h in range(2):
            inverse = INV[m, h][0:1]
            delta = jnp.sum(both[h * 64 : (h + 1) * 64], axis=0, keepdims=True) * inverse
            scaled_t = only_rows(grad_att_t * inverse, h)
            scaled_low_t = scaled_t.astype(BF16)
            scaled_low = scaled_t.T.astype(BF16)
            queries_h = only_lanes(queries, h).astype(BF16)
            for i in range(8):
                rows = pl.ds(i * ROWS, ROWS)
                probs = PT[m, h, rows]
                value = dot(VV[rows], scaled_low_t)
                grad_scores = (probs.astype(F32) * (value - delta)).astype(BF16)
                DV[rows] += dot(probs, scaled_low)
                DK[rows] += dot(grad_scores, queries_h)
                PT[m, h, rows] = grad_scores
            DQ[h * 64 : (h + 1) * 64, :] = dot(KT[h * 64 : (h + 1) * 64, :], PT[m, h]) * (HEAD_DIM ** -0.5)
        dq_rows = DQ[...].T.astype(BF16)
        GMX[lp, :, 0:LANES] = dq_rows[:ROWS]
        GMX[4 + lp, :, 0:LANES] = dq_rows[ROWS:]

    total_d.second()
    gather_b.sibling(0)
    attend_back(0)
    gather_b.forward(2)
    gather_b.forward(1)
    scatter_b.reduce(3)
    gather_b.sibling(2)
    attend_back(1)
    total_i.second()
    gather_b.sibling(1)
    attend_back(2)
    gather_b.forward(3)
    scatter_b.reduce(1)
    scatter_b.reduce(0)
    gather_b.sibling(3)
    attend_back(3)
    scatter_b.reduce(2)

    for blk in range(8):
        rows = pl.ds(blk * ROWS, ROWS)
        GMX[blk, :, LANES : 2 * LANES] = DK[rows].astype(BF16)
        GMX[blk, :, 2 * LANES :] = DV[rows].astype(BF16)
    all_mixed = GMX[...].reshape(8 * ROWS, 3 * LANES)
    scatter_n = Scatter(PA, CS, 3, scatter_m)

    def back_out(m):
        scatter_n.emit(m, dot_nt(cat_rows(GMX, flip_l(m)), WQ[...]))

    def joint_grad(blk):
        product = dot_tn(N1[:, :, blk * LANES : (blk + 1) * LANES].reshape(8 * ROWS, LANES), all_mixed).astype(BF16)
        for r in range(4):
            tt, jj = shard_place(blk * 4 + r)
            for ch in range(3):
                GQ[ch, tt, jj] = product[r * 32 : (r + 1) * 32, ch * LANES : (ch + 1) * LANES]

    for blk in range(8):
        joint_grad(blk)
    for ch in range(3):
        total_q[ch].start_cross()
    for ch in range(3):
        total_q[ch].start_keep()

    back_out(3)
    back_out(1)
    scatter_n.reduce(3)
    back_out(2)
    scatter_n.reduce(1)
    back_out(0)
    GO[...] = GOF[...].astype(BF16)
    sem_go, sem_gs = slots(4), slots(4)

    @pl.when(x != c)
    def _():
        send(GO, XGO.at[0], dev(dx=1), sem_go)

    scatter_n.reduce(0)

    for ch in range(3):
        total_q[ch].second()
    sums = [jnp.zeros((1, D), F32) for _ in range(2)]
    for m in range(4):
        lp = flip_l(m)
        for half in range(2):
            value = PA[m, half].astype(F32)
            sums[0] += jnp.sum(value * N0[half * 4 + lp].astype(F32), axis=0, keepdims=True)
            sums[1] += jnp.sum(value, axis=0, keepdims=True)
    vectors[0], vectors[1] = sums
    scatter_n.reduce(2)
    mixed_sums = jnp.sum(all_mixed.astype(F32), axis=0, keepdims=True)
    for q in range(8):
        VG[q] = jnp.zeros((16, LANES), F32)
        for p in (0, 1, 4, 5, 6, 7):
            VG[q, p : p + 1] = vectors[p][:, q * LANES : (q + 1) * LANES]
        for p, ch in ((2, 0), (3, 2)):
            VG[q, p : p + 1] = jnp.where(own_pair == q, mixed_sums[:, ch * LANES : (ch + 1) * LANES], 0.0)
        ch = (q // 4) * 2 + q % 2
        for r in range(4):
            here = jnp.logical_and(c == (q // 2) % 2, l == r)
            VG[q, 8 + r : 9 + r] = jnp.where(here, BG[0:1, ch * LANES : (ch + 1) * LANES], 0.0)
    sem_v1, sem_v2 = slots(8), slots(4)
    for dx, dc, dzh in line_masks:
        mask = dx * 4 + dc * 2 + dzh
        push(VG.at[flip(x, dx) * 4 + flip(c, dc) * 2 + flip(zh, dzh)], VR.at[mask], dev(dx=dx, dc=dc, dzh=dzh), sem_v1 + mask)

    @pl.when(x == c)
    def _():
        arrive(XGO.at[0], sem_go)
        GOF[...] += XGO[0].astype(F32)

    @pl.when(root_mask == 1)
    def _():
        GO[...] = GOF[...].astype(BF16)
        send(GO, XGO.at[1], dev(dzh=1), sem_go + 1)


    bias_d = PV[7:8, :]
    sem_out, sem_in = slots(), slots()
    scatter_b.finish()
    for r in range(4):
        rows = pl.ds(r * 32, 32)
        BO[rows] = (XO[rows] + scatter_b.rows(rows) + bias_d).astype(BF16)
    put_block = move(BO, out_block.at[0], 6)

    @pl.when(native)
    def _():
        put_block.start()

    @pl.when(foreign)
    def _():
        send(BO, out_block.at[0], partner, sem_out)

    TD[...] = total_d.result().astype(BF16)
    put_d = move(TD, out_d, 7)
    put_d.start()
    TI[...] = total_i.result().astype(BF16)
    sem_ti, sem_tq = slots(8), slots(8 * 3)
    for dc, dl in group_masks:
        push(TI.at[group(dc, dl)], out_i.at[j], dev(dc=dc, dl=dl), sem_ti + dc * 4 + dl)
    put_i = move(TI.at[j], out_i.at[j], 8)
    put_i.start()

    slab = VG[q_own]
    for dx, dc, dzh in line_masks:
        mask = dx * 4 + dc * 2 + dzh
        arrive(VR.at[mask], sem_v1 + mask)
        slab += VR[mask]
    SL[...] = slab
    for dl in (1, 2, 3):
        push(SL, SLR.at[dl], dev(dl=dl), sem_v2 + dl)

    put_o = move(TGO.at[l], out_o, 10)

    @pl.when(is_root)
    def _():
        arrive(XGO.at[1], sem_go + 1)
        TGO[...] = (GOF[...] + XGO[1].astype(F32)).astype(BF16).reshape(4, 32, D)
        for slot in range(4):
            mine = jnp.logical_and(y == c, l == slot)

            @pl.when(mine)
            def _():
                put_o.start()

            @pl.when(jnp.logical_not(mine))
            def _():
                send(TGO.at[slot], out_o, (x * 2 + y, zh * 4 + slot), sem_gs + slot)

    scatter_n.finish()
    for r in range(4):
        rows = pl.ds(r * 32, 32)
        grad = scatter_n.rows(rows)
        normal, root, _ = norm_rows(X[j, rows].astype(F32), gain1, shift1)
        BI[rows] = (N2F[rows] + norm_back(grad, normal, root, gain1)).astype(BF16)
    put_input = move(BI, out_input.at[0], 9)

    @pl.when(native)
    def _():
        put_input.start()

    @pl.when(foreign)
    def _():
        send(BI, out_input.at[0], partner, sem_in)

    for ch in range(3):
        TQ[ch] = total_q[ch].result().astype(BF16)
        for dc, dl in group_masks:
            push(TQ.at[ch, group(dc, dl)], out_q.at[ch, j], dev(dc=dc, dl=dl), sem_tq + ch * 8 + dc * 4 + dl)
    put_q = [move(TQ.at[ch, j], out_q.at[ch, j], 11 + ch) for ch in range(3)]
    for ch in range(3):
        put_q[ch].start()

    for dl in (1, 2, 3):
        arrive(SLR.at[dl], sem_v2 + dl)
        slab += SLR[dl]
    SLF[...] = slab
    put_small = move(SLF, out_small, 14)
    put_small.start()

    for dc, dl in group_masks:
        arrive(out_i.at[group(dc, dl)], sem_ti + dc * 4 + dl)
        for ch in range(3):
            arrive(out_q.at[ch, group(dc, dl)], sem_tq + ch * 8 + dc * 4 + dl)

    put_d.wait()
    put_i.wait()
    put_small.wait()
    for ch in range(3):
        put_q[ch].wait()

    @pl.when(native)
    def _():
        put_block.wait()
        put_input.wait()

    @pl.when(foreign)
    def _():
        left(SGI, sem_ps)
        left(xin.at[0], sem_px)
        left(cin.at[0], sem_pc)
        left(BO, sem_out)
        left(BI, sem_in)
        arrive(out_block.at[0], sem_out)
        arrive(out_input.at[0], sem_in)

    @pl.when(to_self)
    def _():
        put_o.wait()

    @pl.when(jnp.logical_not(to_self))
    def _():
        left(wo, sem_wo + l)
        arrive(out_o, sem_gs + l)

    @pl.when(x != c)
    def _():
        left(GO, sem_go)

    @pl.when(root_mask == 1)
    def _():
        left(GO, sem_go + 1)

    @pl.when(root_mask == 1)
    def _():
        left(WO, sem_wt + 3)

    @pl.when(is_root)
    def _():
        for mask in (1, 2):
            left(WO, sem_wt + mask)
        for slot in range(4):
            @pl.when(jnp.logical_not(jnp.logical_and(y == c, l == slot)))
            def _():
                left(TGO.at[slot], sem_gs + slot)

    scatter_n.close()
    scatter_b.close()
    for k in (1, 2):
        left(X.at[j], gather_x.far + k)
    left(X.at[j], gather_x.near)
    for copy in pending:
        copy.wait_send()


def fused_scratch():
    def v(*shape):
        return pltpu.VMEM(shape, BF16)

    def f(*shape):
        return pltpu.VMEM(shape, F32)

    blocks = (8, ROWS, D)
    return [
        v(*blocks), v(*blocks), v(*blocks), v(*blocks), v(*blocks), v(*blocks),
        f(8, LANES), f(8, 8, LANES), f(16, LANES), f(4, 16, LANES), f(8, 16, LANES), f(16, D),
        v(32, 3 * D), v(8, 3, 32, LANES), v(3, 4, 8, 32, LANES), v(D, 3 * LANES), v(4, 32, D),
        v(32, 4 * D), v(8, 4, 32, LANES), v(4, 8, 4, 32, LANES), v(D, 512), v(4, LANES, D),
        v(D, LANES), v(D, LANES), v(D, LANES), v(LANES, D), v(LANES, D), v(LANES, D),
        f(8, ROWS, LANES), f(2, D, 256), v(4, 2, D, 256), f(4, 2, 8, 256),
        f(4, LANES, 256), v(4, LANES, 256),
        v(4, 2, ROWS, D), v(4, ROWS, D), v(4, 2, ROWS, D), v(4, ROWS, D),
        v(4, 4, ROWS, D), v(4, 4, ROWS, D), f(ROWS, D), f(ROWS, D),
        v(512, D), v(4, 256, 512), v(8, ROWS, 512), f(4, 256, 512),
        f(D, LANES), f(D, LANES), f(LANES, 256), v(8, ROWS, 3 * LANES),
        v(3, 4, 8, 32, LANES), v(4, 8, 4, 32, LANES), v(4, LANES, D),
        v(3, 2, 8, 32, LANES), v(2, 8, 4, 32, LANES), v(2, LANES, D),
        v(3, 8, 32, LANES), v(8, 4, 32, LANES), v(LANES, D),
        v(3, 8, 32, LANES), v(8, 4, 32, LANES), v(LANES, D),
        v(3, 8, 32, LANES), v(8, 4, 32, LANES), v(LANES, D),
        v(LANES, D), f(LANES, D), v(4, LANES, D), v(4, 32, D),
        f(8, 16, LANES), f(8, 16, LANES), f(16, LANES), f(4, 16, LANES), f(16, LANES),
        f(ROWS, LANES), f(8, 512), v(ROWS, D), v(ROWS, D),
        pltpu.SemaphoreType.DMA((COPIES,)),
        pltpu.SemaphoreType.DMA((COPIES,)),
        pltpu.SemaphoreType.DMA((16,)),
    ]


def finish_kernel(
    block, grad_in, grad_q, grad_o, grad_i, grad_d, small,
    out_block, out_input, o0, o1, out_q, o2, o3, out_o, o4, o5, o6, out_i, ob, out_d, o7,
):
    place = lax.rem(lax.axis_index("band"), 4)
    out_block[...] = block[...]
    out_input[...] = grad_in[...]
    for jj in range(8):
        for ch in range(3):
            out_q[:, ch * D + pair_of(jj) * LANES : ch * D + (pair_of(jj) + 1) * LANES] = grad_q[ch, jj].astype(F32)
        for ch in range(4):
            flat = flat_column(jj, ch)
            out_i[:, flat * LANES : (flat + 1) * LANES] = grad_i[jj, ch].astype(F32)
    out_o[...] = grad_o[...].astype(F32)
    out_d[...] = grad_d[...].astype(F32)
    slab = small[...]
    mine = jnp.zeros((16, 32), F32)
    for k in range(4):
        mine = jnp.where(place == k, slab[:, k * 32 : (k + 1) * 32], mine)
    for p, ref in enumerate((o0, o1, o2, o3, o4, o5, o6, o7)):
        ref[...] = mine[p : p + 1].reshape(32)
    pick = lax.broadcasted_iota(jnp.int32, (16, LANES), 0) == 8 + place
    ob[...] = jnp.sum(jnp.where(pick, slab, 0.0), axis=0, keepdims=True).reshape(LANES)


def fused_shards(
    block_in,
    attention_norm_gain,
    attention_norm_bias,
    query_key_value,
    query_bias,
    value_bias,
    output_weight,
    output_bias,
    mlp_norm_gain,
    mlp_norm_bias,
    mlp_in_weight,
    mlp_in_bias,
    mlp_out_weight,
    mlp_out_bias,
    cotangent,
    segment_ids,
    sub_lengths,
):
    vmem = pl.BlockSpec(memory_space=pltpu.VMEM)
    hbm = pl.BlockSpec(memory_space=pl.ANY)

    def shape(dims, kind):
        return jax.ShapeDtypeStruct(dims, kind)

    parts = pl.pallas_call(
        functools.partial(fused_kernel, COPIES),
        out_shape=(
            shape((1, ROWS, D), BF16),
            shape((1, ROWS, D), BF16),
            shape((3, 8, 32, LANES), BF16),
            shape((32, D), BF16),
            shape((8, 4, 32, LANES), BF16),
            shape((LANES, D), BF16),
            shape((16, LANES), F32),
        ),
        in_specs=[hbm, hbm, vmem, vmem, hbm, hbm, hbm, hbm] + [vmem] * 9,
        out_specs=(hbm,) * 7,
        scratch_shapes=fused_scratch(),
        compiler_params=pltpu.CompilerParams(
            collective_id=0, has_side_effects=True, vmem_limit_bytes=63 * 2**20
        ),
    )(
        block_in, cotangent, segment_ids, sub_lengths,
        query_key_value, output_weight, mlp_in_weight, mlp_out_weight,
        attention_norm_gain, attention_norm_bias, query_bias, value_bias,
        output_bias, mlp_norm_gain, mlp_norm_bias, mlp_out_bias, mlp_in_bias,
    )
    vector = shape((32,), F32)
    return pl.pallas_call(
        finish_kernel,
        out_shape=(
            shape((1, ROWS, D), BF16), shape((1, ROWS, D), BF16), vector, vector,
            shape((32, 3 * D), F32), vector, vector, shape((32, D), F32), vector, vector, vector,
            shape((32, 4 * D), F32), shape((LANES,), F32), shape((LANES, D), F32), vector,
        ),
        in_specs=[vmem] * 7,
        out_specs=(vmem,) * 15,
    )(*parts)


def solution(mesh):
    small_slice = dict(mesh.shape) == {"seq": 4, "band": 8}
    return jax.shard_map(
        fused_shards if small_slice else shards,
        mesh=mesh,
        in_specs=(
            P("seq", "band", None),
            P(("seq", "band")),
            P(("seq", "band")),
            P(("seq", "band"), None),
            P(("seq", "band")),
            P(("seq", "band")),
            P(("seq", "band"), None),
            P(("seq", "band")),
            P(("seq", "band")),
            P(("seq", "band")),
            P(("seq", "band"), None),
            P(("seq", "band")),
            P(("seq", "band"), None),
            P(("seq", "band")),
            P("seq", "band", None),
            P("seq", "band"),
            P("seq", None),
        ),
        out_specs=(
            P("seq", "band", None),
            P("seq", "band", None),
            P(("seq", "band")),
            P(("seq", "band")),
            P(("seq", "band"), None),
            P(("seq", "band")),
            P(("seq", "band")),
            P(("seq", "band"), None),
            P(("seq", "band")),
            P(("seq", "band")),
            P(("seq", "band")),
            P(("seq", "band"), None),
            P(("seq", "band")),
            P(("seq", "band"), None),
            P(("seq", "band")),
        ),
        check_vma=False,
    )
```

```python
import functools
import math

import jax
import jax.numpy as jnp
from jax import lax
from jax.experimental import pallas as pl
from jax.experimental.pallas import tpu as pltpu
from jax.sharding import PartitionSpec as P

D = 1024
HEADS = 16
HEAD_DIM = 64
SUBGRIDS = 8


EPSILON = 1e-05
NEGATIVE = -1e30


def prefix(part, axis, combine, identity):
    place = lax.axis_index(axis)
    gathered = lax.all_gather(part, axis)
    state = jnp.zeros_like(part) + jnp.asarray(identity, part.dtype)

    def one(lap, state):
        return combine(state, lax.dynamic_index_in_dim(gathered, lap, 0, False))

    return lax.fori_loop(0, place, one, state)


def layer_norm(values_in, norm_gain, norm_shift):
    average = jnp.mean(values_in, axis=-1, keepdims=True)
    centered = values_in - average
    variance = jnp.mean(centered * centered, axis=-1, keepdims=True)
    return centered * lax.rsqrt(variance + EPSILON) * norm_gain + norm_shift


def gelu_exact(values_in):
    return jax.nn.gelu(values_in, approximate=False)


def add_counts(first_part, second_part):
    return first_part + second_part


def block_scores(query_part, key_part, seg_part, code_part, scale_factor):
    scores = (
        jnp.einsum("qhe,khe->hqk", query_part, key_part, preferred_element_type=jnp.float32)
        * scale_factor
    )
    allowed = (seg_part[:, None] == code_part[None, :])[None]
    return (jnp.where(allowed, scores, NEGATIVE), allowed)


def split_blocks(array_in, block_rows):
    return array_in.reshape((array_in.shape[0] // block_rows, block_rows) + array_in.shape[1:])


def shards(
    block_in,
    attention_norm_gain,
    attention_norm_bias,
    query_key_value,
    query_bias,
    value_bias,
    output_weight,
    output_bias,
    mlp_norm_gain,
    mlp_norm_bias,
    mlp_in_weight,
    mlp_in_bias,
    mlp_out_weight,
    mlp_out_bias,
    cotangent,
    segment_ids,
    sub_lengths,
):
    float_type = jnp.float32
    half_type = jnp.bfloat16
    rows_local = block_in.shape[1]
    seq_length = rows_local * lax.axis_size("band")
    scale_factor = HEAD_DIM ** (-0.5)
    block_rows = math.gcd(seq_length, 1024)
    seg_local = segment_ids[0]
    labels = jnp.arange(SUBGRIDS, dtype=jnp.int32)
    onehot_ids = (seg_local[:, None] == labels[None, :]).astype(jnp.int32)
    earlier_counts = prefix(
        jnp.sum(onehot_ids, axis=0), "band", add_counts, jnp.zeros((SUBGRIDS,), jnp.int32)
    )
    slots = jnp.arange(rows_local)
    earlier = (slots[None, :] < slots[:, None]).astype(float_type)
    before = (
        jnp.dot(earlier, onehot_ids.astype(float_type), precision=lax.Precision.HIGHEST).astype(
            jnp.int32
        )
        + earlier_counts[None, :]
    )
    patch_rank = jnp.sum(before * onehot_ids, axis=1)
    limits = jnp.sum(onehot_ids * sub_lengths[0][None, :], axis=1)
    realness = patch_rank < limits
    key_codes = jnp.where(realness, seg_local, -1)
    gathered = (
        lax.all_gather(attention_norm_gain, ("seq", "band"), axis=0, tiled=True),
        lax.all_gather(attention_norm_bias, ("seq", "band"), axis=0, tiled=True),
        lax.all_gather(query_key_value, ("seq", "band"), axis=0, tiled=True),
        lax.all_gather(query_bias, ("seq", "band"), axis=0, tiled=True),
        lax.all_gather(value_bias, ("seq", "band"), axis=0, tiled=True),
        lax.all_gather(output_weight, ("seq", "band"), axis=0, tiled=True),
        lax.all_gather(output_bias, ("seq", "band"), axis=0, tiled=True),
        lax.all_gather(mlp_norm_gain, ("seq", "band"), axis=0, tiled=True),
        lax.all_gather(mlp_norm_bias, ("seq", "band"), axis=0, tiled=True),
        lax.all_gather(mlp_in_weight, ("seq", "band"), axis=0, tiled=True),
        lax.all_gather(mlp_in_bias, ("seq", "band"), axis=0, tiled=True),
        lax.all_gather(mlp_out_weight, ("seq", "band"), axis=0, tiled=True),
        lax.all_gather(mlp_out_bias, ("seq", "band"), axis=0, tiled=True),
    )
    (
        gain_one,
        shift_one,
        joint_weight,
        bias_query,
        bias_value,
        proj_weight,
        proj_bias,
        gain_two,
        shift_two,
        up_weight,
        up_bias,
        down_weight,
        down_bias,
    ) = gathered
    inputs = block_in[0].astype(float_type)
    normed_float, norm_pull_one = jax.vjp(
        layer_norm, inputs, gain_one.astype(float_type), shift_one.astype(float_type)
    )
    normed_one = normed_float.astype(half_type)
    mixed_all = jnp.dot(normed_one, joint_weight, preferred_element_type=float_type)
    queries = (mixed_all[:, :D] + bias_query.astype(float_type)).astype(half_type)
    keys_local = mixed_all[:, D : 2 * D].astype(half_type)
    values_local = (mixed_all[:, 2 * D :] + bias_value.astype(float_type)).astype(half_type)
    keys_seq, values_seq, codes_seq = (
        lax.all_gather(keys_local, "band", axis=0, tiled=True),
        lax.all_gather(values_local, "band", axis=0, tiled=True),
        lax.all_gather(key_codes, "band", axis=0, tiled=True),
    )
    query_heads = queries.reshape(rows_local, HEADS, HEAD_DIM)
    key_blocks = split_blocks(keys_seq.reshape(seq_length, HEADS, HEAD_DIM), block_rows)
    value_blocks = split_blocks(values_seq.reshape(seq_length, HEADS, HEAD_DIM), block_rows)
    code_blocks = split_blocks(codes_seq, block_rows)

    def stats_step(running, block_items):
        top_now, total_now = running
        key_part, code_part = block_items
        scores, allowed = block_scores(query_heads, key_part, seg_local, code_part, scale_factor)
        top_new = jnp.maximum(top_now, jnp.max(scores, axis=-1))
        exp_terms = jnp.where(allowed, jnp.exp(scores - top_new[..., None]), 0.0)
        return (
            (top_new, total_now * jnp.exp(top_now - top_new) + jnp.sum(exp_terms, axis=-1)),
            None,
        )

    start_stats = (
        jnp.full((HEADS, rows_local), NEGATIVE, float_type),
        jnp.zeros((HEADS, rows_local), float_type),
    )
    (top_final, total_final), unused_stats = lax.scan(
        stats_step, start_stats, (key_blocks, code_blocks)
    )
    log_total = top_final + jnp.log(total_final)

    def value_step(accum_out, block_items):
        key_part, value_part, code_part = block_items
        scores, allowed = block_scores(query_heads, key_part, seg_local, code_part, scale_factor)
        soft_probs = jnp.where(allowed, jnp.exp(scores - log_total[..., None]), 0.0).astype(
            half_type
        )
        return (
            accum_out
            + jnp.einsum("hqk,khe->qhe", soft_probs, value_part, preferred_element_type=float_type),
            None,
        )

    attended, unused_values = lax.scan(
        value_step,
        jnp.zeros((rows_local, HEADS, HEAD_DIM), float_type),
        (key_blocks, value_blocks, code_blocks),
    )
    attended_low = attended.reshape(rows_local, D).astype(half_type)
    residual = (
        inputs
        + jnp.dot(attended_low, proj_weight, preferred_element_type=float_type)
        + proj_bias.astype(float_type)
    )
    normed_float_two, norm_pull_two = jax.vjp(
        layer_norm, residual, gain_two.astype(float_type), shift_two.astype(float_type)
    )
    normed_two = normed_float_two.astype(half_type)
    hidden_pre = jnp.dot(normed_two, up_weight, preferred_element_type=float_type) + up_bias.astype(
        float_type
    )
    hidden_value, gelu_pull = jax.vjp(gelu_exact, hidden_pre)
    hidden_act = hidden_value.astype(half_type)
    block_result = (
        residual
        + jnp.dot(hidden_act, down_weight, preferred_element_type=float_type)
        + down_bias.astype(float_type)
    )
    gathered_back = (
        lax.all_gather(attention_norm_gain, ("seq", "band"), axis=0, tiled=True),
        lax.all_gather(attention_norm_bias, ("seq", "band"), axis=0, tiled=True),
        lax.all_gather(query_key_value, ("seq", "band"), axis=0, tiled=True),
        lax.all_gather(query_bias, ("seq", "band"), axis=0, tiled=True),
        lax.all_gather(value_bias, ("seq", "band"), axis=0, tiled=True),
        lax.all_gather(output_weight, ("seq", "band"), axis=0, tiled=True),
        lax.all_gather(output_bias, ("seq", "band"), axis=0, tiled=True),
        lax.all_gather(mlp_norm_gain, ("seq", "band"), axis=0, tiled=True),
        lax.all_gather(mlp_norm_bias, ("seq", "band"), axis=0, tiled=True),
        lax.all_gather(mlp_in_weight, ("seq", "band"), axis=0, tiled=True),
        lax.all_gather(mlp_in_bias, ("seq", "band"), axis=0, tiled=True),
        lax.all_gather(mlp_out_weight, ("seq", "band"), axis=0, tiled=True),
        lax.all_gather(mlp_out_bias, ("seq", "band"), axis=0, tiled=True),
    )
    joint_back = gathered_back[2]
    proj_back = gathered_back[5]
    up_back = gathered_back[9]
    down_back = gathered_back[11]
    grad_out = cotangent[0].astype(float_type) * realness[:, None].astype(float_type)
    grad_mlp = grad_out.astype(half_type)
    grad_down_weight = jnp.einsum(
        "rf,rd->fd", hidden_act, grad_mlp, preferred_element_type=float_type
    )
    grad_down_bias = jnp.sum(grad_mlp.astype(float_type), axis=0)
    grad_act = jnp.einsum("rd,fd->rf", grad_mlp, down_back, preferred_element_type=float_type)
    grad_pre = gelu_pull(grad_act)[0].astype(half_type)
    grad_up_weight = jnp.einsum(
        "rd,rf->df", normed_two, grad_pre, preferred_element_type=float_type
    )
    grad_up_bias = jnp.sum(grad_pre.astype(float_type), axis=0)
    grad_normed_two = jnp.einsum("rf,df->rd", grad_pre, up_back, preferred_element_type=float_type)
    grad_resid_part, grad_gain_two, grad_shift_two = norm_pull_two(grad_normed_two)
    grad_residual = grad_out + grad_resid_part
    grad_branch = grad_residual.astype(half_type)
    grad_proj_weight = jnp.einsum(
        "rd,re->de", attended_low, grad_branch, preferred_element_type=float_type
    )
    grad_proj_bias = jnp.sum(grad_branch.astype(float_type), axis=0)
    grad_attended = jnp.einsum(
        "re,de->rd", grad_branch, proj_back, preferred_element_type=float_type
    ).astype(half_type)
    grad_heads = grad_attended.reshape(rows_local, HEADS, HEAD_DIM)
    row_delta = jnp.sum(grad_heads.astype(float_type) * attended, axis=-1).T
    keys_back = lax.all_gather(keys_local, "band", axis=0, tiled=True)
    values_back = lax.all_gather(values_local, "band", axis=0, tiled=True)
    codes_back = lax.all_gather(key_codes, "band", axis=0, tiled=True)
    key_back_blocks = split_blocks(keys_back.reshape(seq_length, HEADS, HEAD_DIM), block_rows)
    value_back_blocks = split_blocks(values_back.reshape(seq_length, HEADS, HEAD_DIM), block_rows)
    code_back_blocks = split_blocks(codes_back, block_rows)

    def key_step(query_accum, block_items):
        key_part, value_part, code_part = block_items
        scores, allowed = block_scores(query_heads, key_part, seg_local, code_part, scale_factor)
        soft_probs = jnp.where(allowed, jnp.exp(scores - log_total[..., None]), 0.0)
        grad_probs = jnp.einsum(
            "qhe,khe->hqk", grad_heads, value_part, preferred_element_type=float_type
        )
        grad_scores = (soft_probs * (grad_probs - row_delta[..., None])).astype(half_type)
        query_accum = query_accum + jnp.einsum(
            "hqk,khe->qhe", grad_scores, key_part, preferred_element_type=float_type
        )
        return (query_accum, None)

    query_total, joined_blocks = lax.scan(
        key_step,
        jnp.zeros((rows_local, HEADS, HEAD_DIM), float_type),
        (key_back_blocks, value_back_blocks, code_back_blocks),
    )
    grad_query = (query_total * scale_factor).reshape(rows_local, D)
    query_seq = lax.all_gather(queries, "band", axis=0, tiled=True)
    grad_seq = lax.all_gather(grad_attended, "band", axis=0, tiled=True)
    total_seq = lax.all_gather(log_total, "band", axis=1, tiled=True)
    delta_seq = lax.all_gather(row_delta, "band", axis=1, tiled=True)
    seg_seq = lax.all_gather(seg_local, "band", axis=0, tiled=True)
    block_count = seq_length // block_rows
    key_heads_local = keys_local.reshape(rows_local, HEADS, HEAD_DIM)
    value_heads_local = values_local.reshape(rows_local, HEADS, HEAD_DIM)

    def query_step(running, block_items):
        key_accum, value_accum = running
        query_part, grad_part, total_part, delta_part, seg_part = block_items
        scores, allowed = block_scores(
            query_part, key_heads_local, seg_part, key_codes, scale_factor
        )
        soft_probs = jnp.where(allowed, jnp.exp(scores - total_part[..., None]), 0.0)
        grad_probs = jnp.einsum(
            "qhe,khe->hqk", grad_part, value_heads_local, preferred_element_type=float_type
        )
        grad_scores = (soft_probs * (grad_probs - delta_part[..., None])).astype(half_type)
        key_accum = key_accum + jnp.einsum(
            "hqk,qhe->khe", grad_scores, query_part, preferred_element_type=float_type
        )
        value_accum = value_accum + jnp.einsum(
            "hqk,qhe->khe",
            soft_probs.astype(half_type),
            grad_part,
            preferred_element_type=float_type,
        )
        return ((key_accum, value_accum), None)

    zero_heads = jnp.zeros((rows_local, HEADS, HEAD_DIM), float_type)
    (key_total, value_total), query_blocks = lax.scan(
        query_step,
        (zero_heads, zero_heads),
        (
            split_blocks(query_seq.reshape(seq_length, HEADS, HEAD_DIM), block_rows),
            split_blocks(grad_seq.reshape(seq_length, HEADS, HEAD_DIM), block_rows),
            total_seq.reshape(HEADS, block_count, block_rows).transpose(1, 0, 2),
            delta_seq.reshape(HEADS, block_count, block_rows).transpose(1, 0, 2),
            split_blocks(seg_seq, block_rows),
        ),
    )
    grad_key = (key_total * scale_factor).reshape(rows_local, D)
    grad_value = value_total.reshape(rows_local, D)
    grad_query_low = grad_query.astype(half_type)
    grad_value_low = grad_value.astype(half_type)
    grad_mixed = jnp.concatenate(
        [grad_query_low, grad_key.astype(half_type), grad_value_low], axis=1
    )
    grad_joint_weight = jnp.einsum(
        "rd,rm->dm", normed_one, grad_mixed, preferred_element_type=float_type
    )
    grad_bias_query = jnp.sum(grad_query_low.astype(float_type), axis=0)
    grad_bias_value = jnp.sum(grad_value_low.astype(float_type), axis=0)
    grad_normed_one = jnp.einsum(
        "rm,dm->rd", grad_mixed, joint_back, preferred_element_type=float_type
    )
    grad_input_part, grad_gain_one, grad_shift_one = norm_pull_one(grad_normed_one)
    input_grad = (grad_residual + grad_input_part).astype(half_type)
    shard_grads = (
        lax.psum_scatter(grad_gain_one, ("seq", "band"), scatter_dimension=0, tiled=True),
        lax.psum_scatter(grad_shift_one, ("seq", "band"), scatter_dimension=0, tiled=True),
        lax.psum_scatter(grad_joint_weight, ("seq", "band"), scatter_dimension=0, tiled=True),
        lax.psum_scatter(grad_bias_query, ("seq", "band"), scatter_dimension=0, tiled=True),
        lax.psum_scatter(grad_bias_value, ("seq", "band"), scatter_dimension=0, tiled=True),
        lax.psum_scatter(grad_proj_weight, ("seq", "band"), scatter_dimension=0, tiled=True),
        lax.psum_scatter(grad_proj_bias, ("seq", "band"), scatter_dimension=0, tiled=True),
        lax.psum_scatter(grad_gain_two, ("seq", "band"), scatter_dimension=0, tiled=True),
        lax.psum_scatter(grad_shift_two, ("seq", "band"), scatter_dimension=0, tiled=True),
        lax.psum_scatter(grad_up_weight, ("seq", "band"), scatter_dimension=0, tiled=True),
        lax.psum_scatter(grad_up_bias, ("seq", "band"), scatter_dimension=0, tiled=True),
        lax.psum_scatter(grad_down_weight, ("seq", "band"), scatter_dimension=0, tiled=True),
        lax.psum_scatter(grad_down_bias, ("seq", "band"), scatter_dimension=0, tiled=True),
    )
    return (
        block_result.astype(half_type)[None],
        input_grad[None],
        shard_grads[0],
        shard_grads[1],
        shard_grads[2],
        shard_grads[3],
        shard_grads[4],
        shard_grads[5],
        shard_grads[6],
        shard_grads[7],
        shard_grads[8],
        shard_grads[9],
        shard_grads[10],
        shard_grads[11],
        shard_grads[12],
    )


F32 = jnp.float32
BF16 = jnp.bfloat16
MESH_ID = pl.DeviceIdType.MESH
ROWS = 128
LANES = 128
COPIES = 240


def dot(lhs, rhs):
    return jnp.dot(lhs, rhs, preferred_element_type=F32)


def dot_nt(lhs, rhs):
    return lax.dot_general(lhs, rhs, (((1,), (1,)), ((), ())), preferred_element_type=F32)


def dot_tn(lhs, rhs):
    return lax.dot_general(lhs, rhs, (((0,), (0,)), ((), ())), preferred_element_type=F32)


def pair_of(jj):
    return (jj // 4) * 4 + (jj % 2) * 2 + (jj // 2) % 2


def flat_column(jj, ch):
    return (ch // 2) * 16 + (jj // 4) * 8 + (ch % 2) * 4 + jj % 4


def shard_place(i):
    return (i // 16) * 2 + (i // 4) % 2, ((i // 8) % 2) * 4 + i % 4


def fused_kernel(copies, *refs):
    (
        xin, cin, seg_in, len_in, wq, wo, wi, wd,
        p0, p1, p2, p3, p4, p5, p6, p7, pb,
        out_block, out_input, out_q, out_o, out_i, out_d, out_small,
        X, N0, N1, N2, GM, GB, SGI, SG, PK, SP, FULL, PV,
        WQI, WSQ, RQ, WQ, WO, WII, WSI, RI, WI, WD,
        QS, KK, VV, QT, KT, VT, CODE, SC, PT, INV, OT, OL,
        PA, CS, PB, CSB, SB, RV, XO, N2F, HAT, HA, GP, GA,
        DK, DV, DQ, GMX,
        GQ, GI, GD, XQ, XI, XD, HQ, HI, HD, ZQ, ZI, ZD, TQ, TI, TD,
        GO, GOF, XGO, TGO,
        VG, VR, SL, SLR, SLF, RS_, BG, BO, BI,
        ssem, rsem, lsem,
    ) = refs
    s = lax.axis_index("seq")
    b = lax.axis_index("band")
    x, c = lax.div(s, 2), lax.rem(s, 2)
    zh, l = lax.div(b, 4), lax.rem(b, 4)
    zl, y = lax.div(l, 2), lax.rem(l, 2)
    t, j = x * 2 + zh, c * 4 + l

    def flip(v, d):
        return 1 - v if d else v

    def flip_l(d):
        return flip(zl, d // 2) * 2 + flip(y, d % 2)

    def dev(dx=0, dc=0, dzh=0, dl=0):
        return (flip(x, dx) * 2 + flip(c, dc), flip(zh, dzh) * 4 + flip_l(dl))

    roles = (l, flip_l(2), flip_l(1), flip_l(3))

    counter = [0]
    pending = []

    def slots(n=1):
        first = counter[0]
        counter[0] += n
        assert counter[0] <= copies
        return first

    def send(src, dst, device, sem):
        copy = pltpu.make_async_remote_copy(
            src_ref=src, dst_ref=dst, send_sem=ssem.at[sem], recv_sem=rsem.at[sem],
            device_id=device, device_id_type=MESH_ID)
        copy.start()
        return copy

    def push(src, dst, device, sem):
        copy = send(src, dst, device, sem)
        pending.append(copy)
        return copy

    def arrive(dst, sem):
        pltpu.make_async_remote_copy(
            src_ref=dst, dst_ref=dst, send_sem=ssem.at[sem], recv_sem=rsem.at[sem],
            device_id=dev(dc=1), device_id_type=MESH_ID).wait_recv()

    def left(src, sem):
        pltpu.make_async_remote_copy(
            src_ref=src, dst_ref=src, send_sem=ssem.at[sem], recv_sem=rsem.at[sem],
            device_id=dev(dc=1), device_id_type=MESH_ID).wait_send()

    def move(src, dst, sem):
        return pltpu.make_async_copy(src, dst, lsem.at[sem])

    group_masks = [(dc, dl) for dl in (3, 1, 2, 0) for dc in (0, 1) if (dc, dl) != (0, 0)]
    line_masks = [(dx, dc, dzh) for dx in (1, 0) for dc in (0, 1) for dzh in (1, 0) if dx + dc + dzh]

    def group(dc, dl):
        return flip(c, dc) * 4 + flip_l(dl)

    native = c == zh
    foreign = jnp.logical_not(native)
    partner = dev(dc=1, dzh=1)
    their_block = (1 - c) * 4 + l

    barrier = pltpu.get_barrier_semaphore()
    peers = [dict(dc=dc, dl=dl) for dc, dl in group_masks]
    peers += [dict(dx=a, dc=e, dzh=f) for a, e, f in line_masks if (a, e, f) != (0, 1, 0)]
    for peer in peers:
        pl.semaphore_signal(barrier, inc=1, device_id=dev(**peer), device_id_type=MESH_ID)
    get_q, get_i, get_d = move(wq, WQI, 0), move(wi, WII, 1), move(wd, WD.at[t], 2)
    get_x, get_c = move(xin.at[0], X.at[j], 3), move(cin.at[0], GM.at[j], 4)
    get_q.start()
    get_i.start()
    get_d.start()

    @pl.when(native)
    def _():
        get_x.start()
        get_c.start()

    lane_group = lax.broadcasted_iota(jnp.int32, (1, LANES), 1) // 32
    PK[...] = jnp.zeros_like(PK)
    for p, ref in enumerate((p0, p1, p2, p3, p4, p5, p6, p7)):
        value = ref[...].astype(F32).reshape(1, 32)
        PK[p : p + 1] = jnp.where(lane_group == l, jnp.concatenate([value] * 4, axis=1), 0.0)
    own_bias = pb[...].astype(F32).reshape(1, LANES)
    for r in range(4):
        PK[8 + r : 9 + r] = jnp.where(l == r, own_bias, jnp.zeros_like(own_bias))
    SGI[...] = jnp.zeros_like(SGI)
    SGI[0:1] = seg_in[...].astype(F32)
    SGI[1:2, 0:SUBGRIDS] = len_in[...].astype(F32)
    get_q.wait()
    for jj in range(8):
        for ch in range(3):
            WSQ[jj, ch] = WQI[:, ch * D + pair_of(jj) * LANES : ch * D + (pair_of(jj) + 1) * LANES]
    for ch in range(3):
        RQ[ch, t, j] = WSQ[j, ch]
    pl.semaphore_wait(barrier, len(peers))

    sem_px, sem_pc, sem_ps = slots(), slots(), slots()
    sem_wq, sem_s1 = slots(8), slots(4)
    for dl in (1, 2, 3):
        push(PK, SP.at[dl], dev(dl=dl), sem_s1 + dl)

    @pl.when(native)
    def _():
        SG[j] = SGI[...]

    @pl.when(foreign)
    def _():
        send(SGI, SG.at[their_block], partner, sem_ps)
        send(xin.at[0], X.at[their_block], partner, sem_px)

    for dc, dl in group_masks:
        push(WSQ.at[group(dc, dl)], RQ.at[:, t, j], dev(dc=dc, dl=dl), sem_wq + dc * 4 + dl)

    class Gather:
        def __init__(self, buf):
            self.buf, self.far, self.near = buf, slots(4), slots(4)

        def start(self):
            block = self.buf.at[j]
            copies_out = [
                send(block, block, dev(dc=1), self.near),
                send(block, block, (s, zh * 4 + roles[1]), self.far + 1),
                send(block, block, (s, zh * 4 + roles[2]), self.far + 2),
            ]
            return copies_out

        def begin(self):
            pending.extend(self.start())

        def forward(self, k):
            block = self.buf.at[c * 4 + roles[k]]
            arrive(block, self.far + k)
            if k == 1:
                push(block, block, (s, zh * 4 + roles[2]), self.far + 3)
            push(block, block, dev(dc=1), self.near + k)

        def sibling(self, k):
            arrive(self.buf.at[(1 - c) * 4 + roles[k]], self.near + k)

    gather_x = Gather(X)
    gather_g = Gather(GM)

    @pl.when(native)
    def _():
        get_x.wait()
        gather_x.start()

    sem_wo, sem_wt = slots(4), slots(4)
    own_pair = c * 4 + y * 2 + zl
    pair_l = zh * 2 + c
    to_self = jnp.logical_and(x == c, l == pair_l)
    is_root = jnp.logical_and(x == c, zh == zl)
    root_mask = jnp.abs(x - c) * 2 + jnp.abs(zh - zl)
    get_o = move(wo, WO.at[l], 5)

    @pl.when(to_self)
    def _():
        get_o.start()

    @pl.when(jnp.logical_not(to_self))
    def _():
        send(wo, WO.at[l], (x * 2 + x, zh * 4 + pair_l), sem_wo + l)

    q_own = x * 4 + c * 2 + zh
    slab = PK[...]
    for dl in (1, 2, 3):
        arrive(SP.at[dl], sem_s1 + dl)
        slab += SP[dl]
    FULL[q_own] = slab
    sem_s2 = slots(8)
    for dx, dc, dzh in line_masks:
        push(FULL.at[q_own], FULL.at[q_own], dev(dx=dx, dc=dc, dzh=dzh), sem_s2 + dx * 4 + dc * 2 + dzh)

    class Spread:
        def __init__(self, buf):
            self.buf, self.sem = buf, slots(3)

        def start_z(self, keep=True):
            block = self.buf.at[t]
            copy = send(block, block, dev(dzh=1), self.sem)
            if keep:
                pending.append(copy)

        def start_x(self):
            block = self.buf.at[t]
            push(block, block, dev(dx=1), self.sem + 1)

        def sent_z(self):
            left(self.buf.at[t], self.sem)

        def start(self):
            self.start_z()
            self.start_x()

        def forward(self):
            block = self.buf.at[x * 2 + 1 - zh]
            arrive(block, self.sem)
            push(block, block, dev(dx=1), self.sem + 2)

        def finish(self):
            arrive(self.buf.at[(1 - x) * 2 + zh], self.sem + 1)
            arrive(self.buf.at[(1 - x) * 2 + 1 - zh], self.sem + 2)

    spread_q = [Spread(RQ.at[ch]) for ch in range(3)]
    for dc, dl in group_masks:
        arrive(RQ.at[:, t, group(dc, dl)], sem_wq + dc * 4 + dl)
    for ch in range(3):
        spread_q[ch].start()

    sem_sg = slots(8)

    @pl.when(foreign)
    def _():
        arrive(SG.at[j], sem_ps)

    for dc, dl in group_masks:
        push(SG.at[j], SG.at[j], dev(dc=dc, dl=dl), sem_sg + dc * 4 + dl)
    @pl.when(foreign)
    def _():
        arrive(X.at[j], sem_px)
        gather_x.start()

    for slot in range(4):
        @pl.when(jnp.logical_and(is_root, jnp.logical_not(jnp.logical_and(y == c, l == slot))))
        def _():
            arrive(WO.at[slot], sem_wo + slot)

    @pl.when(to_self)
    def _():
        get_o.wait()

    @pl.when(is_root)
    def _():
        send(WO, WO, dev(dzh=1), sem_wt + 1)
        send(WO, WO, dev(dx=1), sem_wt + 2)


    @pl.when(foreign)
    def _():
        send(cin.at[0], GM.at[their_block], partner, sem_pc)

    for dx, dc, dzh in line_masks:
        arrive(FULL.at[flip(x, dx) * 4 + flip(c, dc) * 2 + flip(zh, dzh)], sem_s2 + dx * 4 + dc * 2 + dzh)
    for q in range(8):
        PV[:, q * LANES : (q + 1) * LANES] = FULL[q]
    gain1, shift1 = PV[0:1, :], PV[1:2, :]

    def norm_rows(value, gain, shift):
        average = jnp.mean(value, axis=-1, keepdims=True)
        centered = value - average
        root = lax.rsqrt(jnp.mean(centered * centered, axis=-1, keepdims=True) + EPSILON)
        normal = centered * root
        return normal, root, normal * gain + shift

    def norm_one(block):
        for r in range(2):
            rows = pl.ds(r * 64, 64)
            normal, _, value = norm_rows(X[block, rows].astype(F32), gain1, shift1)
            N0[block, rows] = normal.astype(BF16)
            N1[block, rows] = value.astype(BF16)

    norm_one(j)

    gather_x.sibling(0)
    norm_one((1 - c) * 4 + l)
    gather_x.forward(1)
    gather_x.forward(2)
    norm_one(c * 4 + roles[1])
    norm_one(c * 4 + roles[2])
    spread_q[0].forward()
    get_i.wait()
    for jj in range(8):
        for ch in range(4):
            flat = flat_column(jj, ch)
            WSI[jj, ch] = WII[:, flat * LANES : (flat + 1) * LANES]
    sem_wi = slots(8)
    for dc, dl in group_masks:
        push(WSI.at[group(dc, dl)], RI.at[t, j], dev(dc=dc, dl=dl), sem_wi + dc * 4 + dl)
    RI[t, j] = WSI[j]
    for k in (1, 2):
        gather_x.sibling(k)
    gather_x.forward(3)
    norm_one((1 - c) * 4 + roles[1])
    spread_q[1].forward()
    norm_one((1 - c) * 4 + roles[2])
    norm_one(c * 4 + roles[3])
    spread_q[2].forward()
    gather_x.sibling(3)
    norm_one((1 - c) * 4 + roles[3])

    get_d.wait()
    spread_i, spread_d = Spread(RI), Spread(WD)

    for dc, dl in group_masks:
        arrive(SG.at[group(dc, dl)], sem_sg + dc * 4 + dl)
    lens = SG[j, 1:2, :]
    row_ids = lax.broadcasted_iota(jnp.int32, (LANES, LANES), 0)
    lane_ids = lax.broadcasted_iota(jnp.int32, (LANES, LANES), 1)
    label_row = lane_ids.astype(F32)
    label_col = row_ids.astype(F32)
    earlier = (lane_ids < row_ids).astype(BF16)
    running = jnp.zeros((1, LANES), F32)
    for blk in range(8):
        onehot = (label_col == SG[blk, 0:1, :]).astype(F32).T
        before = dot(earlier, onehot.astype(BF16)) + running
        running = running + jnp.sum(onehot, axis=0, keepdims=True)
        rank = jnp.sum(before * onehot, axis=1, keepdims=True)
        limit = jnp.sum(onehot * lens, axis=1, keepdims=True)
        ident = jnp.sum(label_row * onehot, axis=1, keepdims=True)
        CODE[blk] = jnp.broadcast_to(jnp.where(rank < limit, ident, -1.0), (ROWS, LANES))

    @pl.when(native)
    def _():
        get_c.wait()

    @pl.when(foreign)
    def _():
        arrive(GM.at[j], sem_pc)

    is_real = CODE[j][:, 0:1] >= 0.0
    GM[j] = jnp.where(is_real, GM[j].astype(F32), 0.0).astype(BF16)
    gather_g.begin()

    @pl.when(jnp.logical_not(is_root))
    def _():
        arrive(WO, sem_wt + root_mask)

    @pl.when(root_mask == 1)
    def _():
        send(WO, WO, dev(dx=1), sem_wt + 3)

    for dc, dl in group_masks:
        arrive(RI.at[t, group(dc, dl)], sem_wi + dc * 4 + dl)
    spread_i.start_z()
    spread_i.start_x()
    spread_d.start_x()
    for ch in range(3):
        spread_q[ch].finish()
        for i in range(32):
            tt, jj = shard_place(i)
            WQ[i * 32 : (i + 1) * 32, ch * LANES : (ch + 1) * LANES] = RQ[ch, tt, jj]
    bias_q, bias_v = FULL[own_pair][2:3, :], FULL[own_pair][3:4, :]
    for k in range(4):
        rows = pl.ds(k * 256, 256)
        normed = N1[2 * k : 2 * k + 2].reshape(256, D)
        mixed = dot(normed, WQ[...])
        queries = (mixed[:, :LANES] + bias_q).astype(BF16).astype(F32) * (HEAD_DIM ** -0.5)
        keys = mixed[:, LANES : 2 * LANES]
        values = mixed[:, 2 * LANES :] + bias_v
        QS[rows] = queries.astype(BF16)
        KK[rows] = keys.astype(BF16)
        VV[rows] = values.astype(BF16)
        QT[:, rows] = queries.T.astype(BF16)
        KT[:, rows] = keys.T.astype(BF16)
        VT[:, rows] = values.T.astype(BF16)


    def pair_lanes(lp):
        return (pl.ds(pl.multiple_of(lp * LANES, LANES), LANES), pl.ds(pl.multiple_of(512 + lp * LANES, LANES), LANES))

    def cat_lanes(ref, lp):
        first, second = pair_lanes(lp)
        return jnp.concatenate([ref[:, first], ref[:, second]], axis=1)

    def cat_rows(ref, lp):
        return jnp.concatenate([ref[lp], ref[4 + lp]], axis=0)

    class Scatter:
        def __init__(self, part, chip, number, before=None, tree=True):
            self.part, self.chip, self.number, self.before, self.tree = part, chip, number, before, tree
            self.near, self.far = slots(4), slots(8)

        def emit(self, m, value):
            if self.before is not None:
                left(self.part.at[m, 1 - c], self.before.near + m)
            low = value.astype(BF16)
            self.part[m, 0] = low[:ROWS]
            self.part[m, 1] = low[ROWS:]
            send(self.part.at[m, 1 - c], SB.at[self.number, m], dev(dc=1), self.near + m)

        def pieces(self, m):
            if self.tree and m > 1:
                return ((pl.ds(0, 64), self.far + m), (pl.ds(64, 64), self.far + 4 + m))
            return ((pl.ds(0, ROWS), self.far + m),)

        def chip_left(self, m):
            for rows, sem in self.pieces(m):
                left(self.chip.at[m, rows], sem)

        def reduce(self, m):
            arrive(SB.at[self.number, m], self.near + m)
            if m == 0:
                return
            if self.before is not None:
                self.before.chip_left(m)
            for k, (rows, sem) in enumerate(self.pieces(m)):
                total = self.part[m, c, rows].astype(F32) + SB[self.number, m, rows].astype(F32)
                if self.tree and m == 2:
                    across = RV.at[self.number, 3, rows]
                    arrive(across, self.pieces(3)[k][1])
                    total += across[...].astype(F32)
                self.chip[m, rows] = total.astype(BF16)
                device = dev(dl=1) if self.tree and m == 3 else dev(dl=m)
                send(self.chip.at[m, rows], RV.at[self.number, m, rows], device, sem)

        def finish(self):
            for m in (1, 2) if self.tree else (1, 2, 3):
                for rows, sem in self.pieces(m):
                    arrive(RV.at[self.number, m, rows], sem)

        def rows(self, rows):
            total = self.part[0, c, rows].astype(F32) + SB[self.number, 0, rows].astype(F32)
            for m in (1, 2) if self.tree else (1, 2, 3):
                total += RV[self.number, m, rows].astype(F32)
            return total

        def close(self):
            for m in range(4):
                left(self.part.at[m, 1 - c], self.near + m)
                if m:
                    self.chip_left(m)

    head_rows = lax.broadcasted_iota(jnp.int32, (LANES, 256), 0)
    head_lanes = lax.broadcasted_iota(jnp.int32, (256, LANES), 1)

    def only_rows(value, h):
        return jnp.where((head_rows >= h * 64) & (head_rows < (h + 1) * 64), value, jnp.zeros_like(value))

    def only_lanes(value, h):
        return jnp.where((head_lanes >= h * 64) & (head_lanes < (h + 1) * 64), value, jnp.zeros_like(value))

    scatter_a = Scatter(PA, CS, 0)
    attend_order = (3, 1, 2, 0)
    for k, m in enumerate(attend_order):
        lp = flip_l(m)
        queries_t = cat_lanes(QT, lp)
        seg_q = jnp.concatenate([SG[lp, 0:1, :], SG[4 + lp, 0:1, :]], axis=1)
        for h in range(2):
            masked_t = only_rows(queries_t.astype(F32), h).astype(BF16)
            top = jnp.full((8, 256), NEGATIVE, F32)
            for i in range(8):
                rows = pl.ds(i * ROWS, ROWS)
                value = dot(KK[rows], masked_t)
                code = CODE[i]
                allowed = jnp.concatenate([code, code], axis=1) == seg_q
                value = jnp.where(allowed, value, NEGATIVE)
                SC[h, rows] = value
                top = jnp.maximum(top, jnp.max(value.reshape(16, 8, 256), axis=0))
            top = jnp.max(top, axis=0, keepdims=True)
            total = jnp.zeros((8, 256), F32)
            for i in range(8):
                rows = pl.ds(i * ROWS, ROWS)
                value = jnp.exp(SC[h, rows] - top)
                PT[m, h, rows] = value.astype(BF16)
                total = total + jnp.sum(value.reshape(16, 8, 256), axis=0)
            inverse = 1.0 / jnp.sum(total, axis=0, keepdims=True)
            INV[m, h] = jnp.broadcast_to(inverse, (8, 256))
            OT[m, h * 64 : (h + 1) * 64] = dot(VT[h * 64 : (h + 1) * 64, :], PT[m, h]) * inverse
            if k and h == 0:
                scatter_a.reduce(attend_order[k - 1])
            if k == 1 and h == 1:
                spread_d.start_z()
            if k == 2 and h == 0:
                gather_g.forward(2)
            if k == 3 and h == 1:
                gather_g.forward(1)
        joined = OT[m]
        OL[m] = joined.astype(BF16)
        scatter_a.emit(m, dot(joined.T.astype(BF16), WO[...].reshape(LANES, D)))
    spread_i.forward()
    scatter_a.reduce(0)
    scatter_a.finish()

    gain2, shift2, bias_o = PV[5:6, :], PV[6:7, :], PV[4:5, :]
    for r in range(4):
        rows = pl.ds(r * 32, 32)
        residual = X[j, rows].astype(F32) + scatter_a.rows(rows) + bias_o
        XO[rows] = residual
        normal, root, value = norm_rows(residual, gain2, shift2)
        N2F[rows] = normal
        RS_[rows] = jnp.broadcast_to(root, (32, LANES))
        N2[j, rows] = value.astype(BF16)
    gather_n = Gather(N2)
    gather_n.begin()

    spread_i.finish()
    for i in range(32):
        tt, jj = shard_place(i)
        for ch in range(4):
            WI[i * 32 : (i + 1) * 32, ch * LANES : (ch + 1) * LANES] = RI[tt, jj, ch]
    pick = lax.broadcasted_iota(jnp.int32, (16, LANES), 0) == 8 + l
    bias_in = jnp.concatenate(
        [
            jnp.sum(jnp.where(pick, FULL[(ch // 2) * 4 + c * 2 + ch % 2], 0.0), axis=0, keepdims=True)
            for ch in range(4)
        ],
        axis=1,
    )
    scatter_m = Scatter(PA, CS, 1, scatter_a, tree=False)
    scatter_b = Scatter(PB, CSB, 2)
    BG[0:1] = jnp.zeros((1, 512), F32)

    def hidden_part(m):
        lp = flip_l(m)
        first, second = pair_lanes(lp)
        hidden = dot(cat_rows(N2, lp), WI[...]) + bias_in
        phi_cap = 0.5 * (1.0 + lax.erf(hidden * 0.7071067811865476))
        phi = jnp.exp(-0.5 * hidden * hidden) * 0.3989422804014327
        act = hidden * phi_cap
        GA[m] = phi_cap + hidden * phi
        HA[m] = act.astype(BF16)
        act_t = act.T.astype(BF16)
        HAT[:, first] = act_t[:, :ROWS]
        HAT[:, second] = act_t[:, ROWS:]

    def hidden_back(m):
        lp = flip_l(m)
        grad_act = dot_nt(cat_rows(GM, lp), WD[...].reshape(512, D))
        grad_pre = (grad_act * GA[m]).astype(BF16)
        GP[lp] = grad_pre[:ROWS]
        GP[4 + lp] = grad_pre[ROWS:]
        BG[0:1] += jnp.sum(grad_pre.astype(F32), axis=0, keepdims=True)
        scatter_m.emit(m, dot_nt(grad_pre, WI[...]))

    gather_n.sibling(0)
    hidden_part(0)
    spread_d.forward()
    gather_n.forward(2)
    gather_n.forward(1)
    gather_g.forward(3)
    gather_g.sibling(0)
    spread_d.finish()
    hidden_back(0)
    gather_n.sibling(2)
    hidden_part(1)
    gather_g.sibling(2)
    hidden_back(1)
    scatter_m.reduce(0)
    gather_n.sibling(1)
    hidden_part(2)
    gather_g.sibling(1)
    hidden_back(2)
    gather_n.forward(3)
    scatter_m.reduce(1)
    gather_n.sibling(3)
    hidden_part(3)
    gather_g.sibling(3)
    scatter_m.reduce(2)
    hidden_back(3)
    scatter_m.reduce(3)

    class Total:
        def __init__(self, part, from_x, middle, from_z):
            self.part, self.from_x, self.middle, self.from_z = part, from_x, middle, from_z
            self.sem = slots(3)

        def start_cross(self):
            push(self.part.at[(1 - x) * 2 + 1 - zh], self.from_x.at[1 - zh], dev(dx=1), self.sem)

        def start_keep(self):
            push(self.part.at[(1 - x) * 2 + zh], self.from_x.at[zh], dev(dx=1), self.sem + 2)

        def second(self):
            arrive(self.from_x.at[1 - zh], self.sem)
            self.middle[...] = (
                self.part[x * 2 + 1 - zh].astype(F32) + self.from_x[1 - zh].astype(F32)
            ).astype(BF16)
            push(self.middle, self.from_z, dev(dzh=1), self.sem + 1)

        def result(self):
            arrive(self.from_x.at[zh], self.sem + 2)
            arrive(self.from_z, self.sem + 1)
            return self.part[t].astype(F32) + self.from_x[zh].astype(F32) + self.from_z[...].astype(F32)

    total_d = Total(GD, XD, HD, ZD)
    total_i = Total(GI, XI, HI, ZI)
    total_q = [Total(GQ.at[ch], XQ.at[ch], HQ.at[ch], ZQ.at[ch]) for ch in range(3)]
    for ch in range(4):
        GD[ch] = dot(HAT[ch * LANES : (ch + 1) * LANES, :], GM[...].reshape(8 * ROWS, D)).astype(BF16)
    total_d.start_cross()
    all_pre = GP[...].reshape(8 * ROWS, 512)
    for blk in range(8):
        product = dot_tn(N2[:, :, blk * LANES : (blk + 1) * LANES].reshape(8 * ROWS, LANES), all_pre).astype(BF16)
        for r in range(4):
            tt, jj = shard_place(blk * 4 + r)
            for ch in range(4):
                GI[tt, jj, ch] = product[r * 32 : (r + 1) * 32, ch * LANES : (ch + 1) * LANES]
    total_i.start_cross()
    total_d.start_keep()
    total_i.start_keep()

    def norm_back(grad, normal, root, gain):
        scaled = grad * gain
        return root * (scaled - jnp.mean(scaled, axis=-1, keepdims=True)
                       - normal * jnp.mean(scaled * normal, axis=-1, keepdims=True))

    def forward_out(m):
        scatter_b.emit(m, dot(HA[m], WD[...].reshape(512, D)))

    for m in attend_order:
        forward_out(m)
    scatter_m.finish()
    sums = [jnp.zeros((1, D), F32) for _ in range(4)]
    for r in range(4):
        rows = pl.ds(r * 32, 32)
        grad = scatter_m.rows(rows)
        normal = N2F[rows]
        top_grad = GM[j, rows].astype(F32)
        grad_residual = top_grad + norm_back(grad, normal, RS_[rows][:, 0:1], gain2)
        low = grad_residual.astype(BF16)
        GB[j, rows] = low
        N2F[rows] = grad_residual
        for i, value in enumerate((grad * normal, grad, low.astype(F32), top_grad)):
            sums[i] += jnp.sum(value, axis=0, keepdims=True)
    vectors = {5: sums[0], 6: sums[1], 4: sums[2], 7: sums[3]}
    gather_b = Gather(GB)
    gather_b.begin()

    DK[...] = jnp.zeros_like(DK)
    DV[...] = jnp.zeros_like(DV)
    GOF[...] = jnp.zeros_like(GOF)

    def attend_back(m):
        lp = flip_l(m)
        first, second = pair_lanes(lp)
        branch = cat_rows(GB, lp)
        grad_att = dot_nt(branch, WO[...].reshape(LANES, D)).astype(BF16).astype(F32)
        GOF[...] += dot(OL[m], branch)
        grad_att_t = grad_att.T
        both = grad_att_t * OT[m]
        queries = jnp.concatenate([QS[first], QS[second]], axis=0).astype(F32)
        for h in range(2):
            inverse = INV[m, h][0:1]
            delta = jnp.sum(both[h * 64 : (h + 1) * 64], axis=0, keepdims=True) * inverse
            scaled_t = only_rows(grad_att_t * inverse, h)
            scaled_low_t = scaled_t.astype(BF16)
            scaled_low = scaled_t.T.astype(BF16)
            queries_h = only_lanes(queries, h).astype(BF16)
            for i in range(8):
                rows = pl.ds(i * ROWS, ROWS)
                probs = PT[m, h, rows]
                value = dot(VV[rows], scaled_low_t)
                grad_scores = (probs.astype(F32) * (value - delta)).astype(BF16)
                DV[rows] += dot(probs, scaled_low)
                DK[rows] += dot(grad_scores, queries_h)
                PT[m, h, rows] = grad_scores
            DQ[h * 64 : (h + 1) * 64, :] = dot(KT[h * 64 : (h + 1) * 64, :], PT[m, h]) * (HEAD_DIM ** -0.5)
        dq_rows = DQ[...].T.astype(BF16)
        GMX[lp, :, 0:LANES] = dq_rows[:ROWS]
        GMX[4 + lp, :, 0:LANES] = dq_rows[ROWS:]

    total_d.second()
    gather_b.sibling(0)
    attend_back(0)
    gather_b.forward(2)
    gather_b.forward(1)
    scatter_b.reduce(3)
    gather_b.sibling(2)
    attend_back(1)
    total_i.second()
    gather_b.sibling(1)
    attend_back(2)
    gather_b.forward(3)
    scatter_b.reduce(1)
    scatter_b.reduce(0)
    gather_b.sibling(3)
    attend_back(3)
    scatter_b.reduce(2)

    for blk in range(8):
        rows = pl.ds(blk * ROWS, ROWS)
        GMX[blk, :, LANES : 2 * LANES] = DK[rows].astype(BF16)
        GMX[blk, :, 2 * LANES :] = DV[rows].astype(BF16)
    all_mixed = GMX[...].reshape(8 * ROWS, 3 * LANES)
    scatter_n = Scatter(PA, CS, 3, scatter_m)

    def back_out(m):
        scatter_n.emit(m, dot_nt(cat_rows(GMX, flip_l(m)), WQ[...]))

    def joint_grad(blk):
        product = dot_tn(N1[:, :, blk * LANES : (blk + 1) * LANES].reshape(8 * ROWS, LANES), all_mixed).astype(BF16)
        for r in range(4):
            tt, jj = shard_place(blk * 4 + r)
            for ch in range(3):
                GQ[ch, tt, jj] = product[r * 32 : (r + 1) * 32, ch * LANES : (ch + 1) * LANES]

    for blk in range(8):
        joint_grad(blk)
    for ch in range(3):
        total_q[ch].start_cross()
    for ch in range(3):
        total_q[ch].start_keep()

    back_out(3)
    back_out(1)
    scatter_n.reduce(3)
    back_out(2)
    scatter_n.reduce(1)
    back_out(0)
    GO[...] = GOF[...].astype(BF16)
    sem_go, sem_gs = slots(4), slots(4)

    @pl.when(x != c)
    def _():
        send(GO, XGO.at[0], dev(dx=1), sem_go)

    scatter_n.reduce(0)

    for ch in range(3):
        total_q[ch].second()
    sums = [jnp.zeros((1, D), F32) for _ in range(2)]
    for m in range(4):
        lp = flip_l(m)
        for half in range(2):
            value = PA[m, half].astype(F32)
            sums[0] += jnp.sum(value * N0[half * 4 + lp].astype(F32), axis=0, keepdims=True)
            sums[1] += jnp.sum(value, axis=0, keepdims=True)
    vectors[0], vectors[1] = sums
    scatter_n.reduce(2)
    mixed_sums = jnp.sum(all_mixed.astype(F32), axis=0, keepdims=True)
    for q in range(8):
        VG[q] = jnp.zeros((16, LANES), F32)
        for p in (0, 1, 4, 5, 6, 7):
            VG[q, p : p + 1] = vectors[p][:, q * LANES : (q + 1) * LANES]
        for p, ch in ((2, 0), (3, 2)):
            VG[q, p : p + 1] = jnp.where(own_pair == q, mixed_sums[:, ch * LANES : (ch + 1) * LANES], 0.0)
        ch = (q // 4) * 2 + q % 2
        for r in range(4):
            here = jnp.logical_and(c == (q // 2) % 2, l == r)
            VG[q, 8 + r : 9 + r] = jnp.where(here, BG[0:1, ch * LANES : (ch + 1) * LANES], 0.0)
    sem_v1, sem_v2 = slots(8), slots(4)
    for dx, dc, dzh in line_masks:
        mask = dx * 4 + dc * 2 + dzh
        push(VG.at[flip(x, dx) * 4 + flip(c, dc) * 2 + flip(zh, dzh)], VR.at[mask], dev(dx=dx, dc=dc, dzh=dzh), sem_v1 + mask)

    @pl.when(x == c)
    def _():
        arrive(XGO.at[0], sem_go)
        GOF[...] += XGO[0].astype(F32)

    @pl.when(root_mask == 1)
    def _():
        GO[...] = GOF[...].astype(BF16)
        send(GO, XGO.at[1], dev(dzh=1), sem_go + 1)


    bias_d = PV[7:8, :]
    sem_out, sem_in = slots(), slots()
    scatter_b.finish()
    for r in range(4):
        rows = pl.ds(r * 32, 32)
        BO[rows] = (XO[rows] + scatter_b.rows(rows) + bias_d).astype(BF16)
    put_block = move(BO, out_block.at[0], 6)

    @pl.when(native)
    def _():
        put_block.start()

    @pl.when(foreign)
    def _():
        send(BO, out_block.at[0], partner, sem_out)

    TD[...] = total_d.result().astype(BF16)
    put_d = move(TD, out_d, 7)
    put_d.start()
    TI[...] = total_i.result().astype(BF16)
    sem_ti, sem_tq = slots(8), slots(8 * 3)
    for dc, dl in group_masks:
        push(TI.at[group(dc, dl)], out_i.at[j], dev(dc=dc, dl=dl), sem_ti + dc * 4 + dl)
    put_i = move(TI.at[j], out_i.at[j], 8)
    put_i.start()

    slab = VG[q_own]
    for dx, dc, dzh in line_masks:
        mask = dx * 4 + dc * 2 + dzh
        arrive(VR.at[mask], sem_v1 + mask)
        slab += VR[mask]
    SL[...] = slab
    for dl in (1, 2, 3):
        push(SL, SLR.at[dl], dev(dl=dl), sem_v2 + dl)

    put_o = move(TGO.at[l], out_o, 10)

    @pl.when(is_root)
    def _():
        arrive(XGO.at[1], sem_go + 1)
        TGO[...] = (GOF[...] + XGO[1].astype(F32)).astype(BF16).reshape(4, 32, D)
        for slot in range(4):
            mine = jnp.logical_and(y == c, l == slot)

            @pl.when(mine)
            def _():
                put_o.start()

            @pl.when(jnp.logical_not(mine))
            def _():
                send(TGO.at[slot], out_o, (x * 2 + y, zh * 4 + slot), sem_gs + slot)

    for ch in range(3):
        TQ[ch] = total_q[ch].result().astype(BF16)
        for dc, dl in group_masks:
            push(TQ.at[ch, group(dc, dl)], out_q.at[ch, j], dev(dc=dc, dl=dl), sem_tq + ch * 8 + dc * 4 + dl)
    put_q = [move(TQ.at[ch, j], out_q.at[ch, j], 11 + ch) for ch in range(3)]
    for ch in range(3):
        put_q[ch].start()

    for r in range(4):
        rows = pl.ds(r * 32, 32)
        normal, root, _ = norm_rows(X[j, rows].astype(F32), gain1, shift1)
        XO[rows] = normal
        RS_[rows] = jnp.broadcast_to(root, (32, LANES))
    scatter_n.finish()
    for r in range(4):
        rows = pl.ds(r * 32, 32)
        grad = scatter_n.rows(rows)
        BI[rows] = (N2F[rows] + norm_back(grad, XO[rows], RS_[rows][:, 0:1], gain1)).astype(BF16)
    put_input = move(BI, out_input.at[0], 9)

    @pl.when(native)
    def _():
        put_input.start()

    @pl.when(foreign)
    def _():
        send(BI, out_input.at[0], partner, sem_in)

    for dl in (1, 2, 3):
        arrive(SLR.at[dl], sem_v2 + dl)
        slab += SLR[dl]
    SLF[...] = slab
    put_small = move(SLF, out_small, 14)
    put_small.start()

    for dc, dl in group_masks:
        arrive(out_i.at[group(dc, dl)], sem_ti + dc * 4 + dl)
        for ch in range(3):
            arrive(out_q.at[ch, group(dc, dl)], sem_tq + ch * 8 + dc * 4 + dl)

    put_d.wait()
    put_i.wait()
    put_small.wait()
    for ch in range(3):
        put_q[ch].wait()

    @pl.when(native)
    def _():
        put_block.wait()
        put_input.wait()

    @pl.when(foreign)
    def _():
        left(SGI, sem_ps)
        left(xin.at[0], sem_px)
        left(cin.at[0], sem_pc)
        left(BO, sem_out)
        left(BI, sem_in)
        arrive(out_block.at[0], sem_out)
        arrive(out_input.at[0], sem_in)

    @pl.when(to_self)
    def _():
        put_o.wait()

    @pl.when(jnp.logical_not(to_self))
    def _():
        left(wo, sem_wo + l)
        arrive(out_o, sem_gs + l)

    @pl.when(x != c)
    def _():
        left(GO, sem_go)

    @pl.when(root_mask == 1)
    def _():
        left(GO, sem_go + 1)

    @pl.when(root_mask == 1)
    def _():
        left(WO, sem_wt + 3)

    @pl.when(is_root)
    def _():
        for mask in (1, 2):
            left(WO, sem_wt + mask)
        for slot in range(4):
            @pl.when(jnp.logical_not(jnp.logical_and(y == c, l == slot)))
            def _():
                left(TGO.at[slot], sem_gs + slot)

    scatter_n.close()
    scatter_b.close()
    for k in (1, 2):
        left(X.at[j], gather_x.far + k)
    left(X.at[j], gather_x.near)
    for copy in pending:
        copy.wait_send()


def fused_scratch():
    def v(*shape):
        return pltpu.VMEM(shape, BF16)

    def f(*shape):
        return pltpu.VMEM(shape, F32)

    blocks = (8, ROWS, D)
    return [
        v(*blocks), v(*blocks), v(*blocks), v(*blocks), v(*blocks), v(*blocks),
        f(8, LANES), f(8, 8, LANES), f(16, LANES), f(4, 16, LANES), f(8, 16, LANES), f(16, D),
        v(32, 3 * D), v(8, 3, 32, LANES), v(3, 4, 8, 32, LANES), v(D, 3 * LANES), v(4, 32, D),
        v(32, 4 * D), v(8, 4, 32, LANES), v(4, 8, 4, 32, LANES), v(D, 512), v(4, LANES, D),
        v(D, LANES), v(D, LANES), v(D, LANES), v(LANES, D), v(LANES, D), v(LANES, D),
        f(8, ROWS, LANES), f(2, D, 256), v(4, 2, D, 256), f(4, 2, 8, 256),
        f(4, LANES, 256), v(4, LANES, 256),
        v(4, 2, ROWS, D), v(4, ROWS, D), v(4, 2, ROWS, D), v(4, ROWS, D),
        v(4, 4, ROWS, D), v(4, 4, ROWS, D), f(ROWS, D), f(ROWS, D),
        v(512, D), v(4, 256, 512), v(8, ROWS, 512), f(4, 256, 512),
        f(D, LANES), f(D, LANES), f(LANES, 256), v(8, ROWS, 3 * LANES),
        v(3, 4, 8, 32, LANES), v(4, 8, 4, 32, LANES), v(4, LANES, D),
        v(3, 2, 8, 32, LANES), v(2, 8, 4, 32, LANES), v(2, LANES, D),
        v(3, 8, 32, LANES), v(8, 4, 32, LANES), v(LANES, D),
        v(3, 8, 32, LANES), v(8, 4, 32, LANES), v(LANES, D),
        v(3, 8, 32, LANES), v(8, 4, 32, LANES), v(LANES, D),
        v(LANES, D), f(LANES, D), v(4, LANES, D), v(4, 32, D),
        f(8, 16, LANES), f(8, 16, LANES), f(16, LANES), f(4, 16, LANES), f(16, LANES),
        f(ROWS, LANES), f(8, 512), v(ROWS, D), v(ROWS, D),
        pltpu.SemaphoreType.DMA((COPIES,)),
        pltpu.SemaphoreType.DMA((COPIES,)),
        pltpu.SemaphoreType.DMA((16,)),
    ]


def finish_kernel(
    block, grad_in, grad_q, grad_o, grad_i, grad_d, small,
    out_block, out_input, o0, o1, out_q, o2, o3, out_o, o4, o5, o6, out_i, ob, out_d, o7,
):
    place = lax.rem(lax.axis_index("band"), 4)
    out_block[...] = block[...]
    out_input[...] = grad_in[...]
    for jj in range(8):
        for ch in range(3):
            out_q[:, ch * D + pair_of(jj) * LANES : ch * D + (pair_of(jj) + 1) * LANES] = grad_q[ch, jj].astype(F32)
        for ch in range(4):
            flat = flat_column(jj, ch)
            out_i[:, flat * LANES : (flat + 1) * LANES] = grad_i[jj, ch].astype(F32)
    out_o[...] = grad_o[...].astype(F32)
    out_d[...] = grad_d[...].astype(F32)
    slab = small[...]
    mine = jnp.zeros((16, 32), F32)
    for k in range(4):
        mine = jnp.where(place == k, slab[:, k * 32 : (k + 1) * 32], mine)
    for p, ref in enumerate((o0, o1, o2, o3, o4, o5, o6, o7)):
        ref[...] = mine[p : p + 1].reshape(32)
    pick = lax.broadcasted_iota(jnp.int32, (16, LANES), 0) == 8 + place
    ob[...] = jnp.sum(jnp.where(pick, slab, 0.0), axis=0, keepdims=True).reshape(LANES)


def fused_shards(
    block_in,
    attention_norm_gain,
    attention_norm_bias,
    query_key_value,
    query_bias,
    value_bias,
    output_weight,
    output_bias,
    mlp_norm_gain,
    mlp_norm_bias,
    mlp_in_weight,
    mlp_in_bias,
    mlp_out_weight,
    mlp_out_bias,
    cotangent,
    segment_ids,
    sub_lengths,
):
    vmem = pl.BlockSpec(memory_space=pltpu.VMEM)
    hbm = pl.BlockSpec(memory_space=pl.ANY)

    def shape(dims, kind):
        return jax.ShapeDtypeStruct(dims, kind)

    parts = pl.pallas_call(
        functools.partial(fused_kernel, COPIES),
        out_shape=(
            shape((1, ROWS, D), BF16),
            shape((1, ROWS, D), BF16),
            shape((3, 8, 32, LANES), BF16),
            shape((32, D), BF16),
            shape((8, 4, 32, LANES), BF16),
            shape((LANES, D), BF16),
            shape((16, LANES), F32),
        ),
        in_specs=[hbm, hbm, vmem, vmem, hbm, hbm, hbm, hbm] + [vmem] * 9,
        out_specs=(hbm,) * 7,
        scratch_shapes=fused_scratch(),
        compiler_params=pltpu.CompilerParams(
            collective_id=0, has_side_effects=True, vmem_limit_bytes=63 * 2**20
        ),
    )(
        block_in, cotangent, segment_ids, sub_lengths,
        query_key_value, output_weight, mlp_in_weight, mlp_out_weight,
        attention_norm_gain, attention_norm_bias, query_bias, value_bias,
        output_bias, mlp_norm_gain, mlp_norm_bias, mlp_out_bias, mlp_in_bias,
    )
    vector = shape((32,), F32)
    return pl.pallas_call(
        finish_kernel,
        out_shape=(
            shape((1, ROWS, D), BF16), shape((1, ROWS, D), BF16), vector, vector,
            shape((32, 3 * D), F32), vector, vector, shape((32, D), F32), vector, vector, vector,
            shape((32, 4 * D), F32), shape((LANES,), F32), shape((LANES, D), F32), vector,
        ),
        in_specs=[vmem] * 7,
        out_specs=(vmem,) * 15,
    )(*parts)


def solution(mesh):
    small_slice = dict(mesh.shape) == {"seq": 4, "band": 8}
    return jax.shard_map(
        fused_shards if small_slice else shards,
        mesh=mesh,
        in_specs=(
            P("seq", "band", None),
            P(("seq", "band")),
            P(("seq", "band")),
            P(("seq", "band"), None),
            P(("seq", "band")),
            P(("seq", "band")),
            P(("seq", "band"), None),
            P(("seq", "band")),
            P(("seq", "band")),
            P(("seq", "band")),
            P(("seq", "band"), None),
            P(("seq", "band")),
            P(("seq", "band"), None),
            P(("seq", "band")),
            P("seq", "band", None),
            P("seq", "band"),
            P("seq", None),
        ),
        out_specs=(
            P("seq", "band", None),
            P("seq", "band", None),
            P(("seq", "band")),
            P(("seq", "band")),
            P(("seq", "band"), None),
            P(("seq", "band")),
            P(("seq", "band")),
            P(("seq", "band"), None),
            P(("seq", "band")),
            P(("seq", "band")),
            P(("seq", "band")),
            P(("seq", "band"), None),
            P(("seq", "band")),
            P(("seq", "band"), None),
            P(("seq", "band")),
        ),
        check_vma=False,
    )
```
